128 devices in a mesh: row: 4 (over y), col: 32 (over x, z, core).
Axes of the slice: x: 4, y: 4, z: 4, core: 2. Of those that a mesh axis runs over, the one named last changes fastest.
Arguments:
- template: float32 [2048, 8192], P('row', 'col')
- template_var: float32 [2048, 8192], P('row', 'col'), may hold values from 0.1 to 1
- coverage: int32 [2048, 8192], P('row', 'col'), may hold values 0 or 1
- exposure: float32 [4, 4096, 4, 256], P('row', 'col')
- exposure_var: float32 [4, 4096, 4, 256], P('row', 'col'), may hold values from 0.25 to 4
- strip_owner: int32 [4, 4096], P('row', 'col'), may hold values from 0 to 127, as said below
- strip_slot: int32 [4, 4096], P('row', 'col'), may hold values from 0 to 127, as said below
Outputs:
- difference: float32 [2048, 8192], P('row', 'col')
- variance: float32 [2048, 8192], P('row', 'col')
The draws below stay inside these ranges and needn't reach their ends.
Inputs may be any that keep to these rules, and one draw needn't show every extreme that they name: `strip_owner`: over all devices, every (owner, position) pair is named by exactly one block. Each device sends exactly 1 block to every owner. `strip_slot`: together with strip_owner, a permutation of all owned row blocks; all blocks of one device take the same position at their owners.
All inputs are finite; a program needn't handle non-finite values. No bound on the sum of `coverage` on one device may be relied on, other than what follows from the above.
Results may differ from the reference program's by a relative error of at most 0.0056.
Values may be sent and summed in bfloat16 or wider, within the bound.
A program may use at most 128 MiB of HBM per device.

```python
import math
import jax
import jax.numpy as jnp
import numpy as np
from jax import lax

PATCH = 256
STRIP = 4
NSTRIP = 128
HEIGHT = 2048
WIDTH = 8192
N_ROW = 4
N_COL = 32
DEVICES = 128


def routing(key):
    order_keys = jax.random.split(jax.random.fold_in(key, 3), DEVICES)
    owners = jax.vmap(lambda k: jax.random.permutation(k, DEVICES))(order_keys)
    position = jax.random.permutation(jax.random.fold_in(key, 2), DEVICES)
    slot_ids = jnp.broadcast_to(position[:, None], (DEVICES, NSTRIP))
    return (owners.astype(jnp.int32), slot_ids.astype(jnp.int32))


def sky(key):
    normal_part = jax.random.normal(jax.random.fold_in(key, 7), (HEIGHT, WIDTH), jnp.float32)
    return normal_part


def draw_template(key, part):
    return sky(key)


def draw_exposure(key, part):
    image = sky(key)
    blurred = 0.55 * jnp.roll(image, 1, axis=1) + 0.3 * jnp.roll(image, 1, axis=0) + 0.15 * image
    owners, slot_ids = routing(key)
    key = jax.random.fold_in(key, 5)
    regions = blurred.reshape(N_ROW, NSTRIP, STRIP, N_COL, PATCH).transpose(0, 3, 1, 2, 4).reshape(DEVICES, NSTRIP, STRIP, PATCH)
    picked = regions[owners, slot_ids]
    gains = jnp.exp(jax.random.uniform(jax.random.fold_in(key, 1), (DEVICES, 2), jnp.float32, -0.6931, 0.6931))
    patch_of = slot_ids * STRIP // PATCH
    scale = gains[owners, patch_of][:, :, None, None]
    noise = 0.5 * jax.random.normal(jax.random.fold_in(key, 2), picked.shape, jnp.float32)
    return (scale * picked + noise).reshape(N_ROW, N_COL * NSTRIP, STRIP, PATCH)


def draw_strip_owner(key, part):
    owners, slot_ids = routing(key)
    return owners.reshape(N_ROW, N_COL * NSTRIP)


def draw_strip_slot(key, part):
    owners, slot_ids = routing(key)
    return slot_ids.reshape(N_ROW, N_COL * NSTRIP)


def set_ends(drawn, rng, smallest, top_value):
    shape = drawn.shape
    index_at = [jax.random.randint(jax.random.fold_in(rng, axis), (), 0, shape[axis]) for axis in range(len(shape))]
    drawn = drawn.at[tuple(index_at)].set(smallest)
    longest = shape.index(max(shape))
    index_at[longest] = (index_at[longest] + 1) % shape[longest]
    return drawn.at[tuple(index_at)].set(top_value)


def block_levels(own_key, shape, cuts, smallest, top_value):
    def one(axis_at, shards_of):
        steps = jax.random.uniform(jax.random.fold_in(jax.random.fold_in(own_key, 6), axis_at), (shards_of,), jnp.float32, smallest / len(cuts), top_value / len(cuts))
        return jnp.repeat(jnp.exp(steps), shape[axis_at] // shards_of).reshape((-1,) + (1,) * (len(shape) - axis_at - 1))

    factor_of = one(*cuts[0])
    for cut in cuts[1:]:
        factor_of = factor_of * one(*cut)
    return factor_of


def setup_inputs(seed: int = 0) -> dict:
    streams_of = jax.random.split(jax.random.key(seed), 8)
    template = draw_template(jax.random.fold_in(streams_of[7], 71), 0)
    template_var = jnp.clip(jnp.exp(math.log(1.0) - 2.3025851 * jax.random.uniform(streams_of[1], (HEIGHT, WIDTH), jnp.float32) ** block_levels(streams_of[1], (HEIGHT, WIDTH), ((0, 4), (1, 32)), -0.2, 0.2)), 0.1, 1.0)
    coverage = set_ends((jax.random.randint(streams_of[2], (HEIGHT, WIDTH), 0, 8) < 7).astype(jnp.int32), jax.random.fold_in(streams_of[2], 1), 0, 1)
    exposure = draw_exposure(jax.random.fold_in(streams_of[7], 71), 0)
    exposure_var = jnp.clip(jnp.exp(math.log(4.0) - 2.7725887 * jax.random.uniform(streams_of[4], (N_ROW, N_COL * NSTRIP, STRIP, PATCH), jnp.float32) ** block_levels(streams_of[4], (N_ROW, N_COL * NSTRIP, STRIP, PATCH), ((0, 4), (1, 32)), -0.2, 0.2)), 0.25, 4.0)
    strip_owner = draw_strip_owner(jax.random.fold_in(streams_of[7], 71), 0)
    strip_slot = draw_strip_slot(jax.random.fold_in(streams_of[7], 71), 0)
    return {"template": template, "template_var": template_var, "coverage": coverage, "exposure": exposure, "exposure_var": exposure_var, "strip_owner": strip_owner, "strip_slot": strip_slot}


RIDGE = 0.05
SIGMAS = (1.0, 2.0, 4.0)

def filter_bank():
    taps = np.arange(31) - 15.0
    collected = []
    for sigma in SIGMAS:
        for degree in range(5):
            scaled = taps / sigma
            shape = scaled ** degree * np.exp(-0.5 * scaled * scaled)
            collected.append(shape / np.sqrt(np.sum(shape * shape)))
    return np.array(collected, np.float32)

def basis_pairs():
    x_index = []
    y_index = []
    for s in range(3):
        for j in range(5):
            for i in range(5 - j):
                x_index.append(s * 5 + i)
                y_index.append(s * 5 + j)
    return (np.array(x_index), np.array(y_index))

def x_table(block_cols):
    bank = filter_bank()
    table = np.zeros((block_cols + 30, 15, block_cols), np.float32)
    across = np.arange(block_cols)
    for q in range(31):
        table[across + q, :, across] = bank[:, q]
    return jnp.asarray(table.reshape(block_cols + 30, 15 * block_cols)).astype(jnp.bfloat16)

def y_table(block_rows):
    bank = filter_bank()
    table = np.zeros((15, block_rows, block_rows + 30), np.float32)
    across = np.arange(block_rows)
    for q in range(31):
        table[:, across, across + q] = bank[:, q][:, None]
    return jnp.asarray(table).astype(jnp.bfloat16)

def convolve(extended):
    height = extended.shape[0] - 30
    width = extended.shape[1] - 30
    block_cols = math.gcd(width, 128)
    x_weights = x_table(block_cols)
    pieces = []
    for c in range(width // block_cols):
        window = extended[:, c * block_cols:c * block_cols + block_cols + 30]
        product = jnp.dot(window.astype(jnp.float32), x_weights.astype(jnp.float32), preferred_element_type=jnp.float32)
        pieces.append(product.reshape(height + 30, 15, block_cols))
    filtered = jnp.concatenate(pieces, 2).astype(jnp.bfloat16)
    block_rows = math.gcd(height, 128)
    y_weights = y_table(block_rows)

    def one_block(number):
        window = lax.dynamic_slice_in_dim(filtered, number * block_rows, block_rows + 30, 0)
        outputs = []
        for s in range(3):
            for j in range(5):
                selected = window[:, s * 5:s * 5 + 5 - j, :].reshape(block_rows + 30, (5 - j) * width)
                product = jnp.dot(y_weights[s * 5 + j].astype(jnp.float32), selected.astype(jnp.float32), preferred_element_type=jnp.float32)
                outputs.append(product.reshape(block_rows, 5 - j, width))
        return jnp.concatenate(outputs, 1).astype(jnp.bfloat16)
    blocks = lax.map(one_block, jnp.arange(height // block_rows, dtype=jnp.int32))
    return blocks.reshape(height, 45, width)

def solve_patches(pooled):
    gram = pooled[..., :2025].reshape(pooled.shape[:-1] + (45, 45))
    cross = pooled[..., 2025:]
    trace = jnp.trace(gram, axis1=-2, axis2=-1)
    system = gram + (RIDGE * trace / 45.0)[..., None, None] * jnp.eye(45, dtype=jnp.float32)
    lower = jnp.linalg.cholesky(system)
    halfway = lax.linalg.triangular_solve(lower, cross[..., None], left_side=True, lower=True)
    coefficients = lax.linalg.triangular_solve(lower, halfway, left_side=True, lower=True, transpose_a=True)[..., 0]
    bank = jnp.asarray(filter_bank()).astype(jnp.bfloat16).astype(jnp.float32)
    x_index, y_index = basis_pairs()
    kernel = jnp.einsum('...k,kq,kt->...qt', coefficients, bank[y_index], bank[x_index], precision=lax.Precision.HIGHEST)
    return (coefficients, lax.optimization_barrier(jnp.sum(kernel * kernel, axis=(-2, -1))))

def reference(template, template_var, coverage, exposure, exposure_var, strip_owner, strip_slot):
    height = 2 * PATCH
    width = PATCH
    devices = N_ROW * N_COL
    owners = strip_owner.reshape(-1)
    slot_ids = strip_slot.reshape(-1)

    def assemble(values):
        rows_in = values.reshape(devices * NSTRIP, STRIP * PATCH)
        placed = jnp.zeros((devices, NSTRIP, STRIP * PATCH), jnp.float32).at[owners, slot_ids].set(rows_in)
        return placed.reshape(devices, height, width)

    def to_regions(image):
        return image.reshape(N_ROW, height, N_COL, width).transpose(0, 2, 1, 3).reshape(devices, height, width)

    def from_regions(regions):
        return regions.reshape(N_ROW, N_COL, height, width).transpose(0, 2, 1, 3).reshape(N_ROW * height, N_COL * width)
    science = assemble(exposure)
    noise_var = assemble(exposure_var)
    mask = to_regions(coverage).astype(jnp.float32)
    tvar = to_regions(template_var)
    root_weight = mask * lax.rsqrt(noise_var)
    padded = jnp.pad(template.astype(jnp.bfloat16), 15)

    def window_of(index):
        start_row = index // N_COL * height
        start_col = index % N_COL * width
        return lax.dynamic_slice(padded, (start_row, start_col), (height + 30, width + 30))

    def normals(index):
        conv = convolve(window_of(index))
        weighted = lax.optimization_barrier((conv * root_weight[index][:, None, :]).astype(jnp.bfloat16))
        target = lax.optimization_barrier((root_weight[index] * science[index]).astype(jnp.bfloat16))
        weighted = weighted.astype(jnp.float32).reshape(2, PATCH, 45, width)
        target = target.astype(jnp.float32).reshape(2, PATCH, width)
        gram = jnp.einsum('prkx,prlx->pkl', weighted, weighted, precision=lax.Precision.HIGHEST)
        cross = jnp.einsum('prkx,prx->pk', weighted, target, precision=lax.Precision.HIGHEST)
        return jnp.concatenate([gram.reshape(2, 2025), cross], 1)
    packed = lax.map(normals, jnp.arange(devices, dtype=jnp.int32))
    grid = packed.reshape(N_ROW, N_COL, 2, 2070).transpose(0, 2, 1, 3).reshape(2 * N_ROW, N_COL, 2070)
    padded_grid = jnp.pad(grid, ((1, 1), (1, 1), (0, 0)))
    pooled = jnp.zeros_like(grid)
    for a in range(3):
        for b in range(3):
            pooled = pooled + padded_grid[a:a + 2 * N_ROW, b:b + N_COL]
    pooled = pooled.reshape(N_ROW, 2, N_COL, 2070).transpose(0, 2, 1, 3).reshape(devices, 2, 2070)
    coefficients, kernel_power = solve_patches(pooled)

    def finish(index):
        conv = convolve(window_of(index)).astype(jnp.float32).reshape(2, PATCH, 45, width)
        model = jnp.einsum('prkx,pk->prx', conv, coefficients[index], precision=lax.Precision.HIGHEST)
        diff = mask[index] * (science[index] - model.reshape(height, width))
        spread = (kernel_power[index][:, None, None] * tvar[index].reshape(2, PATCH, width)).reshape(height, width)
        return (diff, mask[index] * (noise_var[index] + spread))
    diffs, spreads = lax.map(finish, jnp.arange(devices, dtype=jnp.int32))
    return (from_regions(diffs), from_regions(spreads))
```

```python
import jax
import jax.numpy as jnp
import numpy as np
from jax import lax
from jax.experimental import pallas as pl
from jax.experimental.pallas import tpu as pltpu
from jax.sharding import PartitionSpec as P

RIDGE = 0.05
SIGMAS = (1.0, 2.0, 4.0)
MESH = pl.DeviceIdType.MESH
F32 = jnp.float32
BF16 = jnp.bfloat16

SLOTS = (
    (0, 0), (0, 2), (1, 0), (1, 2), (2, 0), (2, 2), (0, 1), (1, 1),
    (2, 1), (0, 3), (1, 3), None, (2, 3), (0, 4), (1, 4), (2, 4),
)
GROUP_OF_PASS = (0, 1, 2, 3, 4, 4, 5, 5)
BLOCK = 96
TARGET = 47
DIRECTIONS = ((0, -1), (0, 1), (-1, 0), (1, 0), (-1, -1), (-1, 1), (1, -1), (1, 1))


def filter_bank():
    taps = np.arange(31) - 15.0
    collected = []
    for sigma in SIGMAS:
        for degree in range(5):
            scaled = taps / sigma
            shape = scaled**degree * np.exp(-0.5 * scaled * scaled)
            collected.append(shape / np.sqrt(np.sum(shape * shape)))
    return np.array(collected, np.float32).astype(jnp.bfloat16).astype(np.float32)


def tables():
    bank = filter_bank()
    x_weights = np.zeros((8, 256, 2, 128), np.float32)
    y_weights = np.zeros((8, BLOCK, 8, 2, 128), np.float32)
    across = np.arange(128)
    down = np.arange(BLOCK)
    order = []
    filled = [0] * 6
    for number, slot in enumerate(SLOTS):
        if slot is None:
            continue
        half, which = number // 2, number % 2
        s, i = slot
        group = GROUP_OF_PASS[half]
        for q in range(31):
            x_weights[half, across + q - 15 + 64, which, across] = bank[s * 5 + i, q]
        for j in range(5 - i):
            lane = filled[group]
            filled[group] += 1
            order.append((group * 8 + lane, s, i, j))
            for p in range(31):
                y_weights[half, down, lane, which, down + p - 15 + 16] = bank[s * 5 + j, p]
    shapes = np.zeros((48, 31 * 31), np.float64)
    for t, s, i, j in order:
        shapes[t] = np.outer(bank[s * 5 + j], bank[s * 5 + i]).reshape(-1).astype(np.float64)
    values, vectors = np.linalg.eigh(shapes @ shapes.T)
    root = np.sqrt(np.maximum(values, 0.0))[:, None] * vectors.T
    power = np.zeros((48, 128), np.float32)
    power[:, :48] = root
    power[:, 64:112] = root
    spread = np.zeros((2, 128, 768), np.float32)
    for patch in range(2):
        spread[patch, 64 * patch + np.arange(768) % 48, np.arange(768)] = 1.0
    return (
        x_weights.reshape(8, 256, 256).astype(jnp.bfloat16),
        y_weights.reshape(8, BLOCK * 8, 256).astype(jnp.bfloat16),
        power,
        spread.astype(jnp.bfloat16),
    )


def inverse_row(columns, size=128):
    rows = lax.broadcasted_iota(jnp.int32, (size, size), 0)
    lanes = lax.broadcasted_iota(jnp.int32, (size, size), 1)
    return jnp.max(jnp.where(columns == lanes, rows, 0), 0, keepdims=True)


def within(number):
    return jnp.clip(number, 0, 127)


def kernel(
    template, template_var, coverage, flux, noise, owner, slot, x_weights, y_weights, power, spread,
    difference, variance,
    wide, filtered, conv, send, recv, labels, science, science_var, root, own_gram, near_gram,
    row_index, table_in, table_out,
    halo_out, halo_in, part_out, part_in, label_out, label_in, gram_out, gram_in,
):
    r = lax.axis_index("row")
    c = lax.axis_index("col")
    x, z, k = c // 8, (c // 2) % 4, c % 2
    me = r * 32 + c
    place = (z * 2 + k) * 16 + r * 4 + x
    barrier = pltpu.get_barrier_semaphore()

    wide[...] = jnp.zeros_like(wide)
    near_gram[...] = jnp.zeros_like(near_gram)

    def greet(step, carry):
        other = lax.rem(me + step, 128)
        pl.semaphore_signal(barrier, inc=1, device_id=(other // 32, other % 32), device_id_type=MESH)
        return carry

    lax.fori_loop(1, 128, greet, 0)

    wide[16:528, 128:384] = template[...].astype(BF16)
    labels[pl.ds(place, 1), :] = slot[...]
    columns = jnp.transpose(jnp.broadcast_to(owner[...], (128, 128)))
    row_index[...] = jnp.broadcast_to(inverse_row(columns), (8, 128))
    pltpu.sync_copy(row_index, table_in)

    def pack(number, carry):
        block = within(table_in[0, number])
        send[number] = jnp.concatenate([flux[block], noise[block]], 0).astype(BF16)
        return carry

    lax.fori_loop(0, 128, pack, 0, unroll=4)
    recv[place] = send[me]
    filtered[:, 544:608, :] = jnp.zeros((16, 64, 256), BF16)
    pl.semaphore_wait(barrier, 127)

    def inside(dr, dc):
        return jnp.logical_and(
            jnp.logical_and(r + dr >= 0, r + dr < 4), jnp.logical_and(c + dc >= 0, c + dc < 32)
        )

    def target(dr, dc):
        return (jnp.clip(r + dr, 0, 3), jnp.clip(c + dc, 0, 31))

    source_rows = {-1: pl.ds(16, 16), 0: pl.ds(16, 512), 1: pl.ds(512, 16)}
    target_rows = {-1: pl.ds(528, 16), 0: pl.ds(16, 512), 1: pl.ds(0, 16)}
    source_cols = {-1: pl.ds(128, 128), 0: pl.ds(128, 256), 1: pl.ds(256, 128)}
    target_cols = {-1: pl.ds(384, 128), 0: pl.ds(128, 256), 1: pl.ds(0, 128)}

    def halo(number):
        dr, dc = DIRECTIONS[number]
        return pltpu.make_async_remote_copy(
            src_ref=wide.at[source_rows[dr], source_cols[dc]],
            dst_ref=wide.at[target_rows[dr], target_cols[dc]],
            send_sem=halo_out.at[number],
            recv_sem=halo_in.at[number],
            device_id=target(dr, dc),
            device_id_type=MESH,
        )

    def gram_copy(number):
        dr, dc = DIRECTIONS[number]
        return pltpu.make_async_remote_copy(
            src_ref=own_gram,
            dst_ref=near_gram.at[number],
            send_sem=gram_out.at[number],
            recv_sem=gram_in.at[number],
            device_id=target(dr, dc),
            device_id_type=MESH,
        )

    def each_sent(make, action):
        for number, (dr, dc) in enumerate(DIRECTIONS):
            @pl.when(inside(dr, dc))
            def _():
                action(make(number))

    def each_received(make):
        for number, (dr, dc) in enumerate(DIRECTIONS):
            @pl.when(inside(-dr, -dc))
            def _():
                make(number).wait_recv()

    each_sent(halo, lambda copy: copy.start())

    def label_copy(first, count, row, col, which):
        return pltpu.make_async_remote_copy(
            src_ref=labels.at[pl.ds(first, count)],
            dst_ref=labels.at[pl.ds(first, count)],
            send_sem=label_out.at[which],
            recv_sem=label_in.at[which],
            device_id=(row, col),
            device_id_type=MESH,
        )

    for dr in range(4):
        for dx in range(4):
            if dr or dx:
                label_copy(place, 1, (r + dr) % 4, ((x + dx) % 4) * 8 + z * 2 + k, 0).start()

    def send_part(step, carry):
        other = lax.rem(me + step, 128)
        pltpu.make_async_remote_copy(
            src_ref=send.at[other],
            dst_ref=recv.at[place],
            send_sem=part_out,
            recv_sem=part_in,
            device_id=(other // 32, other % 32),
            device_id_type=MESH,
        ).start()
        return carry

    lax.fori_loop(1, 128, send_part, 0)

    each_received(halo)

    whole = wide[...]
    windows = (whole[:, 64:320], whole[:, 192:448])

    def along_x(half, carry):
        for side in range(2):
            product = jnp.dot(windows[side], x_weights[half], preferred_element_type=F32).astype(BF16)
            for which in range(2):
                filtered[2 * half + which, 0:544, side * 128 : side * 128 + 128] = product[
                    :, which * 128 : which * 128 + 128
                ]
        return carry

    lax.fori_loop(0, 8, along_x, 0)

    def label_wait(count, which):
        part = labels.at[pl.ds(0, count)]
        pltpu.make_async_copy(part, part, label_in.at[which]).wait()
        pltpu.make_async_copy(part, part, label_out.at[which]).wait()

    label_wait(15, 0)
    for dz in range(4):
        for dk in range(2):
            if dz or dk:
                label_copy(
                    pl.multiple_of((z * 2 + k) * 16, 16), 16, r, x * 8 + ((z + dz) % 4) * 2 + (k + dk) % 2, 1
                ).start()

    def along_y(first, rows):
        for pair in range(3):
            groups = []
            for group in (2 * pair, 2 * pair + 1):
                total = None
                for half in range(8):
                    if GROUP_OF_PASS[half] == group:
                        window = filtered[2 * half : 2 * half + 2, pl.ds(first, 128), :].reshape(256, 256)
                        product = jnp.dot(
                            y_weights[half, 0 : rows * 8, :], window, preferred_element_type=F32
                        )
                        total = product if total is None else total + product
                groups.append(total.reshape(rows, 8, 256))
            conv[pl.ds(first, rows), pair * 16 : pair * 16 + 16, :] = jnp.concatenate(groups, 1).astype(BF16)

    def y_block(number, carry):
        along_y(pl.multiple_of(number * BLOCK, 16), BLOCK)
        return carry

    lax.fori_loop(0, 5, y_block, 0)
    along_y(480, 32)

    label_wait(112, 1)
    row_index[...] = jnp.broadcast_to(inverse_row(labels[...]), (8, 128))
    pltpu.sync_copy(row_index, table_out)
    parts = recv.at[pl.ds(0, 127)]
    pltpu.make_async_copy(parts, parts, part_in).wait()
    pltpu.make_async_copy(parts, parts, part_out).wait()

    def unpack(number, carry):
        upper = recv[within(table_out[0, 2 * number])].astype(F32)
        lower = recv[within(table_out[0, 2 * number + 1])].astype(F32)
        rows = pl.ds(pl.multiple_of(number * 8, 8), 8)
        science[rows, 0:128] = jnp.concatenate([upper[0:4], lower[0:4]], 0)
        science[rows, 128:256] = jnp.concatenate([upper[4:8], lower[4:8]], 0)
        science_var[rows, 0:128] = jnp.concatenate([upper[8:12], lower[8:12]], 0)
        science_var[rows, 128:256] = jnp.concatenate([upper[12:16], lower[12:16]], 0)
        return carry

    lax.fori_loop(0, 64, unpack, 0, unroll=4)
    root[...] = coverage[...].astype(F32) * lax.rsqrt(science_var[...])

    is_target = lax.broadcasted_iota(jnp.int32, (16, 256), 0) == TARGET - 32

    def gram_rows(number, total):
        base = pl.multiple_of(number * 8, 8)
        pieces = []
        for row in range(8):
            weight = root[pl.ds(base + row, 1), :]
            goal = weight * science[pl.ds(base + row, 1), :]
            basis = conv[base + row].astype(F32) * weight
            last = jnp.where(is_target, goal, basis[32:48])
            pieces.append(jnp.concatenate([basis[0:32].astype(BF16), last.astype(BF16)], 0))
        block = jnp.concatenate(pieces, 1)
        return total + lax.dot_general(
            block, block, (((1,), (1,)), ((), ())), preferred_element_type=F32
        )

    own_gram[...] = jnp.zeros_like(own_gram)
    for patch in range(2):
        total = lax.fori_loop(32 * patch, 32 * patch + 32, gram_rows, jnp.zeros((48, 48), F32))
        own_gram[:, patch * 64 : patch * 64 + 48] = total

    each_sent(gram_copy, lambda copy: copy.start())
    each_received(gram_copy)

    lane = lax.broadcasted_iota(jnp.int32, (48, 128), 1)
    sub = lax.broadcasted_iota(jnp.int32, (48, 128), 0)
    beside = own_gram[...] + near_gram[0] + near_gram[1]
    from_below = near_gram[2] + near_gram[4] + near_gram[5]
    from_above = near_gram[3] + near_gram[6] + near_gram[7]
    moved = beside + jnp.where(lane < 64, from_below, from_above)
    system = beside + pltpu.roll(moved, 64, 1)
    half_lane = lane % 64
    diagonal = jnp.logical_and(sub == half_lane, sub < 45)
    on_diagonal = jnp.where(diagonal, system, 0.0)
    trace_upper = jnp.sum(jnp.where(lane < 64, on_diagonal, 0.0))
    trace_lower = jnp.sum(jnp.where(lane < 64, 0.0, on_diagonal))
    ridge = jnp.where(lane < 64, trace_upper, trace_lower) * (RIDGE / 45.0)
    system = jnp.where(diagonal, system + ridge, system)

    def eliminate(step, system):
        pivot_row = jnp.sum(jnp.where(sub == step, system, 0.0), 0, keepdims=True)
        pick = (lane - half_lane) + step
        column = jnp.take_along_axis(system, pick, axis=1)
        pivot = jnp.sum(jnp.where(sub == step, column, 0.0), 0, keepdims=True)
        scaled = column * (1.0 / pivot)
        return jnp.where(half_lane == step, scaled, system - scaled * pivot_row)

    system = lax.fori_loop(0, 45, eliminate, system)
    answer = jnp.where(jnp.logical_and(half_lane[47:48] < 45, lane[47:48] < 128), system[TARGET : TARGET + 1], 0.0)
    terms = power[...] * answer
    upper_terms = jnp.sum(jnp.where(lane < 64, terms, 0.0), 1, keepdims=True)
    lower_terms = jnp.sum(jnp.where(lane < 64, 0.0, terms), 1, keepdims=True)
    powers = (jnp.sum(upper_terms * upper_terms), jnp.sum(lower_terms * lower_terms))

    coarse = answer.astype(BF16)
    fine = (answer - coarse.astype(F32)).astype(BF16)
    row_of = lax.broadcasted_iota(jnp.int32, (32, 768), 0)
    lane_of = lax.broadcasted_iota(jnp.int32, (32, 768), 1)
    chosen = lane_of // 48 == row_of % 16
    both = jnp.concatenate(
        [jnp.broadcast_to(coarse.astype(F32), (16, 128)), jnp.broadcast_to(fine.astype(F32), (16, 128))], 0
    ).astype(BF16)
    for patch in range(2):
        coefficients = jnp.where(
            chosen, jnp.dot(both, spread[patch], preferred_element_type=F32), 0.0
        ).astype(BF16)
        kernel_power = powers[patch]

        def finish(number, carry):
            rows = pl.ds(pl.multiple_of(number * 16, 16), 16)
            product = jnp.dot(coefficients, conv[rows].reshape(768, 256), preferred_element_type=F32)
            model = product[0:16] + product[16:32]
            mask = coverage[rows].astype(F32)
            difference[rows] = mask * (science[rows] - model)
            variance[rows] = mask * (science_var[rows] + kernel_power * template_var[rows])
            return carry

        lax.fori_loop(16 * patch, 16 * patch + 16, finish, 0)

    each_sent(halo, lambda copy: copy.wait_send())
    each_sent(gram_copy, lambda copy: copy.wait_send())


def local(template, template_var, coverage, exposure, exposure_var, strip_owner, strip_slot):
    def blocks(array):
        return array.reshape(128, 4, 2, 128).transpose(0, 2, 1, 3).reshape(128, 8, 128)

    vmem = pl.BlockSpec(memory_space=pltpu.VMEM)
    dma = pltpu.SemaphoreType.DMA
    return pl.pallas_call(
        kernel,
        out_shape=[jax.ShapeDtypeStruct((512, 256), F32)] * 2,
        in_specs=[vmem] * 11,
        out_specs=[vmem] * 2,
        scratch_shapes=[
            pltpu.VMEM((544, 512), BF16),
            pltpu.VMEM((16, 608, 256), BF16),
            pltpu.VMEM((512, 48, 256), BF16),
            pltpu.VMEM((128, 16, 128), BF16),
            pltpu.VMEM((128, 16, 128), BF16),
            pltpu.VMEM((128, 128), jnp.int32),
            pltpu.VMEM((512, 256), F32),
            pltpu.VMEM((512, 256), F32),
            pltpu.VMEM((512, 256), F32),
            pltpu.VMEM((48, 128), F32),
            pltpu.VMEM((8, 48, 128), F32),
            pltpu.VMEM((8, 128), jnp.int32),
            pltpu.SMEM((8, 128), jnp.int32),
            pltpu.SMEM((8, 128), jnp.int32),
            dma((8,)), dma((8,)), dma, dma, dma((2,)), dma((2,)), dma((8,)), dma((8,)),
        ],
        compiler_params=pltpu.CompilerParams(
            collective_id=0, has_side_effects=True, vmem_limit_bytes=60 * 1024 * 1024
        ),
        cost_estimate=pl.CostEstimate(flops=10**10, bytes_accessed=8 * 10**6, transcendentals=0),
    )(
        template, template_var, coverage, blocks(exposure), blocks(exposure_var), strip_owner, strip_slot,
        *[jnp.asarray(table) for table in tables()],
    )


def solution(mesh):
    image = P("row", "col")
    strips = P("row", "col", None, None)
    return jax.shard_map(
        local,
        mesh=mesh,
        in_specs=(image, image, image, strips, strips, image, image),
        out_specs=(image, image),
        check_vma=False,
    )
```

```python
import jax
import jax.numpy as jnp
import numpy as np
from jax import lax
from jax.experimental import pallas as pl
from jax.experimental.pallas import tpu as pltpu
from jax.sharding import PartitionSpec as P

RIDGE = 0.05
SIGMAS = (1.0, 2.0, 4.0)
MESH = pl.DeviceIdType.MESH
F32 = jnp.float32
BF16 = jnp.bfloat16

SLOTS = (
    (0, 0), (0, 2), (1, 0), (1, 2), (2, 0), (2, 2), (0, 1), (1, 1),
    (2, 1), (0, 3), (1, 3), None, (2, 3), (0, 4), (1, 4), (2, 4),
)
GROUP_OF_PASS = (0, 1, 2, 3, 4, 4, 5, 5)
BLOCK = 96
TARGET = 47
DIRECTIONS = ((0, -1), (0, 1), (-1, 0), (1, 0), (-1, -1), (-1, 1), (1, -1), (1, 1))


def filter_bank():
    taps = np.arange(31) - 15.0
    collected = []
    for sigma in SIGMAS:
        for degree in range(5):
            scaled = taps / sigma
            shape = scaled**degree * np.exp(-0.5 * scaled * scaled)
            collected.append(shape / np.sqrt(np.sum(shape * shape)))
    return np.array(collected, np.float32).astype(jnp.bfloat16).astype(np.float32)


def tables():
    bank = filter_bank()
    x_weights = np.zeros((8, 256, 2, 128), np.float32)
    y_weights = np.zeros((8, BLOCK, 8, 2, 128), np.float32)
    across = np.arange(128)
    down = np.arange(BLOCK)
    order = []
    filled = [0] * 6
    for number, slot in enumerate(SLOTS):
        if slot is None:
            continue
        half, which = number // 2, number % 2
        s, i = slot
        group = GROUP_OF_PASS[half]
        for q in range(31):
            x_weights[half, across + q - 15 + 64, which, across] = bank[s * 5 + i, q]
        for j in range(5 - i):
            lane = filled[group]
            filled[group] += 1
            order.append((group * 8 + lane, s, i, j))
            for p in range(31):
                y_weights[half, down, lane, which, down + p - 15 + 16] = bank[s * 5 + j, p]
    shapes = np.zeros((48, 31 * 31), np.float64)
    for t, s, i, j in order:
        shapes[t] = np.outer(bank[s * 5 + j], bank[s * 5 + i]).reshape(-1).astype(np.float64)
    values, vectors = np.linalg.eigh(shapes @ shapes.T)
    root = np.sqrt(np.maximum(values, 0.0))[:, None] * vectors.T
    power = np.zeros((48, 128), np.float32)
    power[:, :48] = root
    power[:, 64:112] = root
    spread = np.zeros((2, 128, 768), np.float32)
    for patch in range(2):
        spread[patch, 64 * patch + np.arange(768) % 48, np.arange(768)] = 1.0
    return (
        x_weights.reshape(8, 256, 256).astype(jnp.bfloat16),
        y_weights.reshape(8, BLOCK * 8, 256).astype(jnp.bfloat16),
        power,
        spread.astype(jnp.bfloat16),
    )


def inverse_row(columns, size=128):
    rows = lax.broadcasted_iota(jnp.int32, (size, size), 0)
    lanes = lax.broadcasted_iota(jnp.int32, (size, size), 1)
    return jnp.max(jnp.where(columns == lanes, rows, 0), 0, keepdims=True)


def within(number):
    return jnp.clip(number, 0, 127)


def kernel(
    template, template_var, coverage, flux, noise, owner, slot, x_weights, y_weights, power, spread,
    difference, variance,
    wide, filtered, conv, send, recv, labels, science, science_var, root, own_gram, near_gram,
    row_index, table_in, table_out,
    halo_out, halo_in, part_out, part_in, label_out, label_in, gram_out, gram_in,
):
    r = lax.axis_index("row")
    c = lax.axis_index("col")
    x, z, k = c // 8, (c // 2) % 4, c % 2
    me = r * 32 + c
    place = (z * 2 + k) * 16 + r * 4 + x
    barrier = pltpu.get_barrier_semaphore()

    wide[...] = jnp.zeros_like(wide)
    near_gram[...] = jnp.zeros_like(near_gram)

    def greet(step, carry):
        other = lax.rem(me + step, 128)
        pl.semaphore_signal(barrier, inc=1, device_id=(other // 32, other % 32), device_id_type=MESH)
        return carry

    lax.fori_loop(1, 128, greet, 0)

    wide[16:528, 128:384] = template[...].astype(BF16)
    labels[pl.ds(place, 1), :] = slot[...]
    columns = jnp.transpose(jnp.broadcast_to(owner[...], (128, 128)))
    row_index[...] = jnp.broadcast_to(inverse_row(columns), (8, 128))
    pltpu.sync_copy(row_index, table_in)

    def pack(number, carry):
        block = within(table_in[0, number])
        send[number] = jnp.concatenate([flux[block], noise[block]], 0).astype(BF16)
        return carry

    lax.fori_loop(0, 128, pack, 0, unroll=4)
    recv[place] = send[me]
    filtered[:, 544:608, :] = jnp.zeros((16, 64, 256), BF16)
    pl.semaphore_wait(barrier, 127)

    def inside(dr, dc):
        return jnp.logical_and(
            jnp.logical_and(r + dr >= 0, r + dr < 4), jnp.logical_and(c + dc >= 0, c + dc < 32)
        )

    def target(dr, dc):
        return (jnp.clip(r + dr, 0, 3), jnp.clip(c + dc, 0, 31))

    source_rows = {-1: pl.ds(16, 16), 0: pl.ds(16, 512), 1: pl.ds(512, 16)}
    target_rows = {-1: pl.ds(528, 16), 0: pl.ds(16, 512), 1: pl.ds(0, 16)}
    source_cols = {-1: pl.ds(128, 128), 0: pl.ds(128, 256), 1: pl.ds(256, 128)}
    target_cols = {-1: pl.ds(384, 128), 0: pl.ds(128, 256), 1: pl.ds(0, 128)}

    def halo(number):
        dr, dc = DIRECTIONS[number]
        return pltpu.make_async_remote_copy(
            src_ref=wide.at[source_rows[dr], source_cols[dc]],
            dst_ref=wide.at[target_rows[dr], target_cols[dc]],
            send_sem=halo_out.at[number],
            recv_sem=halo_in.at[number],
            device_id=target(dr, dc),
            device_id_type=MESH,
        )

    def gram_copy(number):
        dr, dc = DIRECTIONS[number]
        return pltpu.make_async_remote_copy(
            src_ref=own_gram,
            dst_ref=near_gram.at[number],
            send_sem=gram_out.at[number],
            recv_sem=gram_in.at[number],
            device_id=target(dr, dc),
            device_id_type=MESH,
        )

    def each_sent(make, action):
        for number, (dr, dc) in enumerate(DIRECTIONS):
            @pl.when(inside(dr, dc))
            def _():
                action(make(number))

    def each_received(make):
        for number, (dr, dc) in enumerate(DIRECTIONS):
            @pl.when(inside(-dr, -dc))
            def _():
                make(number).wait_recv()

    each_sent(halo, lambda copy: copy.start())

    def label_copy(first, count, row, col, which):
        return pltpu.make_async_remote_copy(
            src_ref=labels.at[pl.ds(first, count)],
            dst_ref=labels.at[pl.ds(first, count)],
            send_sem=label_out.at[which],
            recv_sem=label_in.at[which],
            device_id=(row, col),
            device_id_type=MESH,
        )

    for dr in range(4):
        for dx in range(4):
            if dr or dx:
                label_copy(place, 1, (r + dr) % 4, ((x + dx) % 4) * 8 + z * 2 + k, 0).start()

    def send_part(step, carry):
        other = lax.rem(me + step, 128)
        pltpu.make_async_remote_copy(
            src_ref=send.at[other],
            dst_ref=recv.at[place],
            send_sem=part_out,
            recv_sem=part_in,
            device_id=(other // 32, other % 32),
            device_id_type=MESH,
        ).start()
        return carry

    lax.fori_loop(1, 128, send_part, 0)

    each_received(halo)

    whole = wide[...]
    windows = (whole[:, 64:320], whole[:, 192:448])

    def along_x(half, carry):
        for side in range(2):
            product = jnp.dot(windows[side], x_weights[half], preferred_element_type=F32).astype(BF16)
            for which in range(2):
                filtered[2 * half + which, 0:544, side * 128 : side * 128 + 128] = product[
                    :, which * 128 : which * 128 + 128
                ]
        return carry

    lax.fori_loop(0, 8, along_x, 0, unroll=True)

    def label_wait(count, which):
        part = labels.at[pl.ds(0, count)]
        pltpu.make_async_copy(part, part, label_in.at[which]).wait()
        pltpu.make_async_copy(part, part, label_out.at[which]).wait()

    label_wait(15, 0)
    for dz in range(4):
        for dk in range(2):
            if dz or dk:
                label_copy(
                    pl.multiple_of((z * 2 + k) * 16, 16), 16, r, x * 8 + ((z + dz) % 4) * 2 + (k + dk) % 2, 1
                ).start()

    def along_y(first, rows):
        for pair in range(3):
            groups = []
            for group in (2 * pair, 2 * pair + 1):
                total = None
                for half in range(8):
                    if GROUP_OF_PASS[half] == group:
                        window = filtered[2 * half : 2 * half + 2, pl.ds(first, 128), :].reshape(256, 256)
                        product = jnp.dot(
                            y_weights[half, 0 : rows * 8, :], window, preferred_element_type=F32
                        )
                        total = product if total is None else total + product
                groups.append(total.reshape(rows, 8, 256))
            conv[pl.ds(first, rows), pair * 16 : pair * 16 + 16, :] = jnp.concatenate(groups, 1).astype(BF16)

    def y_block(number, carry):
        along_y(pl.multiple_of(number * BLOCK, 16), BLOCK)
        return carry

    lax.fori_loop(0, 5, y_block, 0, unroll=True)
    along_y(480, 32)

    label_wait(112, 1)
    row_index[...] = jnp.broadcast_to(inverse_row(labels[...]), (8, 128))
    pltpu.sync_copy(row_index, table_out)
    parts = recv.at[pl.ds(0, 127)]
    pltpu.make_async_copy(parts, parts, part_in).wait()
    pltpu.make_async_copy(parts, parts, part_out).wait()

    def unpack(number, carry):
        upper = recv[within(table_out[0, 2 * number])].astype(F32)
        lower = recv[within(table_out[0, 2 * number + 1])].astype(F32)
        rows = pl.ds(pl.multiple_of(number * 8, 8), 8)
        science[rows, 0:128] = jnp.concatenate([upper[0:4], lower[0:4]], 0)
        science[rows, 128:256] = jnp.concatenate([upper[4:8], lower[4:8]], 0)
        science_var[rows, 0:128] = jnp.concatenate([upper[8:12], lower[8:12]], 0)
        science_var[rows, 128:256] = jnp.concatenate([upper[12:16], lower[12:16]], 0)
        return carry

    lax.fori_loop(0, 64, unpack, 0, unroll=4)
    root[...] = coverage[...].astype(F32) * lax.rsqrt(science_var[...])

    is_target = lax.broadcasted_iota(jnp.int32, (16, 256), 0) == TARGET - 32

    def gram_rows(number, total):
        base = pl.multiple_of(number * 64, 64)
        pieces = []
        for row in range(64):
            weight = root[pl.ds(base + row, 1), :]
            goal = weight * science[pl.ds(base + row, 1), :]
            basis = conv[base + row].astype(F32) * weight
            last = jnp.where(is_target, goal, basis[32:48])
            pieces.append(jnp.concatenate([basis[0:32].astype(BF16), last.astype(BF16)], 0))
        block = jnp.concatenate(pieces, 1)
        return total + lax.dot_general(
            block, block, (((1,), (1,)), ((), ())), preferred_element_type=F32
        )

    own_gram[...] = jnp.zeros_like(own_gram)
    for patch in range(2):
        total = lax.fori_loop(4 * patch, 4 * patch + 4, gram_rows, jnp.zeros((48, 48), F32))
        own_gram[:, patch * 64 : patch * 64 + 48] = total

    each_sent(gram_copy, lambda copy: copy.start())
    each_received(gram_copy)

    lane = lax.broadcasted_iota(jnp.int32, (48, 128), 1)
    sub = lax.broadcasted_iota(jnp.int32, (48, 128), 0)
    beside = own_gram[...] + near_gram[0] + near_gram[1]
    from_below = near_gram[2] + near_gram[4] + near_gram[5]
    from_above = near_gram[3] + near_gram[6] + near_gram[7]
    moved = beside + jnp.where(lane < 64, from_below, from_above)
    system = beside + pltpu.roll(moved, 64, 1)
    half_lane = lane % 64
    diagonal = jnp.logical_and(sub == half_lane, sub < 45)
    on_diagonal = jnp.where(diagonal, system, 0.0)
    trace_upper = jnp.sum(jnp.where(lane < 64, on_diagonal, 0.0))
    trace_lower = jnp.sum(jnp.where(lane < 64, 0.0, on_diagonal))
    ridge = jnp.where(lane < 64, trace_upper, trace_lower) * (RIDGE / 45.0)
    system = jnp.where(diagonal, system + ridge, system)

    for step in range(45):
        column = jnp.take_along_axis(system, (lane - half_lane) + step, axis=1)
        inverse = 1.0 / column[step : step + 1]
        system = jnp.where(
            half_lane == step, column * inverse, system - column * (inverse * system[step : step + 1])
        )
    answer = jnp.where(jnp.logical_and(half_lane[47:48] < 45, lane[47:48] < 128), system[TARGET : TARGET + 1], 0.0)
    terms = power[...] * answer
    upper_terms = jnp.sum(jnp.where(lane < 64, terms, 0.0), 1, keepdims=True)
    lower_terms = jnp.sum(jnp.where(lane < 64, 0.0, terms), 1, keepdims=True)
    powers = (jnp.sum(upper_terms * upper_terms), jnp.sum(lower_terms * lower_terms))

    coarse = answer.astype(BF16)
    fine = (answer - coarse.astype(F32)).astype(BF16)
    row_of = lax.broadcasted_iota(jnp.int32, (32, 768), 0)
    lane_of = lax.broadcasted_iota(jnp.int32, (32, 768), 1)
    chosen = lane_of // 48 == row_of % 16
    both = jnp.concatenate(
        [jnp.broadcast_to(coarse.astype(F32), (16, 128)), jnp.broadcast_to(fine.astype(F32), (16, 128))], 0
    ).astype(BF16)
    for patch in range(2):
        coefficients = jnp.where(
            chosen, jnp.dot(both, spread[patch], preferred_element_type=F32), 0.0
        ).astype(BF16)
        kernel_power = powers[patch]

        def finish(number, carry):
            rows = pl.ds(pl.multiple_of(number * 16, 16), 16)
            product = jnp.dot(coefficients, conv[rows].reshape(768, 256), preferred_element_type=F32)
            model = product[0:16] + product[16:32]
            mask = coverage[rows].astype(F32)
            difference[rows] = mask * (science[rows] - model)
            variance[rows] = mask * (science_var[rows] + kernel_power * template_var[rows])
            return carry

        lax.fori_loop(16 * patch, 16 * patch + 16, finish, 0, unroll=8)

    each_sent(halo, lambda copy: copy.wait_send())
    each_sent(gram_copy, lambda copy: copy.wait_send())


def local(template, template_var, coverage, exposure, exposure_var, strip_owner, strip_slot):
    def blocks(array):
        return array.reshape(128, 4, 2, 128).transpose(0, 2, 1, 3).reshape(128, 8, 128)

    vmem = pl.BlockSpec(memory_space=pltpu.VMEM)
    dma = pltpu.SemaphoreType.DMA
    return pl.pallas_call(
        kernel,
        out_shape=[jax.ShapeDtypeStruct((512, 256), F32)] * 2,
        in_specs=[vmem] * 11,
        out_specs=[vmem] * 2,
        scratch_shapes=[
            pltpu.VMEM((544, 512), BF16),
            pltpu.VMEM((16, 608, 256), BF16),
            pltpu.VMEM((512, 48, 256), BF16),
            pltpu.VMEM((128, 16, 128), BF16),
            pltpu.VMEM((128, 16, 128), BF16),
            pltpu.VMEM((128, 128), jnp.int32),
            pltpu.VMEM((512, 256), F32),
            pltpu.VMEM((512, 256), F32),
            pltpu.VMEM((512, 256), F32),
            pltpu.VMEM((48, 128), F32),
            pltpu.VMEM((8, 48, 128), F32),
            pltpu.VMEM((8, 128), jnp.int32),
            pltpu.SMEM((8, 128), jnp.int32),
            pltpu.SMEM((8, 128), jnp.int32),
            dma((8,)), dma((8,)), dma, dma, dma((2,)), dma((2,)), dma((8,)), dma((8,)),
        ],
        compiler_params=pltpu.CompilerParams(
            collective_id=0, has_side_effects=True, vmem_limit_bytes=60 * 1024 * 1024
        ),
        cost_estimate=pl.CostEstimate(flops=10**10, bytes_accessed=8 * 10**6, transcendentals=0),
    )(
        template, template_var, coverage, blocks(exposure), blocks(exposure_var), strip_owner, strip_slot,
        *[jnp.asarray(table) for table in tables()],
    )


def solution(mesh):
    image = P("row", "col")
    strips = P("row", "col", None, None)
    return jax.shard_map(
        local,
        mesh=mesh,
        in_specs=(image, image, image, strips, strips, image, image),
        out_specs=(image, image),
        check_vma=False,
    )
```

```python
import jax
import jax.numpy as jnp
import numpy as np
from jax import lax
from jax.experimental import pallas as pl
from jax.experimental.pallas import tpu as pltpu
from jax.sharding import PartitionSpec as P

RIDGE = 0.05
SIGMAS = (1.0, 2.0, 4.0)
MESH = pl.DeviceIdType.MESH
F32 = jnp.float32
BF16 = jnp.bfloat16

SLOTS = (
    (0, 0), (0, 2), (1, 0), (1, 2), (2, 0), (2, 2), (0, 1), (1, 1),
    (2, 1), (0, 3), (1, 3), None, (2, 3), (0, 4), (1, 4), (2, 4),
)
GROUP_OF_PASS = (0, 1, 2, 3, 4, 4, 5, 5)
BLOCK = 96
TARGET = 47
DIRECTIONS = ((0, -1), (0, 1), (-1, 0), (1, 0), (-1, -1), (-1, 1), (1, -1), (1, 1))


def filter_bank():
    taps = np.arange(31) - 15.0
    collected = []
    for sigma in SIGMAS:
        for degree in range(5):
            scaled = taps / sigma
            shape = scaled**degree * np.exp(-0.5 * scaled * scaled)
            collected.append(shape / np.sqrt(np.sum(shape * shape)))
    return np.array(collected, np.float32).astype(jnp.bfloat16).astype(np.float32)


def tables():
    bank = filter_bank()
    x_weights = np.zeros((8, 256, 2, 128), np.float32)
    y_weights = np.zeros((8, BLOCK, 8, 2, 128), np.float32)
    across = np.arange(128)
    down = np.arange(BLOCK)
    order = []
    filled = [0] * 6
    for number, slot in enumerate(SLOTS):
        if slot is None:
            continue
        half, which = number // 2, number % 2
        s, i = slot
        group = GROUP_OF_PASS[half]
        for q in range(31):
            x_weights[half, across + q - 15 + 64, which, across] = bank[s * 5 + i, q]
        for j in range(5 - i):
            lane = filled[group]
            filled[group] += 1
            order.append((group * 8 + lane, s, i, j))
            for p in range(31):
                y_weights[half, down, lane, which, down + p - 15 + 16] = bank[s * 5 + j, p]
    shapes = np.zeros((48, 31 * 31), np.float64)
    for t, s, i, j in order:
        shapes[t] = np.outer(bank[s * 5 + j], bank[s * 5 + i]).reshape(-1).astype(np.float64)
    values, vectors = np.linalg.eigh(shapes @ shapes.T)
    root = np.sqrt(np.maximum(values, 0.0))[:, None] * vectors.T
    power = np.zeros((48, 128), np.float32)
    power[:, :48] = root
    power[:, 64:112] = root
    spread = np.zeros((2, 128, 768), np.float32)
    for patch in range(2):
        spread[patch, 64 * patch + np.arange(768) % 48, np.arange(768)] = 1.0
    return (
        x_weights.reshape(8, 256, 256).astype(jnp.bfloat16),
        y_weights.reshape(8, BLOCK * 8, 256).astype(jnp.bfloat16),
        power,
        spread.astype(jnp.bfloat16),
    )


def inverse_row(columns, size=128):
    rows = lax.broadcasted_iota(jnp.int32, (size, size), 0)
    lanes = lax.broadcasted_iota(jnp.int32, (size, size), 1)
    return jnp.max(jnp.where(columns == lanes, rows, 0), 0, keepdims=True)


def within(number):
    return jnp.clip(number, 0, 127)


def kernel(
    template_hbm, template_var_hbm, coverage_hbm, flux_hbm, noise_hbm, x_weights_hbm, y_weights_hbm, spread_hbm,
    owner, slot, power,
    residual_hbm, spread_var_hbm,
    template, template_var, coverage, flux, noise, x_weights, y_weights, spread, residual, spread_var,
    wide, filtered, conv, send, recv, labels, science, science_var, root, own_gram, near_gram,
    row_index, table_in, table_out,
    halo_out, halo_in, part_out, part_in, label_out, label_in, gram_out, gram_in, load_in, store_out,
):
    r = lax.axis_index("row")
    c = lax.axis_index("col")
    x, z, k = c // 8, (c // 2) % 4, c % 2
    me = r * 32 + c
    place = (z * 2 + k) * 16 + r * 4 + x
    barrier = pltpu.get_barrier_semaphore()

    loads = [
        pltpu.make_async_copy(source, held, load_in.at[number])
        for number, (source, held) in enumerate((
            (flux_hbm, flux), (noise_hbm, noise), (template_hbm, template), (x_weights_hbm, x_weights),
            (y_weights_hbm, y_weights), (coverage_hbm, coverage), (template_var_hbm, template_var), (spread_hbm, spread),
        ))
    ]
    for load in loads:
        load.start()

    wide[...] = jnp.zeros_like(wide)
    near_gram[...] = jnp.zeros_like(near_gram)

    def greet(step, carry):
        other = lax.rem(me + step, 128)
        pl.semaphore_signal(barrier, inc=1, device_id=(other // 32, other % 32), device_id_type=MESH)
        return carry

    lax.fori_loop(1, 128, greet, 0)

    labels[pl.ds(place, 1), :] = slot[...]
    owners = jnp.transpose(jnp.broadcast_to(owner[...], (128, 128)))
    row_index[...] = jnp.broadcast_to(inverse_row(owners), (8, 128))
    pltpu.sync_copy(row_index, table_in)
    loads[2].wait()
    wide[16:528, 128:384] = template[...].astype(BF16)
    loads[0].wait()
    loads[1].wait()

    def pack(number, carry):
        block = within(table_in[0, number])
        send[number] = jnp.concatenate([flux[block], noise[block]], 0).astype(BF16)
        return carry

    lax.fori_loop(0, 128, pack, 0, unroll=4)
    recv[place] = send[me]
    filtered[:, 544:608, :] = jnp.zeros((16, 64, 256), BF16)
    pl.semaphore_wait(barrier, 127)

    def inside(dr, dc):
        return jnp.logical_and(
            jnp.logical_and(r + dr >= 0, r + dr < 4), jnp.logical_and(c + dc >= 0, c + dc < 32)
        )

    def target(dr, dc):
        return (jnp.clip(r + dr, 0, 3), jnp.clip(c + dc, 0, 31))

    source_rows = {-1: pl.ds(16, 16), 0: pl.ds(16, 512), 1: pl.ds(512, 16)}
    target_rows = {-1: pl.ds(528, 16), 0: pl.ds(16, 512), 1: pl.ds(0, 16)}
    source_cols = {-1: pl.ds(128, 128), 0: pl.ds(128, 256), 1: pl.ds(256, 128)}
    target_cols = {-1: pl.ds(384, 128), 0: pl.ds(128, 256), 1: pl.ds(0, 128)}

    def halo(number):
        dr, dc = DIRECTIONS[number]
        return pltpu.make_async_remote_copy(
            src_ref=wide.at[source_rows[dr], source_cols[dc]],
            dst_ref=wide.at[target_rows[dr], target_cols[dc]],
            send_sem=halo_out.at[number],
            recv_sem=halo_in.at[number],
            device_id=target(dr, dc),
            device_id_type=MESH,
        )

    def gram_copy(number):
        dr, dc = DIRECTIONS[number]
        return pltpu.make_async_remote_copy(
            src_ref=own_gram,
            dst_ref=near_gram.at[number],
            send_sem=gram_out.at[number],
            recv_sem=gram_in.at[number],
            device_id=target(dr, dc),
            device_id_type=MESH,
        )

    def each_sent(make, action):
        for number, (dr, dc) in enumerate(DIRECTIONS):
            @pl.when(inside(dr, dc))
            def _():
                action(make(number))

    def each_received(make):
        for number, (dr, dc) in enumerate(DIRECTIONS):
            @pl.when(inside(-dr, -dc))
            def _():
                make(number).wait_recv()

    each_sent(halo, lambda copy: copy.start())

    def label_copy(first, count, row, col, which):
        return pltpu.make_async_remote_copy(
            src_ref=labels.at[pl.ds(first, count)],
            dst_ref=labels.at[pl.ds(first, count)],
            send_sem=label_out.at[which],
            recv_sem=label_in.at[which],
            device_id=(row, col),
            device_id_type=MESH,
        )

    for dr in range(4):
        for dx in range(4):
            if dr or dx:
                label_copy(place, 1, (r + dr) % 4, ((x + dx) % 4) * 8 + z * 2 + k, 0).start()

    def send_part(step, carry):
        other = lax.rem(me + step, 128)
        pltpu.make_async_remote_copy(
            src_ref=send.at[other],
            dst_ref=recv.at[place],
            send_sem=part_out,
            recv_sem=part_in,
            device_id=(other // 32, other % 32),
            device_id_type=MESH,
        ).start()
        return carry

    lax.fori_loop(1, 128, send_part, 0)

    each_received(halo)

    loads[3].wait()
    whole = wide[...]
    windows = (whole[:, 64:320], whole[:, 192:448])

    def along_x(half, carry):
        for side in range(2):
            product = jnp.dot(windows[side], x_weights[half], preferred_element_type=F32).astype(BF16)
            for which in range(2):
                filtered[2 * half + which, 0:544, side * 128 : side * 128 + 128] = product[
                    :, which * 128 : which * 128 + 128
                ]
        return carry

    lax.fori_loop(0, 8, along_x, 0, unroll=True)

    def label_wait(count, which):
        part = labels.at[pl.ds(0, count)]
        pltpu.make_async_copy(part, part, label_in.at[which]).wait()
        pltpu.make_async_copy(part, part, label_out.at[which]).wait()

    label_wait(15, 0)
    for dz in range(4):
        for dk in range(2):
            if dz or dk:
                label_copy(
                    pl.multiple_of((z * 2 + k) * 16, 16), 16, r, x * 8 + ((z + dz) % 4) * 2 + (k + dk) % 2, 1
                ).start()

    def along_y(first, rows):
        for pair in range(3):
            groups = []
            for group in (2 * pair, 2 * pair + 1):
                total = None
                for half in range(8):
                    if GROUP_OF_PASS[half] == group:
                        window = filtered[2 * half : 2 * half + 2, pl.ds(first, 128), :].reshape(256, 256)
                        product = jnp.dot(
                            y_weights[half, 0 : rows * 8, :], window, preferred_element_type=F32
                        )
                        total = product if total is None else total + product
                groups.append(total.reshape(rows, 8, 256))
            conv[pl.ds(first, rows), pair * 16 : pair * 16 + 16, :] = jnp.concatenate(groups, 1).astype(BF16)

    loads[4].wait()

    def y_block(number, carry):
        along_y(pl.multiple_of(number * BLOCK, 16), BLOCK)
        return carry

    lax.fori_loop(0, 5, y_block, 0, unroll=True)
    along_y(480, 32)

    label_wait(112, 1)
    row_index[...] = jnp.broadcast_to(inverse_row(labels[...]), (8, 128))
    pltpu.sync_copy(row_index, table_out)
    parts = recv.at[pl.ds(0, 127)]
    pltpu.make_async_copy(parts, parts, part_in).wait()
    pltpu.make_async_copy(parts, parts, part_out).wait()

    def unpack(number, carry):
        upper = recv[within(table_out[0, 2 * number])].astype(F32)
        lower = recv[within(table_out[0, 2 * number + 1])].astype(F32)
        rows = pl.ds(pl.multiple_of(number * 8, 8), 8)
        science[rows, 0:128] = jnp.concatenate([upper[0:4], lower[0:4]], 0)
        science[rows, 128:256] = jnp.concatenate([upper[4:8], lower[4:8]], 0)
        science_var[rows, 0:128] = jnp.concatenate([upper[8:12], lower[8:12]], 0)
        science_var[rows, 128:256] = jnp.concatenate([upper[12:16], lower[12:16]], 0)
        return carry

    lax.fori_loop(0, 64, unpack, 0, unroll=4)
    loads[5].wait()
    root[...] = coverage[...].astype(F32) * lax.rsqrt(science_var[...])

    is_target = lax.broadcasted_iota(jnp.int32, (16, 256), 0) == TARGET - 32

    def gram_rows(number, total):
        base = pl.multiple_of(number * 64, 64)
        pieces = []
        for row in range(64):
            weight = root[pl.ds(base + row, 1), :]
            goal = weight * science[pl.ds(base + row, 1), :]
            basis = conv[base + row].astype(F32) * weight
            last = jnp.where(is_target, goal, basis[32:48])
            pieces.append(jnp.concatenate([basis[0:32].astype(BF16), last.astype(BF16)], 0))
        block = jnp.concatenate(pieces, 1)
        return total + lax.dot_general(
            block, block, (((1,), (1,)), ((), ())), preferred_element_type=F32
        )

    own_gram[...] = jnp.zeros_like(own_gram)
    for patch in range(2):
        total = lax.fori_loop(4 * patch, 4 * patch + 4, gram_rows, jnp.zeros((48, 48), F32))
        own_gram[:, patch * 64 : patch * 64 + 48] = total

    each_sent(gram_copy, lambda copy: copy.start())
    each_received(gram_copy)

    lane = lax.broadcasted_iota(jnp.int32, (48, 128), 1)
    sub = lax.broadcasted_iota(jnp.int32, (48, 128), 0)
    beside = own_gram[...] + near_gram[0] + near_gram[1]
    from_below = near_gram[2] + near_gram[4] + near_gram[5]
    from_above = near_gram[3] + near_gram[6] + near_gram[7]
    moved = beside + jnp.where(lane < 64, from_below, from_above)
    system = beside + pltpu.roll(moved, 64, 1)
    half_lane = lane % 64
    diagonal = jnp.logical_and(sub == half_lane, sub < 45)
    on_diagonal = jnp.where(diagonal, system, 0.0)
    trace_upper = jnp.sum(jnp.where(lane < 64, on_diagonal, 0.0))
    trace_lower = jnp.sum(jnp.where(lane < 64, 0.0, on_diagonal))
    ridge = jnp.where(lane < 64, trace_upper, trace_lower) * (RIDGE / 45.0)
    system = jnp.where(diagonal, system + ridge, system)

    def column_of(matrix, step):
        return jnp.take_along_axis(matrix, (lane - half_lane) + step, axis=1)

    def pivot_pair(first, second, step):
        a, b = first[step : step + 1], second[step : step + 1]
        c, d = first[step + 1 : step + 2], second[step + 1 : step + 2]
        inverse = 1.0 / (a * d - b * c)
        return first * (d * inverse) - second * (c * inverse), second * (a * inverse) - first * (b * inverse)

    for step in range(0, 44, 4):
        columns = [column_of(system, step + number) for number in range(4)]
        row = [system[step + number : step + number + 1] for number in range(4)]
        u0, u1 = pivot_pair(columns[0], columns[1], step)
        third, fourth = (
            column - u0 * column[step : step + 1] - u1 * column[step + 1 : step + 2] for column in columns[2:]
        )
        u2, u3 = pivot_pair(third, fourth, step + 2)
        row[2] = row[2] - u0[step + 2 : step + 3] * row[0] - u1[step + 2 : step + 3] * row[1]
        row[3] = row[3] - u0[step + 3 : step + 4] * row[0] - u1[step + 3 : step + 4] * row[1]
        v0 = u0 - u2 * u0[step + 2 : step + 3] - u3 * u0[step + 3 : step + 4]
        v1 = u1 - u2 * u1[step + 2 : step + 3] - u3 * u1[step + 3 : step + 4]
        system = system - u0 * row[0] - u1 * row[1] - u2 * row[2] - u3 * row[3]
        for number, column in enumerate((v0, v1, u2, u3)):
            system = jnp.where(half_lane == step + number, column, system)
    column = column_of(system, 44)
    inverse = 1.0 / column[44:45]
    system = jnp.where(half_lane == 44, column * inverse, system - column * (inverse * system[44:45]))
    answer = jnp.where(jnp.logical_and(half_lane[47:48] < 45, lane[47:48] < 128), system[TARGET : TARGET + 1], 0.0)
    terms = power[...] * answer
    upper_terms = jnp.sum(jnp.where(lane < 64, terms, 0.0), 1, keepdims=True)
    lower_terms = jnp.sum(jnp.where(lane < 64, 0.0, terms), 1, keepdims=True)
    powers = (jnp.sum(upper_terms * upper_terms), jnp.sum(lower_terms * lower_terms))

    coarse = answer.astype(BF16)
    fine = (answer - coarse.astype(F32)).astype(BF16)
    row_of = lax.broadcasted_iota(jnp.int32, (32, 768), 0)
    lane_of = lax.broadcasted_iota(jnp.int32, (32, 768), 1)
    chosen = lane_of // 48 == row_of % 16
    both = jnp.concatenate(
        [jnp.broadcast_to(coarse.astype(F32), (16, 128)), jnp.broadcast_to(fine.astype(F32), (16, 128))], 0
    ).astype(BF16)
    loads[6].wait()
    loads[7].wait()
    stores = []
    for patch in range(2):
        coefficients = jnp.where(
            chosen, jnp.dot(both, spread[patch], preferred_element_type=F32), 0.0
        ).astype(BF16)
        kernel_power = powers[patch]

        def finish(number, carry):
            rows = pl.ds(pl.multiple_of(number * 16, 16), 16)
            product = jnp.dot(coefficients, conv[rows].reshape(768, 256), preferred_element_type=F32)
            model = product[0:16] + product[16:32]
            residual[rows] = science[rows] - model
            spread_var[rows] = science_var[rows] + kernel_power * template_var[rows]
            return carry

        lax.fori_loop(16 * patch, 16 * patch + 16, finish, 0, unroll=8)
        part = pl.ds(256 * patch, 256)
        for number, (held, goal) in enumerate(((residual, residual_hbm), (spread_var, spread_var_hbm))):
            store = pltpu.make_async_copy(held.at[part], goal.at[part], store_out.at[2 * patch + number])
            store.start()
            stores.append(store)

    each_sent(halo, lambda copy: copy.wait_send())
    each_sent(gram_copy, lambda copy: copy.wait_send())
    for store in stores:
        store.wait()


def local(template, template_var, coverage, exposure, exposure_var, strip_owner, strip_slot):
    def blocks(array):
        return array.reshape(128, 4, 2, 128).transpose(0, 2, 1, 3).reshape(128, 8, 128)

    vmem = pl.BlockSpec(memory_space=pltpu.VMEM)
    hbm = pl.BlockSpec(memory_space=pltpu.HBM)
    dma = pltpu.SemaphoreType.DMA
    x_weights, y_weights, power, spread = [jnp.asarray(table) for table in tables()]
    residual, spread_var = pl.pallas_call(
        kernel,
        out_shape=[jax.ShapeDtypeStruct((512, 256), F32)] * 2,
        in_specs=[hbm] * 8 + [vmem] * 3,
        out_specs=[hbm] * 2,
        scratch_shapes=[
            pltpu.VMEM((512, 256), F32),
            pltpu.VMEM((512, 256), F32),
            pltpu.VMEM((512, 256), jnp.int32),
            pltpu.VMEM((128, 8, 128), F32),
            pltpu.VMEM((128, 8, 128), F32),
            pltpu.VMEM((8, 256, 256), BF16),
            pltpu.VMEM((8, BLOCK * 8, 256), BF16),
            pltpu.VMEM((2, 128, 768), BF16),
            pltpu.VMEM((512, 256), F32),
            pltpu.VMEM((512, 256), F32),
            pltpu.VMEM((544, 512), BF16),
            pltpu.VMEM((16, 608, 256), BF16),
            pltpu.VMEM((512, 48, 256), BF16),
            pltpu.VMEM((128, 16, 128), BF16),
            pltpu.VMEM((128, 16, 128), BF16),
            pltpu.VMEM((128, 128), jnp.int32),
            pltpu.VMEM((512, 256), F32),
            pltpu.VMEM((512, 256), F32),
            pltpu.VMEM((512, 256), F32),
            pltpu.VMEM((48, 128), F32),
            pltpu.VMEM((8, 48, 128), F32),
            pltpu.VMEM((8, 128), jnp.int32),
            pltpu.SMEM((8, 128), jnp.int32),
            pltpu.SMEM((8, 128), jnp.int32),
            dma((8,)), dma((8,)), dma, dma, dma((2,)), dma((2,)), dma((8,)), dma((8,)), dma((8,)), dma((4,)),
        ],
        compiler_params=pltpu.CompilerParams(
            collective_id=0, has_side_effects=True, vmem_limit_bytes=60 * 1024 * 1024
        ),
        cost_estimate=pl.CostEstimate(flops=10**10, bytes_accessed=8 * 10**6, transcendentals=0),
    )(
        template, template_var, coverage, blocks(exposure), blocks(exposure_var), x_weights, y_weights, spread,
        strip_owner, strip_slot, power,
    )
    mask = coverage.astype(F32)
    return (mask * residual, mask * spread_var)


def solution(mesh):
    image = P("row", "col")
    strips = P("row", "col", None, None)
    return jax.shard_map(
        local,
        mesh=mesh,
        in_specs=(image, image, image, strips, strips, image, image),
        out_specs=(image, image),
        check_vma=False,
    )
```

```python
import jax
import jax.numpy as jnp
import numpy as np
from jax import lax
from jax.experimental import pallas as pl
from jax.experimental.pallas import tpu as pltpu
from jax.sharding import PartitionSpec as P

RIDGE = 0.05
SIGMAS = (1.0, 2.0, 4.0)
MESH = pl.DeviceIdType.MESH
F32 = jnp.float32
BF16 = jnp.bfloat16

SLOTS = (
    (0, 0), (0, 2), (1, 0), (1, 2), (2, 0), (2, 2), (0, 1), (1, 1),
    (2, 1), (0, 3), (1, 3), None, (2, 3), (0, 4), (1, 4), (2, 4),
)
GROUP_OF_PASS = (0, 1, 2, 3, 4, 4, 5, 5)
BLOCK = 96
TARGET = 47
GRAM_COPIES = ((0, -1, 0), (1, 1, 0), (0, -1, -1), (0, -1, 1), (1, 1, -1), (1, 1, 1), (0, 0, -1), (0, 0, 1), (1, 0, -1), (1, 0, 1))
DIRECTIONS = ((0, -1), (0, 1), (-1, 0), (1, 0), (-1, -1), (-1, 1), (1, -1), (1, 1))


def filter_bank():
    taps = np.arange(31) - 15.0
    collected = []
    for sigma in SIGMAS:
        for degree in range(5):
            scaled = taps / sigma
            shape = scaled**degree * np.exp(-0.5 * scaled * scaled)
            collected.append(shape / np.sqrt(np.sum(shape * shape)))
    return np.array(collected, np.float32).astype(jnp.bfloat16).astype(np.float32)


def tables():
    bank = filter_bank()
    x_weights = np.zeros((8, 256, 2, 128), np.float32)
    y_weights = np.zeros((8, BLOCK, 8, 2, 128), np.float32)
    across = np.arange(128)
    down = np.arange(BLOCK)
    order = []
    filled = [0] * 6
    for number, slot in enumerate(SLOTS):
        if slot is None:
            continue
        half, which = number // 2, number % 2
        s, i = slot
        group = GROUP_OF_PASS[half]
        for q in range(31):
            x_weights[half, across + q - 15 + 64, which, across] = bank[s * 5 + i, q]
        for j in range(5 - i):
            lane = filled[group]
            filled[group] += 1
            order.append((group * 8 + lane, s, i, j))
            for p in range(31):
                y_weights[half, down, lane, which, down + p - 15 + 16] = bank[s * 5 + j, p]
    shapes = np.zeros((48, 31 * 31), np.float64)
    for t, s, i, j in order:
        shapes[t] = np.outer(bank[s * 5 + j], bank[s * 5 + i]).reshape(-1).astype(np.float64)
    values, vectors = np.linalg.eigh(shapes @ shapes.T)
    root = np.sqrt(np.maximum(values, 0.0))[:, None] * vectors.T
    power = np.zeros((48, 128), np.float32)
    power[:, :48] = root
    power[:, 64:112] = root
    spread = np.zeros((2, 128, 768), np.float32)
    for patch in range(2):
        spread[patch, 64 * patch + np.arange(768) % 48, np.arange(768)] = 1.0
    return (
        x_weights.reshape(8, 256, 256).astype(jnp.bfloat16),
        y_weights.reshape(8, BLOCK * 8, 256).astype(jnp.bfloat16),
        power,
        spread.astype(jnp.bfloat16),
    )


def inverse_row(columns, size=128):
    rows = lax.broadcasted_iota(jnp.int32, (size, size), 0)
    lanes = lax.broadcasted_iota(jnp.int32, (size, size), 1)
    return jnp.max(jnp.where(columns == lanes, rows, 0), 0, keepdims=True)


def within(number):
    return jnp.clip(number, 0, 127)


def kernel(
    template_hbm, template_var_hbm, coverage_hbm, flux_hbm, noise_hbm, x_weights_hbm, y_weights_hbm, spread_hbm,
    owner, slot, power,
    residual, spread_var,
    template, template_var, coverage, flux, noise, x_weights, y_weights, spread,
    wide, filtered, conv, send, recv, labels, science, science_var, root, own_gram, near_gram,
    row_index, table_in, table_out,
    halo_out, halo_in, part_out, part_in, label_out, label_in, gram_out, gram_in, load_in, ready,
):
    r = lax.axis_index("row")
    c = lax.axis_index("col")
    x, z, k = c // 8, (c // 2) % 4, c % 2
    me = r * 32 + c
    place = (z * 2 + k) * 16 + r * 4 + x
    barrier = pltpu.get_barrier_semaphore()

    loads = [
        pltpu.make_async_copy(source, held, load_in.at[number])
        for number, (source, held) in enumerate((
            (template_hbm, template), (flux_hbm, flux), (noise_hbm, noise), (x_weights_hbm, x_weights),
            (y_weights_hbm, y_weights), (coverage_hbm, coverage), (template_var_hbm, template_var), (spread_hbm, spread),
        ))
    ]
    for load in loads:
        load.start()

    wide[...] = jnp.zeros_like(wide)
    near_gram[...] = jnp.zeros_like(near_gram)
    own_gram[...] = jnp.zeros_like(own_gram)

    def column(dx, dz, dk):
        return (x + dx) % 4 * 8 + (z + dz) % 4 * 2 + (k + dk) % 2

    across = [((r + dr) % 4, column(dx, 0, 0)) for dr in range(4) for dx in range(4) if dr or dx]
    along = [(r, column(0, dz, dk)) for dz in range(4) for dk in range(2) if dz or dk]
    around = [((r + dr) % 4, (c + dc) % 32) for dr, dc in DIRECTIONS]
    for other in around + across + along:
        pl.semaphore_signal(barrier, inc=1, device_id=other, device_id_type=MESH)

    labels[pl.ds(place, 1), :] = slot[...]
    loads[0].wait()
    wide[16:528, 128:384] = template[...].astype(BF16)
    pl.semaphore_wait(barrier, 30)

    def inside(dr, dc):
        return jnp.logical_and(
            jnp.logical_and(r + dr >= 0, r + dr < 4), jnp.logical_and(c + dc >= 0, c + dc < 32)
        )

    def target(dr, dc):
        return (jnp.clip(r + dr, 0, 3), jnp.clip(c + dc, 0, 31))

    source_rows = {-1: pl.ds(16, 16), 0: pl.ds(16, 512), 1: pl.ds(512, 16)}
    target_rows = {-1: pl.ds(528, 16), 0: pl.ds(16, 512), 1: pl.ds(0, 16)}
    source_cols = {-1: pl.ds(128, 128), 0: pl.ds(128, 256), 1: pl.ds(256, 128)}
    target_cols = {-1: pl.ds(384, 128), 0: pl.ds(128, 256), 1: pl.ds(0, 128)}

    def halo(number):
        dr, dc = DIRECTIONS[number]
        return pltpu.make_async_remote_copy(
            src_ref=wide.at[source_rows[dr], source_cols[dc]],
            dst_ref=wide.at[target_rows[dr], target_cols[dc]],
            send_sem=halo_out.at[number],
            recv_sem=halo_in.at[number],
            device_id=target(dr, dc),
            device_id_type=MESH,
        )

    def gram_copy(number):
        patch, dr, dc = GRAM_COPIES[number]
        return pltpu.make_async_remote_copy(
            src_ref=own_gram.at[patch],
            dst_ref=near_gram.at[number],
            send_sem=gram_out.at[number],
            recv_sem=gram_in.at[number],
            device_id=target(dr, dc),
            device_id_type=MESH,
        )

    def grams_sent(action):
        for number, (_, dr, dc) in enumerate(GRAM_COPIES):
            @pl.when(inside(dr, dc))
            def _():
                action(gram_copy(number))

    def grams_received():
        for number, (_, dr, dc) in enumerate(GRAM_COPIES):
            @pl.when(inside(-dr, -dc))
            def _():
                gram_copy(number).wait_recv()

    def each_sent(make, action):
        for number, (dr, dc) in enumerate(DIRECTIONS):
            @pl.when(inside(dr, dc))
            def _():
                action(make(number))

    def each_received(make):
        for number, (dr, dc) in enumerate(DIRECTIONS):
            @pl.when(inside(-dr, -dc))
            def _():
                make(number).wait_recv()

    each_sent(halo, lambda copy: copy.start())

    def label_copy(first, count, row, col, which):
        return pltpu.make_async_remote_copy(
            src_ref=labels.at[pl.ds(first, count)],
            dst_ref=labels.at[pl.ds(first, count)],
            send_sem=label_out.at[which],
            recv_sem=label_in.at[which],
            device_id=(row, col),
            device_id_type=MESH,
        )

    for other in along:
        pl.semaphore_signal(ready, inc=1, device_id=other, device_id_type=MESH)
    for other in across:
        label_copy(place, 1, *other, 0).start()

    owners = jnp.transpose(jnp.broadcast_to(owner[...], (128, 128)))
    row_index[...] = jnp.broadcast_to(inverse_row(owners), (8, 128))
    pltpu.sync_copy(row_index, table_in)
    loads[1].wait()
    loads[2].wait()

    def pack(number, carry):
        block = within(table_in[0, number])
        send[number] = jnp.concatenate([flux[block], noise[block]], 0).astype(BF16)
        return carry

    lax.fori_loop(0, 128, pack, 0, unroll=4)
    recv[place] = send[me]
    pl.semaphore_wait(ready, 7)

    def send_part(step, carry):
        other = lax.rem(me + step, 128)
        pltpu.make_async_remote_copy(
            src_ref=send.at[other],
            dst_ref=recv.at[place],
            send_sem=part_out,
            recv_sem=part_in,
            device_id=(other // 32, other % 32),
            device_id_type=MESH,
        ).start()
        return carry

    lax.fori_loop(1, 128, send_part, 0)

    each_received(halo)

    filtered[:, 544:608, :] = jnp.zeros((16, 64, 256), BF16)
    loads[3].wait()
    whole = wide[...]
    windows = (whole[:, 64:320], whole[:, 192:448])

    def along_x(half, carry):
        for side in range(2):
            product = jnp.dot(windows[side], x_weights[half], preferred_element_type=F32).astype(BF16)
            for which in range(2):
                filtered[2 * half + which, 0:544, side * 128 : side * 128 + 128] = product[
                    :, which * 128 : which * 128 + 128
                ]
        return carry

    lax.fori_loop(0, 8, along_x, 0, unroll=True)

    def label_wait(count, which):
        part = labels.at[pl.ds(0, count)]
        pltpu.make_async_copy(part, part, label_in.at[which]).wait()
        pltpu.make_async_copy(part, part, label_out.at[which]).wait()

    label_wait(15, 0)
    for other in along:
        label_copy(pl.multiple_of((z * 2 + k) * 16, 16), 16, *other, 1).start()

    def along_y(first, rows):
        for pair in range(3):
            groups = []
            for group in (2 * pair, 2 * pair + 1):
                total = None
                for half in range(8):
                    if GROUP_OF_PASS[half] == group:
                        window = filtered[2 * half : 2 * half + 2, pl.ds(first, 128), :].reshape(256, 256)
                        product = jnp.dot(
                            y_weights[half, 0 : rows * 8, :], window, preferred_element_type=F32
                        )
                        total = product if total is None else total + product
                groups.append(total.reshape(rows, 8, 256))
            conv[pl.ds(first, rows), pair * 16 : pair * 16 + 16, :] = jnp.concatenate(groups, 1).astype(BF16)

    loads[4].wait()

    def y_block(number, carry):
        along_y(pl.multiple_of(number * BLOCK, 16), BLOCK)
        return carry

    lax.fori_loop(0, 5, y_block, 0, unroll=True)
    along_y(480, 32)

    label_wait(112, 1)
    row_index[...] = jnp.broadcast_to(inverse_row(labels[...]), (8, 128))
    pltpu.sync_copy(row_index, table_out)
    parts = recv.at[pl.ds(0, 127)]
    pltpu.make_async_copy(parts, parts, part_in).wait()
    pltpu.make_async_copy(parts, parts, part_out).wait()

    def unpack(number, carry):
        upper = recv[within(table_out[0, 2 * number])].astype(F32)
        lower = recv[within(table_out[0, 2 * number + 1])].astype(F32)
        rows = pl.ds(pl.multiple_of(number * 8, 8), 8)
        science[rows, 0:128] = jnp.concatenate([upper[0:4], lower[0:4]], 0)
        science[rows, 128:256] = jnp.concatenate([upper[4:8], lower[4:8]], 0)
        science_var[rows, 0:128] = jnp.concatenate([upper[8:12], lower[8:12]], 0)
        science_var[rows, 128:256] = jnp.concatenate([upper[12:16], lower[12:16]], 0)
        return carry

    lax.fori_loop(0, 64, unpack, 0, unroll=4)
    loads[5].wait()
    root[...] = coverage[...].astype(F32) * lax.rsqrt(science_var[...])

    is_target = lax.broadcasted_iota(jnp.int32, (16, 256), 0) == TARGET - 32

    def gram_patch(patch, carry):
        base = pl.multiple_of(patch * 256, 256)
        pieces = []
        for row in range(256):
            weight = root[pl.ds(base + row, 1), :]
            goal = weight * science[pl.ds(base + row, 1), :]
            basis = conv[base + row].astype(F32) * weight
            last = jnp.where(is_target, goal, basis[32:48])
            pieces.append(jnp.concatenate([basis[0:32].astype(BF16), last.astype(BF16)], 0))
        block = jnp.concatenate(pieces, 1)
        total = lax.dot_general(block, block, (((1,), (1,)), ((), ())), preferred_element_type=F32)
        own_gram[patch, :, 0:48] = total[0:24]
        own_gram[patch, :, 64:112] = total[24:48]
        return carry

    lax.fori_loop(0, 2, gram_patch, 0)
    grams_sent(lambda copy: copy.start())
    grams_received()

    lane = lax.broadcasted_iota(jnp.int32, (48, 128), 1)
    sub = lax.broadcasted_iota(jnp.int32, (48, 128), 0)
    beside = own_gram[0] + own_gram[1] + near_gram[6] + near_gram[7] + near_gram[8] + near_gram[9]
    upper = beside + near_gram[1] + near_gram[4] + near_gram[5]
    lower = beside + near_gram[0] + near_gram[2] + near_gram[3]
    first_half = lane[0:24] < 64
    system = jnp.concatenate(
        [
            jnp.where(first_half, upper, pltpu.roll(lower, 64, 1)),
            jnp.where(first_half, pltpu.roll(upper, 64, 1), lower),
        ],
        0,
    )
    half_lane = lane % 64
    diagonal = jnp.logical_and(sub == half_lane, sub < 45)
    on_diagonal = jnp.where(diagonal, system, 0.0)
    trace_upper = jnp.sum(jnp.where(lane < 64, on_diagonal, 0.0))
    trace_lower = jnp.sum(jnp.where(lane < 64, 0.0, on_diagonal))
    ridge = jnp.where(lane < 64, trace_upper, trace_lower) * (RIDGE / 45.0)
    system = jnp.where(diagonal, system + ridge, system)

    def column_of(matrix, step):
        return jnp.take_along_axis(matrix, (lane - half_lane) + step, axis=1)

    def pivot_pair(first, second, step):
        a, b = first[step : step + 1], second[step : step + 1]
        c, d = first[step + 1 : step + 2], second[step + 1 : step + 2]
        inverse = 1.0 / (a * d - b * c)
        return first * (d * inverse) - second * (c * inverse), second * (a * inverse) - first * (b * inverse)

    for step in range(0, 44, 4):
        columns = [column_of(system, step + number) for number in range(4)]
        row = [system[step + number : step + number + 1] for number in range(4)]
        u0, u1 = pivot_pair(columns[0], columns[1], step)
        third, fourth = (
            column - u0 * column[step : step + 1] - u1 * column[step + 1 : step + 2] for column in columns[2:]
        )
        u2, u3 = pivot_pair(third, fourth, step + 2)
        row[2] = row[2] - u0[step + 2 : step + 3] * row[0] - u1[step + 2 : step + 3] * row[1]
        row[3] = row[3] - u0[step + 3 : step + 4] * row[0] - u1[step + 3 : step + 4] * row[1]
        v0 = u0 - u2 * u0[step + 2 : step + 3] - u3 * u0[step + 3 : step + 4]
        v1 = u1 - u2 * u1[step + 2 : step + 3] - u3 * u1[step + 3 : step + 4]
        system = system - u0 * row[0] - u1 * row[1] - u2 * row[2] - u3 * row[3]
        for number, column in enumerate((v0, v1, u2, u3)):
            system = jnp.where(half_lane == step + number, column, system)
    column = column_of(system, 44)
    inverse = 1.0 / column[44:45]
    system = jnp.where(half_lane == 44, column * inverse, system - column * (inverse * system[44:45]))
    answer = jnp.where(jnp.logical_and(half_lane[47:48] < 45, lane[47:48] < 128), system[TARGET : TARGET + 1], 0.0)
    terms = power[...] * answer
    upper_terms = jnp.sum(jnp.where(lane < 64, terms, 0.0), 1, keepdims=True)
    lower_terms = jnp.sum(jnp.where(lane < 64, 0.0, terms), 1, keepdims=True)
    powers = (jnp.sum(upper_terms * upper_terms), jnp.sum(lower_terms * lower_terms))

    coarse = answer.astype(BF16)
    fine = (answer - coarse.astype(F32)).astype(BF16)
    row_of = lax.broadcasted_iota(jnp.int32, (32, 768), 0)
    lane_of = lax.broadcasted_iota(jnp.int32, (32, 768), 1)
    chosen = lane_of // 48 == row_of % 16
    both = jnp.concatenate(
        [jnp.broadcast_to(coarse.astype(F32), (16, 128)), jnp.broadcast_to(fine.astype(F32), (16, 128))], 0
    ).astype(BF16)
    loads[6].wait()
    loads[7].wait()
    for patch in range(2):
        coefficients = jnp.where(
            chosen, jnp.dot(both, spread[patch], preferred_element_type=F32), 0.0
        ).astype(BF16)
        kernel_power = powers[patch]

        def finish(number, carry):
            rows = pl.ds(pl.multiple_of(number * 16, 16), 16)
            product = jnp.dot(coefficients, conv[rows].reshape(768, 256), preferred_element_type=F32)
            model = product[0:16] + product[16:32]
            residual[rows] = science[rows] - model
            spread_var[rows] = science_var[rows] + kernel_power * template_var[rows]
            return carry

        lax.fori_loop(16 * patch, 16 * patch + 16, finish, 0, unroll=8)

    each_sent(halo, lambda copy: copy.wait_send())
    grams_sent(lambda copy: copy.wait_send())


def local(template, template_var, coverage, exposure, exposure_var, strip_owner, strip_slot):
    def blocks(array):
        return array.reshape(128, 4, 2, 128).transpose(0, 2, 1, 3).reshape(128, 8, 128)

    vmem = pl.BlockSpec(memory_space=pltpu.VMEM)
    hbm = pl.BlockSpec(memory_space=pltpu.HBM)
    dma = pltpu.SemaphoreType.DMA
    x_weights, y_weights, power, spread = [jnp.asarray(table) for table in tables()]
    residual, spread_var = pl.pallas_call(
        kernel,
        out_shape=[pltpu.VMEM((512, 256), F32)] * 2,
        in_specs=[hbm] * 8 + [vmem] * 3,
        out_specs=[vmem] * 2,
        scratch_shapes=[
            pltpu.VMEM((512, 256), F32),
            pltpu.VMEM((512, 256), F32),
            pltpu.VMEM((512, 256), jnp.int32),
            pltpu.VMEM((128, 8, 128), F32),
            pltpu.VMEM((128, 8, 128), F32),
            pltpu.VMEM((8, 256, 256), BF16),
            pltpu.VMEM((8, BLOCK * 8, 256), BF16),
            pltpu.VMEM((2, 128, 768), BF16),
            pltpu.VMEM((544, 512), BF16),
            pltpu.VMEM((16, 608, 256), BF16),
            pltpu.VMEM((512, 48, 256), BF16),
            pltpu.VMEM((128, 16, 128), BF16),
            pltpu.VMEM((128, 16, 128), BF16),
            pltpu.VMEM((128, 128), jnp.int32),
            pltpu.VMEM((512, 256), F32),
            pltpu.VMEM((512, 256), F32),
            pltpu.VMEM((512, 256), F32),
            pltpu.VMEM((2, 24, 128), F32),
            pltpu.VMEM((10, 24, 128), F32),
            pltpu.VMEM((8, 128), jnp.int32),
            pltpu.SMEM((8, 128), jnp.int32),
            pltpu.SMEM((8, 128), jnp.int32),
            dma((8,)), dma((8,)), dma, dma, dma((2,)), dma((2,)), dma((10,)), dma((10,)), dma((8,)), pltpu.SemaphoreType.REGULAR,
        ],
        compiler_params=pltpu.CompilerParams(
            collective_id=0, has_side_effects=True, vmem_limit_bytes=60 * 1024 * 1024
        ),
        cost_estimate=pl.CostEstimate(flops=10**10, bytes_accessed=8 * 10**6, transcendentals=0),
    )(
        template, template_var, coverage, blocks(exposure), blocks(exposure_var), x_weights, y_weights, spread,
        strip_owner, strip_slot, power,
    )
    mask = coverage.astype(F32)
    return (mask * residual, mask * spread_var)


def solution(mesh):
    image = P("row", "col")
    strips = P("row", "col", None, None)
    return jax.shard_map(
        local,
        mesh=mesh,
        in_specs=(image, image, image, strips, strips, image, image),
        out_specs=(image, image),
        check_vma=False,
    )
```

```python
import jax
import jax.numpy as jnp
import numpy as np
from jax import lax
from jax.experimental import pallas as pl
from jax.experimental.pallas import tpu as pltpu
from jax.sharding import PartitionSpec as P

RIDGE = 0.05
SIGMAS = (1.0, 2.0, 4.0)
MESH = pl.DeviceIdType.MESH
F32 = jnp.float32
BF16 = jnp.bfloat16

SLOTS = (
    (0, 0), (0, 2), (1, 0), (1, 2), (2, 0), (2, 2), (0, 1), (1, 1),
    (2, 1), (0, 3), (1, 3), None, (2, 3), (0, 4), (1, 4), (2, 4),
)
GROUP_OF_PASS = (0, 1, 2, 3, 4, 4, 5, 5)
BLOCK = 96
TARGET = 47
GRAM_COPIES = ((0, -1, 0), (1, 1, 0), (0, -1, -1), (0, -1, 1), (1, 1, -1), (1, 1, 1), (0, 0, -1), (0, 0, 1), (1, 0, -1), (1, 0, 1))
DIRECTIONS = ((0, -1), (0, 1), (-1, 0), (1, 0), (-1, -1), (-1, 1), (1, -1), (1, 1))


def filter_bank():
    taps = np.arange(31) - 15.0
    collected = []
    for sigma in SIGMAS:
        for degree in range(5):
            scaled = taps / sigma
            shape = scaled**degree * np.exp(-0.5 * scaled * scaled)
            collected.append(shape / np.sqrt(np.sum(shape * shape)))
    return np.array(collected, np.float32).astype(jnp.bfloat16).astype(np.float32)


def tables():
    bank = filter_bank()
    x_weights = np.zeros((8, 256, 2, 128), np.float32)
    y_weights = np.zeros((8, BLOCK, 8, 2, 128), np.float32)
    across = np.arange(128)
    down = np.arange(BLOCK)
    order = []
    filled = [0] * 6
    for number, slot in enumerate(SLOTS):
        if slot is None:
            continue
        half, which = number // 2, number % 2
        s, i = slot
        group = GROUP_OF_PASS[half]
        for q in range(31):
            x_weights[half, across + q - 15 + 64, which, across] = bank[s * 5 + i, q]
        for j in range(5 - i):
            lane = filled[group]
            filled[group] += 1
            order.append((group * 8 + lane, s, i, j))
            for p in range(31):
                y_weights[half, down, lane, which, down + p - 15 + 16] = bank[s * 5 + j, p]
    shapes = np.zeros((48, 31 * 31), np.float64)
    for t, s, i, j in order:
        shapes[t] = np.outer(bank[s * 5 + j], bank[s * 5 + i]).reshape(-1).astype(np.float64)
    values, vectors = np.linalg.eigh(shapes @ shapes.T)
    root = np.sqrt(np.maximum(values, 0.0))[:, None] * vectors.T
    power = np.zeros((48, 128), np.float32)
    power[:, :48] = root
    power[:, 64:112] = root
    spread = np.zeros((2, 128, 768), np.float32)
    for patch in range(2):
        spread[patch, 64 * patch + np.arange(768) % 48, np.arange(768)] = 1.0
    return (
        x_weights.reshape(8, 256, 256).astype(jnp.bfloat16),
        y_weights.reshape(8, BLOCK * 8, 256).astype(jnp.bfloat16),
        power,
        spread.astype(jnp.bfloat16),
    )


def inverse_row(columns, size=128):
    rows = lax.broadcasted_iota(jnp.int32, (size, size), 0)
    lanes = lax.broadcasted_iota(jnp.int32, (size, size), 1)
    return jnp.max(jnp.where(columns == lanes, rows, 0), 0, keepdims=True)


def within(number):
    return jnp.clip(number, 0, 127)


def kernel(
    template_hbm, template_var_hbm, coverage_hbm, flux_hbm, noise_hbm, x_weights_hbm, y_weights_hbm, spread_hbm,
    owner, slot, power,
    residual, spread_var,
    template, template_var, coverage, flux, noise, x_weights, y_weights, spread,
    wide, filtered, conv, send, recv, labels, science, science_var, root, own_gram, near_gram,
    row_index, table_in, table_out,
    halo_out, halo_in, part_out, part_in, label_out, label_in, gram_out, gram_in, load_in, ready,
):
    r = lax.axis_index("row")
    c = lax.axis_index("col")
    x, z, k = c // 8, (c // 2) % 4, c % 2
    me = r * 32 + c
    place = (z * 2 + k) * 16 + r * 4 + x
    barrier = pltpu.get_barrier_semaphore()

    loads = [
        pltpu.make_async_copy(source, held, load_in.at[number])
        for number, (source, held) in enumerate((
            (template_hbm, template), (flux_hbm, flux), (noise_hbm, noise), (x_weights_hbm, x_weights),
            (y_weights_hbm, y_weights), (coverage_hbm, coverage), (template_var_hbm, template_var), (spread_hbm, spread),
        ))
    ]
    loads[0].start()

    wide[...] = jnp.zeros_like(wide)
    near_gram[...] = jnp.zeros_like(near_gram)
    own_gram[...] = jnp.zeros_like(own_gram)

    def column(dx, dz, dk):
        return (x + dx) % 4 * 8 + (z + dz) % 4 * 2 + (k + dk) % 2

    across = [((r + dr) % 4, column(dx, 0, 0)) for dr in range(4) for dx in range(4) if dr or dx]
    along = [(r, column(0, dz, dk)) for dz in range(4) for dk in range(2) if dz or dk]
    around = [((r + dr) % 4, (c + dc) % 32) for dr, dc in DIRECTIONS]
    for other in around + across + along:
        pl.semaphore_signal(barrier, inc=1, device_id=other, device_id_type=MESH)
    for load in loads[1:]:
        load.start()

    labels[pl.ds(place, 1), :] = slot[...]
    loads[0].wait()
    wide[16:528, 128:384] = template[...].astype(BF16)
    pl.semaphore_wait(barrier, 30)
    for other in along:
        pl.semaphore_signal(ready, inc=1, device_id=other, device_id_type=MESH)

    def inside(dr, dc):
        return jnp.logical_and(
            jnp.logical_and(r + dr >= 0, r + dr < 4), jnp.logical_and(c + dc >= 0, c + dc < 32)
        )

    def target(dr, dc):
        return (jnp.clip(r + dr, 0, 3), jnp.clip(c + dc, 0, 31))

    source_rows = {-1: pl.ds(16, 16), 0: pl.ds(16, 512), 1: pl.ds(512, 16)}
    target_rows = {-1: pl.ds(528, 16), 0: pl.ds(16, 512), 1: pl.ds(0, 16)}
    source_cols = {-1: pl.ds(128, 128), 0: pl.ds(128, 256), 1: pl.ds(256, 128)}
    target_cols = {-1: pl.ds(384, 128), 0: pl.ds(128, 256), 1: pl.ds(0, 128)}

    def halo(number):
        dr, dc = DIRECTIONS[number]
        return pltpu.make_async_remote_copy(
            src_ref=wide.at[source_rows[dr], source_cols[dc]],
            dst_ref=wide.at[target_rows[dr], target_cols[dc]],
            send_sem=halo_out.at[number],
            recv_sem=halo_in.at[number],
            device_id=target(dr, dc),
            device_id_type=MESH,
        )

    def gram_copy(number):
        patch, dr, dc = GRAM_COPIES[number]
        return pltpu.make_async_remote_copy(
            src_ref=own_gram.at[patch],
            dst_ref=near_gram.at[number],
            send_sem=gram_out.at[number],
            recv_sem=gram_in.at[number],
            device_id=target(dr, dc),
            device_id_type=MESH,
        )

    def grams_sent(action):
        for number, (_, dr, dc) in enumerate(GRAM_COPIES):
            @pl.when(inside(dr, dc))
            def _():
                action(gram_copy(number))

    def grams_received():
        for number, (_, dr, dc) in enumerate(GRAM_COPIES):
            @pl.when(inside(-dr, -dc))
            def _():
                gram_copy(number).wait_recv()

    def each_sent(make, action):
        for number, (dr, dc) in enumerate(DIRECTIONS):
            @pl.when(inside(dr, dc))
            def _():
                action(make(number))

    def each_received(make):
        for number, (dr, dc) in enumerate(DIRECTIONS):
            @pl.when(inside(-dr, -dc))
            def _():
                make(number).wait_recv()

    each_sent(halo, lambda copy: copy.start())

    def label_copy(first, count, row, col, which):
        return pltpu.make_async_remote_copy(
            src_ref=labels.at[pl.ds(first, count)],
            dst_ref=labels.at[pl.ds(first, count)],
            send_sem=label_out.at[which],
            recv_sem=label_in.at[which],
            device_id=(row, col),
            device_id_type=MESH,
        )

    for other in across:
        label_copy(place, 1, *other, 0).start()

    owners = jnp.transpose(jnp.broadcast_to(owner[...], (128, 128)))
    row_index[...] = jnp.broadcast_to(inverse_row(owners), (8, 128))
    pltpu.sync_copy(row_index, table_in)
    loads[1].wait()
    loads[2].wait()

    def chunk(number):
        block = within(table_in[0, number])
        return jnp.concatenate([flux[block], noise[block]], 0).astype(BF16)

    def send_part(step, carry):
        other = lax.rem(me + step, 128)
        send[other] = chunk(other)
        pltpu.make_async_remote_copy(
            src_ref=send.at[other],
            dst_ref=recv.at[place],
            send_sem=part_out,
            recv_sem=part_in,
            device_id=(other // 32, other % 32),
            device_id_type=MESH,
        ).start()
        return carry

    recv[place] = chunk(me)
    pl.semaphore_wait(ready, 7)
    lax.fori_loop(1, 127, send_part, 0, unroll=6)
    send_part(127, 0)

    each_received(halo)

    filtered[:, 544:608, :] = jnp.zeros((16, 64, 256), BF16)
    loads[3].wait()
    whole = wide[...]
    windows = (whole[:, 64:320], whole[:, 192:448])

    def along_x(half, carry):
        for side in range(2):
            product = jnp.dot(windows[side], x_weights[half], preferred_element_type=F32).astype(BF16)
            for which in range(2):
                filtered[2 * half + which, 0:544, side * 128 : side * 128 + 128] = product[
                    :, which * 128 : which * 128 + 128
                ]
        return carry

    lax.fori_loop(0, 8, along_x, 0, unroll=True)

    def label_wait(count, which):
        part = labels.at[pl.ds(0, count)]
        pltpu.make_async_copy(part, part, label_in.at[which]).wait()
        pltpu.make_async_copy(part, part, label_out.at[which]).wait()

    label_wait(15, 0)
    for other in along:
        label_copy(pl.multiple_of((z * 2 + k) * 16, 16), 16, *other, 1).start()

    def along_y(first, rows):
        for pair in range(3):
            groups = []
            for group in (2 * pair, 2 * pair + 1):
                total = None
                for half in range(8):
                    if GROUP_OF_PASS[half] == group:
                        window = filtered[2 * half : 2 * half + 2, pl.ds(first, 128), :].reshape(256, 256)
                        product = jnp.dot(
                            y_weights[half, 0 : rows * 8, :], window, preferred_element_type=F32
                        )
                        total = product if total is None else total + product
                groups.append(total.reshape(rows, 8, 256))
            conv[pl.ds(first, rows), pair * 16 : pair * 16 + 16, :] = jnp.concatenate(groups, 1).astype(BF16)

    loads[4].wait()

    def y_block(number, carry):
        along_y(pl.multiple_of(number * BLOCK, 16), BLOCK)
        return carry

    lax.fori_loop(0, 4, y_block, 0, unroll=True)
    label_wait(112, 1)
    row_index[...] = jnp.broadcast_to(inverse_row(labels[...]), (8, 128))
    table_copy = pltpu.make_async_copy(row_index, table_out, load_in.at[0])
    table_copy.start()
    y_block(4, 0)
    along_y(480, 32)

    table_copy.wait()
    parts = recv.at[pl.ds(0, 127)]
    pltpu.make_async_copy(parts, parts, part_in).wait()
    pltpu.make_async_copy(parts, parts, part_out).wait()

    def unpack(number, carry):
        upper = recv[within(table_out[0, 2 * number])].astype(F32)
        lower = recv[within(table_out[0, 2 * number + 1])].astype(F32)
        rows = pl.ds(pl.multiple_of(number * 8, 8), 8)
        science[rows, 0:128] = jnp.concatenate([upper[0:4], lower[0:4]], 0)
        science[rows, 128:256] = jnp.concatenate([upper[4:8], lower[4:8]], 0)
        science_var[rows, 0:128] = jnp.concatenate([upper[8:12], lower[8:12]], 0)
        science_var[rows, 128:256] = jnp.concatenate([upper[12:16], lower[12:16]], 0)
        return carry

    lax.fori_loop(0, 64, unpack, 0, unroll=4)
    loads[5].wait()
    root[...] = coverage[...].astype(F32) * lax.rsqrt(science_var[...])

    is_target = lax.broadcasted_iota(jnp.int32, (16, 256), 0) == TARGET - 32

    def gram_patch(patch, carry):
        base = pl.multiple_of(patch * 256, 256)
        pieces = []
        for row in range(256):
            weight = root[pl.ds(base + row, 1), :]
            goal = weight * science[pl.ds(base + row, 1), :]
            basis = conv[base + row].astype(F32) * weight
            last = jnp.where(is_target, goal, basis[32:48])
            pieces.append(jnp.concatenate([basis[0:32].astype(BF16), last.astype(BF16)], 0))
        block = jnp.concatenate(pieces, 1)
        total = lax.dot_general(block, block, (((1,), (1,)), ((), ())), preferred_element_type=F32)
        own_gram[patch, :, 0:48] = total[0:24]
        own_gram[patch, :, 64:112] = total[24:48]
        return carry

    lax.fori_loop(0, 2, gram_patch, 0)
    grams_sent(lambda copy: copy.start())
    grams_received()

    lane = lax.broadcasted_iota(jnp.int32, (48, 128), 1)
    sub = lax.broadcasted_iota(jnp.int32, (48, 128), 0)
    beside = own_gram[0] + own_gram[1] + near_gram[6] + near_gram[7] + near_gram[8] + near_gram[9]
    upper = beside + near_gram[1] + near_gram[4] + near_gram[5]
    lower = beside + near_gram[0] + near_gram[2] + near_gram[3]
    first_half = lane[0:24] < 64
    system = jnp.concatenate(
        [
            jnp.where(first_half, upper, pltpu.roll(lower, 64, 1)),
            jnp.where(first_half, pltpu.roll(upper, 64, 1), lower),
        ],
        0,
    )
    half_lane = lane % 64
    diagonal = jnp.logical_and(sub == half_lane, sub < 45)
    on_diagonal = jnp.where(diagonal, system, 0.0)
    trace_upper = jnp.sum(jnp.where(lane < 64, on_diagonal, 0.0))
    trace_lower = jnp.sum(jnp.where(lane < 64, 0.0, on_diagonal))
    ridge = jnp.where(lane < 64, trace_upper, trace_lower) * (RIDGE / 45.0)
    system = jnp.where(diagonal, system + ridge, system)

    def column_of(matrix, step):
        return jnp.take_along_axis(matrix, (lane - half_lane) + step, axis=1)

    def pivot_pair(first, second, step):
        a, b = first[step : step + 1], second[step : step + 1]
        c, d = first[step + 1 : step + 2], second[step + 1 : step + 2]
        inverse = 1.0 / (a * d - b * c)
        return first * (d * inverse) - second * (c * inverse), second * (a * inverse) - first * (b * inverse)

    for step in range(0, 44, 4):
        columns = [column_of(system, step + number) for number in range(4)]
        row = [system[step + number : step + number + 1] for number in range(4)]
        u0, u1 = pivot_pair(columns[0], columns[1], step)
        third, fourth = (
            column - u0 * column[step : step + 1] - u1 * column[step + 1 : step + 2] for column in columns[2:]
        )
        u2, u3 = pivot_pair(third, fourth, step + 2)
        row[2] = row[2] - u0[step + 2 : step + 3] * row[0] - u1[step + 2 : step + 3] * row[1]
        row[3] = row[3] - u0[step + 3 : step + 4] * row[0] - u1[step + 3 : step + 4] * row[1]
        v0 = u0 - u2 * u0[step + 2 : step + 3] - u3 * u0[step + 3 : step + 4]
        v1 = u1 - u2 * u1[step + 2 : step + 3] - u3 * u1[step + 3 : step + 4]
        system = system - u0 * row[0] - u1 * row[1] - u2 * row[2] - u3 * row[3]
        for number, column in enumerate((v0, v1, u2, u3)):
            system = jnp.where(half_lane == step + number, column, system)
    column = column_of(system, 44)
    inverse = 1.0 / column[44:45]
    system = jnp.where(half_lane == 44, column * inverse, system - column * (inverse * system[44:45]))
    answer = jnp.where(jnp.logical_and(half_lane[47:48] < 45, lane[47:48] < 128), system[TARGET : TARGET + 1], 0.0)
    terms = power[...] * answer
    upper_terms = jnp.sum(jnp.where(lane < 64, terms, 0.0), 1, keepdims=True)
    lower_terms = jnp.sum(jnp.where(lane < 64, 0.0, terms), 1, keepdims=True)
    powers = (jnp.sum(upper_terms * upper_terms), jnp.sum(lower_terms * lower_terms))

    coarse = answer.astype(BF16)
    fine = (answer - coarse.astype(F32)).astype(BF16)
    row_of = lax.broadcasted_iota(jnp.int32, (32, 768), 0)
    lane_of = lax.broadcasted_iota(jnp.int32, (32, 768), 1)
    chosen = lane_of // 48 == row_of % 16
    both = jnp.concatenate(
        [jnp.broadcast_to(coarse.astype(F32), (16, 128)), jnp.broadcast_to(fine.astype(F32), (16, 128))], 0
    ).astype(BF16)
    loads[6].wait()
    loads[7].wait()
    for patch in range(2):
        coefficients = jnp.where(
            chosen, jnp.dot(both, spread[patch], preferred_element_type=F32), 0.0
        ).astype(BF16)
        kernel_power = powers[patch]

        def finish(number, carry):
            rows = pl.ds(pl.multiple_of(number * 16, 16), 16)
            product = jnp.dot(coefficients, conv[rows].reshape(768, 256), preferred_element_type=F32)
            model = product[0:16] + product[16:32]
            residual[rows] = science[rows] - model
            spread_var[rows] = science_var[rows] + kernel_power * template_var[rows]
            return carry

        lax.fori_loop(16 * patch, 16 * patch + 16, finish, 0, unroll=8)

    each_sent(halo, lambda copy: copy.wait_send())
    grams_sent(lambda copy: copy.wait_send())


def local(template, template_var, coverage, exposure, exposure_var, strip_owner, strip_slot):
    def blocks(array):
        return array.reshape(128, 4, 2, 128).transpose(0, 2, 1, 3).reshape(128, 8, 128)

    vmem = pl.BlockSpec(memory_space=pltpu.VMEM)
    hbm = pl.BlockSpec(memory_space=pltpu.HBM)
    dma = pltpu.SemaphoreType.DMA
    x_weights, y_weights, power, spread = [jnp.asarray(table) for table in tables()]
    residual, spread_var = pl.pallas_call(
        kernel,
        out_shape=[pltpu.VMEM((512, 256), F32)] * 2,
        in_specs=[hbm] * 8 + [vmem] * 3,
        out_specs=[vmem] * 2,
        scratch_shapes=[
            pltpu.VMEM((512, 256), F32),
            pltpu.VMEM((512, 256), F32),
            pltpu.VMEM((512, 256), jnp.int32),
            pltpu.VMEM((128, 8, 128), F32),
            pltpu.VMEM((128, 8, 128), F32),
            pltpu.VMEM((8, 256, 256), BF16),
            pltpu.VMEM((8, BLOCK * 8, 256), BF16),
            pltpu.VMEM((2, 128, 768), BF16),
            pltpu.VMEM((544, 512), BF16),
            pltpu.VMEM((16, 608, 256), BF16),
            pltpu.VMEM((512, 48, 256), BF16),
            pltpu.VMEM((128, 16, 128), BF16),
            pltpu.VMEM((128, 16, 128), BF16),
            pltpu.VMEM((128, 128), jnp.int32),
            pltpu.VMEM((512, 256), F32),
            pltpu.VMEM((512, 256), F32),
            pltpu.VMEM((512, 256), F32),
            pltpu.VMEM((2, 24, 128), F32),
            pltpu.VMEM((10, 24, 128), F32),
            pltpu.VMEM((8, 128), jnp.int32),
            pltpu.SMEM((8, 128), jnp.int32),
            pltpu.SMEM((8, 128), jnp.int32),
            dma((8,)), dma((8,)), dma, dma, dma((2,)), dma((2,)), dma((10,)), dma((10,)), dma((8,)), pltpu.SemaphoreType.REGULAR,
        ],
        compiler_params=pltpu.CompilerParams(
            collective_id=0, has_side_effects=True, vmem_limit_bytes=60 * 1024 * 1024
        ),
        cost_estimate=pl.CostEstimate(flops=10**10, bytes_accessed=8 * 10**6, transcendentals=0),
    )(
        template, template_var, coverage, blocks(exposure), blocks(exposure_var), x_weights, y_weights, spread,
        strip_owner, strip_slot, power,
    )
    mask = coverage.astype(F32)
    return (mask * residual, mask * spread_var)


def solution(mesh):
    image = P("row", "col")
    strips = P("row", "col", None, None)
    return jax.shard_map(
        local,
        mesh=mesh,
        in_specs=(image, image, image, strips, strips, image, image),
        out_specs=(image, image),
        check_vma=False,
    )
```

```python
import jax
import jax.numpy as jnp
import numpy as np
from jax import lax
from jax.experimental import pallas as pl
from jax.experimental.pallas import tpu as pltpu
from jax.sharding import PartitionSpec as P

RIDGE = 0.05
SIGMAS = (1.0, 2.0, 4.0)
MESH = pl.DeviceIdType.MESH
F32 = jnp.float32
BF16 = jnp.bfloat16

SLOTS = (
    (0, 0), (0, 2), (1, 0), (1, 2), (2, 0), (2, 2), (0, 1), (1, 1),
    (2, 1), (0, 3), (1, 3), None, (2, 3), (0, 4), (1, 4), (2, 4),
)
GROUP_OF_PASS = (0, 1, 2, 3, 4, 4, 5, 5)
BLOCK = 96
TARGET = 47
GRAM_COPIES = ((0, -1, 0), (1, 1, 0), (0, -1, -1), (0, -1, 1), (1, 1, -1), (1, 1, 1), (0, 0, -1), (0, 0, 1), (1, 0, -1), (1, 0, 1))
DIRECTIONS = ((0, -1), (0, 1), (-1, 0), (1, 0), (-1, -1), (-1, 1), (1, -1), (1, 1))


def filter_bank():
    taps = np.arange(31) - 15.0
    collected = []
    for sigma in SIGMAS:
        for degree in range(5):
            scaled = taps / sigma
            shape = scaled**degree * np.exp(-0.5 * scaled * scaled)
            collected.append(shape / np.sqrt(np.sum(shape * shape)))
    return np.array(collected, np.float32).astype(jnp.bfloat16).astype(np.float32)


def tables():
    bank = filter_bank()
    x_weights = np.zeros((8, 256, 2, 128), np.float32)
    y_weights = np.zeros((8, BLOCK, 8, 2, 128), np.float32)
    across = np.arange(128)
    down = np.arange(BLOCK)
    order = []
    filled = [0] * 6
    for number, slot in enumerate(SLOTS):
        if slot is None:
            continue
        half, which = number // 2, number % 2
        s, i = slot
        group = GROUP_OF_PASS[half]
        for q in range(31):
            x_weights[half, across + q - 15 + 64, which, across] = bank[s * 5 + i, q]
        for j in range(5 - i):
            lane = filled[group]
            filled[group] += 1
            order.append((group * 8 + lane, s, i, j))
            for p in range(31):
                y_weights[half, down, lane, which, down + p - 15 + 16] = bank[s * 5 + j, p]
    shapes = np.zeros((48, 31 * 31), np.float64)
    for t, s, i, j in order:
        shapes[t] = np.outer(bank[s * 5 + j], bank[s * 5 + i]).reshape(-1).astype(np.float64)
    values, vectors = np.linalg.eigh(shapes @ shapes.T)
    root = np.sqrt(np.maximum(values, 0.0))[:, None] * vectors.T
    power = np.zeros((48, 128), np.float32)
    power[:, :48] = root
    power[:, 64:112] = root
    spread = np.zeros((2, 128, 768), np.float32)
    for patch in range(2):
        spread[patch, 64 * patch + np.arange(768) % 48, np.arange(768)] = 1.0
    return (
        x_weights.reshape(8, 256, 256).astype(jnp.bfloat16),
        y_weights.reshape(8, BLOCK * 8, 256).astype(jnp.bfloat16),
        power,
        spread.astype(jnp.bfloat16),
    )


def inverse_row(columns, size=128):
    rows = lax.broadcasted_iota(jnp.int32, (size, size), 0)
    lanes = lax.broadcasted_iota(jnp.int32, (size, size), 1)
    return jnp.max(jnp.where(columns == lanes, rows, 0), 0, keepdims=True)


def within(number):
    return jnp.clip(number, 0, 127)


def kernel(
    template_hbm, template_var_hbm, coverage_hbm, flux_hbm, noise_hbm, x_weights_hbm, y_weights_hbm, spread_hbm,
    owner, slot, power,
    residual, spread_var,
    template, template_var, coverage, flux, noise, x_weights, y_weights, spread,
    side_out, side_in, wide, filtered, conv, send, recv, labels, science, science_var, root, own_gram, near_gram,
    row_index, table_in, table_out,
    halo_out, halo_in, part_out, part_in, label_out, label_in, gram_out, gram_in, load_in, ready,
):
    r = lax.axis_index("row")
    c = lax.axis_index("col")
    x, z, k = c // 8, (c // 2) % 4, c % 2
    me = r * 32 + c
    place = (z * 2 + k) * 16 + r * 4 + x
    barrier = pltpu.get_barrier_semaphore()

    loads = [
        pltpu.make_async_copy(source, held, load_in.at[number])
        for number, (source, held) in enumerate((
            (template_hbm, template), (flux_hbm, flux), (noise_hbm, noise), (x_weights_hbm, x_weights),
            (y_weights_hbm, y_weights), (coverage_hbm, coverage), (template_var_hbm, template_var), (spread_hbm, spread),
        ))
    ]
    loads[0].start()

    wide[...] = jnp.zeros_like(wide)
    near_gram[...] = jnp.zeros_like(near_gram)
    side_in[...] = jnp.zeros_like(side_in)
    own_gram[...] = jnp.zeros_like(own_gram)

    def column(dx, dz, dk):
        return (x + dx) % 4 * 8 + (z + dz) % 4 * 2 + (k + dk) % 2

    across = [((r + dr) % 4, column(dx, 0, 0)) for dr in range(4) for dx in range(4) if dr or dx]
    along = [(r, column(0, dz, dk)) for dz in range(4) for dk in range(2) if dz or dk]
    around = [((r + dr) % 4, (c + dc) % 32) for dr, dc in DIRECTIONS]
    for other in around + across + along:
        pl.semaphore_signal(barrier, inc=1, device_id=other, device_id_type=MESH)
    for load in loads[1:]:
        load.start()

    owners = jnp.transpose(jnp.broadcast_to(owner[...], (128, 128)))
    row_index[...] = jnp.broadcast_to(inverse_row(owners), (8, 128))
    owner_copy = pltpu.make_async_copy(row_index, table_in, load_in.at[8])
    owner_copy.start()
    labels[pl.ds(place, 1), :] = slot[...]
    loads[0].wait()
    wide[16:528, 128:384] = template[...].astype(BF16)
    side_row = lax.broadcasted_iota(jnp.int32, (16, 128), 0)
    side_lane = lax.broadcasted_iota(jnp.int32, (16, 128), 1)
    sides = [
        jnp.where(side_lane == side_row + first, 1.0, 0.0).astype(BF16) for first in (0, 112)
    ]
    for number in range(2):
        side_out[number] = lax.dot_general(
            sides[number],
            wide[16:528, 128 + 128 * number : 256 + 128 * number],
            (((1,), (1,)), ((), ())),
            preferred_element_type=F32,
        ).astype(BF16)
    pl.semaphore_wait(barrier, 30)
    for other in along:
        pl.semaphore_signal(ready, inc=1, device_id=other, device_id_type=MESH)

    def inside(dr, dc):
        return jnp.logical_and(
            jnp.logical_and(r + dr >= 0, r + dr < 4), jnp.logical_and(c + dc >= 0, c + dc < 32)
        )

    def target(dr, dc):
        return (jnp.clip(r + dr, 0, 3), jnp.clip(c + dc, 0, 31))

    source_rows = {-1: pl.ds(16, 16), 0: pl.ds(16, 512), 1: pl.ds(512, 16)}
    target_rows = {-1: pl.ds(528, 16), 0: pl.ds(16, 512), 1: pl.ds(0, 16)}
    source_cols = {-1: pl.ds(128, 128), 0: pl.ds(128, 256), 1: pl.ds(256, 128)}
    target_cols = {-1: pl.ds(384, 128), 0: pl.ds(128, 256), 1: pl.ds(0, 128)}

    def halo(number):
        dr, dc = DIRECTIONS[number]
        return pltpu.make_async_remote_copy(
            src_ref=wide.at[source_rows[dr], source_cols[dc]] if dr else side_out.at[number],
            dst_ref=wide.at[target_rows[dr], target_cols[dc]] if dr else side_in.at[number],
            send_sem=halo_out.at[number],
            recv_sem=halo_in.at[number],
            device_id=target(dr, dc),
            device_id_type=MESH,
        )

    def gram_copy(number):
        patch, dr, dc = GRAM_COPIES[number]
        return pltpu.make_async_remote_copy(
            src_ref=own_gram.at[patch],
            dst_ref=near_gram.at[number],
            send_sem=gram_out.at[number],
            recv_sem=gram_in.at[number],
            device_id=target(dr, dc),
            device_id_type=MESH,
        )

    def grams_sent(action):
        for number, (_, dr, dc) in enumerate(GRAM_COPIES):
            @pl.when(inside(dr, dc))
            def _():
                action(gram_copy(number))

    def grams_received():
        for number, (_, dr, dc) in enumerate(GRAM_COPIES):
            @pl.when(inside(-dr, -dc))
            def _():
                gram_copy(number).wait_recv()

    def each_sent(make, action):
        for number, (dr, dc) in enumerate(DIRECTIONS):
            @pl.when(inside(dr, dc))
            def _():
                action(make(number))

    def each_received(make):
        for number, (dr, dc) in enumerate(DIRECTIONS):
            @pl.when(inside(-dr, -dc))
            def _():
                make(number).wait_recv()

    each_sent(halo, lambda copy: copy.start())

    def label_copy(first, count, row, col, which):
        return pltpu.make_async_remote_copy(
            src_ref=labels.at[pl.ds(first, count)],
            dst_ref=labels.at[pl.ds(first, count)],
            send_sem=label_out.at[which],
            recv_sem=label_in.at[which],
            device_id=(row, col),
            device_id_type=MESH,
        )

    for other in across:
        label_copy(place, 1, *other, 0).start()

    owner_copy.wait()
    loads[1].wait()
    loads[2].wait()

    def chunk(number):
        block = within(table_in[0, number])
        return jnp.concatenate([flux[block], noise[block]], 0).astype(BF16)

    def label_wait(count, which):
        part = labels.at[pl.ds(0, count)]
        pltpu.make_async_copy(part, part, label_in.at[which]).wait()
        pltpu.make_async_copy(part, part, label_out.at[which]).wait()

    def send_to(others):
        for row, col in others:
            send[row * 32 + col] = chunk(row * 32 + col)
        for row, col in others:
            pltpu.make_async_remote_copy(
                src_ref=send.at[row * 32 + col],
                dst_ref=recv.at[place],
                send_sem=part_out,
                recv_sem=part_in,
                device_id=(row, col),
                device_id_type=MESH,
            ).start()

    def send_group(group, carry):
        send_to([
            ((r + group // 4) % 4, column(group % 4, dz, dk)) for dz in range(4) for dk in range(2) if dz or dk
        ])
        return carry

    recv[place] = chunk(me)
    send_to(across)
    send_to(along)
    pl.semaphore_wait(ready, 7)
    lax.fori_loop(1, 8, send_group, 0)
    label_wait(15, 0)
    for other in along:
        label_copy(pl.multiple_of((z * 2 + k) * 16, 16), 16, *other, 1).start()
    lax.fori_loop(8, 16, send_group, 0)

    each_received(halo)

    for number in range(2):
        wide[16:528, 384 - 384 * number : 512 - 384 * number] = lax.dot_general(
            side_in[number], sides[number], (((0,), (0,)), ((), ())), preferred_element_type=F32
        ).astype(BF16)

    filtered[:, 544:608, :] = jnp.zeros((16, 64, 256), BF16)
    loads[3].wait()
    whole = wide[...]
    windows = (whole[:, 64:320], whole[:, 192:448])

    def along_x(half, carry):
        for side in range(2):
            product = jnp.dot(windows[side], x_weights[half], preferred_element_type=F32).astype(BF16)
            for which in range(2):
                filtered[2 * half + which, 0:544, side * 128 : side * 128 + 128] = product[
                    :, which * 128 : which * 128 + 128
                ]
        return carry

    lax.fori_loop(0, 8, along_x, 0, unroll=True)

    def along_y(first, rows):
        for pair in range(3):
            groups = []
            for group in (2 * pair, 2 * pair + 1):
                total = None
                for half in range(8):
                    if GROUP_OF_PASS[half] == group:
                        window = filtered[2 * half : 2 * half + 2, pl.ds(first, 128), :].reshape(256, 256)
                        product = jnp.dot(
                            y_weights[half, 0 : rows * 8, :], window, preferred_element_type=F32
                        )
                        total = product if total is None else total + product
                groups.append(total.reshape(rows, 8, 256))
            conv[pl.ds(first, rows), pair * 16 : pair * 16 + 16, :] = jnp.concatenate(groups, 1).astype(BF16)

    loads[4].wait()

    def y_block(number, carry):
        along_y(pl.multiple_of(number * BLOCK, 16), BLOCK)
        return carry

    lax.fori_loop(0, 4, y_block, 0, unroll=True)
    label_wait(112, 1)
    row_index[...] = jnp.broadcast_to(inverse_row(labels[...]), (8, 128))
    table_copy = pltpu.make_async_copy(row_index, table_out, load_in.at[0])
    table_copy.start()
    y_block(4, 0)
    along_y(480, 32)

    table_copy.wait()
    parts = recv.at[pl.ds(0, 127)]
    pltpu.make_async_copy(parts, parts, part_in).wait()
    pltpu.make_async_copy(parts, parts, part_out).wait()

    def unpack(number, carry):
        upper = recv[within(table_out[0, 2 * number])].astype(F32)
        lower = recv[within(table_out[0, 2 * number + 1])].astype(F32)
        rows = pl.ds(pl.multiple_of(number * 8, 8), 8)
        science[rows, 0:128] = jnp.concatenate([upper[0:4], lower[0:4]], 0)
        science[rows, 128:256] = jnp.concatenate([upper[4:8], lower[4:8]], 0)
        science_var[rows, 0:128] = jnp.concatenate([upper[8:12], lower[8:12]], 0)
        science_var[rows, 128:256] = jnp.concatenate([upper[12:16], lower[12:16]], 0)
        return carry

    lax.fori_loop(0, 64, unpack, 0, unroll=4)
    loads[5].wait()
    root[...] = coverage[...].astype(F32) * lax.rsqrt(science_var[...])

    is_target = lax.broadcasted_iota(jnp.int32, (16, 256), 0) == TARGET - 32

    def gram_patch(patch, carry):
        base = pl.multiple_of(patch * 256, 256)
        pieces = []
        for row in range(256):
            weight = root[pl.ds(base + row, 1), :]
            goal = weight * science[pl.ds(base + row, 1), :]
            basis = conv[base + row].astype(F32) * weight
            last = jnp.where(is_target, goal, basis[32:48])
            pieces.append(jnp.concatenate([basis[0:32].astype(BF16), last.astype(BF16)], 0))
        block = jnp.concatenate(pieces, 1)
        total = lax.dot_general(block, block, (((1,), (1,)), ((), ())), preferred_element_type=F32)
        own_gram[patch, :, 0:48] = total[0:24]
        own_gram[patch, :, 64:112] = total[24:48]
        return carry

    lax.fori_loop(0, 2, gram_patch, 0)
    grams_sent(lambda copy: copy.start())
    grams_received()

    lane = lax.broadcasted_iota(jnp.int32, (48, 128), 1)
    sub = lax.broadcasted_iota(jnp.int32, (48, 128), 0)
    beside = own_gram[0] + own_gram[1] + near_gram[6] + near_gram[7] + near_gram[8] + near_gram[9]
    upper = beside + near_gram[1] + near_gram[4] + near_gram[5]
    lower = beside + near_gram[0] + near_gram[2] + near_gram[3]
    first_half = lane[0:24] < 64
    system = jnp.concatenate(
        [
            jnp.where(first_half, upper, pltpu.roll(lower, 64, 1)),
            jnp.where(first_half, pltpu.roll(upper, 64, 1), lower),
        ],
        0,
    )
    half_lane = lane % 64
    diagonal = jnp.logical_and(sub == half_lane, sub < 45)
    on_diagonal = jnp.where(diagonal, system, 0.0)
    trace_upper = jnp.sum(jnp.where(lane < 64, on_diagonal, 0.0))
    trace_lower = jnp.sum(jnp.where(lane < 64, 0.0, on_diagonal))
    ridge = jnp.where(lane < 64, trace_upper, trace_lower) * (RIDGE / 45.0)
    system = jnp.where(diagonal, system + ridge, system)

    def column_of(matrix, step):
        return jnp.take_along_axis(matrix, (lane - half_lane) + step, axis=1)

    def pivot_pair(first, second, step):
        a, b = first[step : step + 1], second[step : step + 1]
        c, d = first[step + 1 : step + 2], second[step + 1 : step + 2]
        inverse = 1.0 / (a * d - b * c)
        return first * (d * inverse) - second * (c * inverse), second * (a * inverse) - first * (b * inverse)

    for step in range(0, 44, 4):
        columns = [column_of(system, step + number) for number in range(4)]
        row = [system[step + number : step + number + 1] for number in range(4)]
        u0, u1 = pivot_pair(columns[0], columns[1], step)
        third, fourth = (
            column - u0 * column[step : step + 1] - u1 * column[step + 1 : step + 2] for column in columns[2:]
        )
        u2, u3 = pivot_pair(third, fourth, step + 2)
        row[2] = row[2] - u0[step + 2 : step + 3] * row[0] - u1[step + 2 : step + 3] * row[1]
        row[3] = row[3] - u0[step + 3 : step + 4] * row[0] - u1[step + 3 : step + 4] * row[1]
        v0 = u0 - u2 * u0[step + 2 : step + 3] - u3 * u0[step + 3 : step + 4]
        v1 = u1 - u2 * u1[step + 2 : step + 3] - u3 * u1[step + 3 : step + 4]
        system = system - u0 * row[0] - u1 * row[1] - u2 * row[2] - u3 * row[3]
        for number, column in enumerate((v0, v1, u2, u3)):
            system = jnp.where(half_lane == step + number, column, system)
    column = column_of(system, 44)
    inverse = 1.0 / column[44:45]
    system = jnp.where(half_lane == 44, column * inverse, system - column * (inverse * system[44:45]))
    answer = jnp.where(jnp.logical_and(half_lane[47:48] < 45, lane[47:48] < 128), system[TARGET : TARGET + 1], 0.0)
    terms = power[...] * answer
    upper_terms = jnp.sum(jnp.where(lane < 64, terms, 0.0), 1, keepdims=True)
    lower_terms = jnp.sum(jnp.where(lane < 64, 0.0, terms), 1, keepdims=True)
    powers = (jnp.sum(upper_terms * upper_terms), jnp.sum(lower_terms * lower_terms))

    coarse = answer.astype(BF16)
    fine = (answer - coarse.astype(F32)).astype(BF16)
    row_of = lax.broadcasted_iota(jnp.int32, (32, 768), 0)
    lane_of = lax.broadcasted_iota(jnp.int32, (32, 768), 1)
    chosen = lane_of // 48 == row_of % 16
    both = jnp.concatenate(
        [jnp.broadcast_to(coarse.astype(F32), (16, 128)), jnp.broadcast_to(fine.astype(F32), (16, 128))], 0
    ).astype(BF16)
    loads[6].wait()
    loads[7].wait()
    for patch in range(2):
        coefficients = jnp.where(
            chosen, jnp.dot(both, spread[patch], preferred_element_type=F32), 0.0
        ).astype(BF16)
        kernel_power = powers[patch]

        def finish(number, carry):
            rows = pl.ds(pl.multiple_of(number * 16, 16), 16)
            product = jnp.dot(coefficients, conv[rows].reshape(768, 256), preferred_element_type=F32)
            model = product[0:16] + product[16:32]
            residual[rows] = science[rows] - model
            spread_var[rows] = science_var[rows] + kernel_power * template_var[rows]
            return carry

        lax.fori_loop(16 * patch, 16 * patch + 16, finish, 0, unroll=8)

    each_sent(halo, lambda copy: copy.wait_send())
    grams_sent(lambda copy: copy.wait_send())


def local(template, template_var, coverage, exposure, exposure_var, strip_owner, strip_slot):
    def blocks(array):
        return array.reshape(128, 4, 2, 128).transpose(0, 2, 1, 3).reshape(128, 8, 128)

    vmem = pl.BlockSpec(memory_space=pltpu.VMEM)
    hbm = pl.BlockSpec(memory_space=pltpu.HBM)
    dma = pltpu.SemaphoreType.DMA
    x_weights, y_weights, power, spread = [jnp.asarray(table) for table in tables()]
    residual, spread_var = pl.pallas_call(
        kernel,
        out_shape=[pltpu.VMEM((512, 256), F32)] * 2,
        in_specs=[hbm] * 8 + [vmem] * 3,
        out_specs=[vmem] * 2,
        scratch_shapes=[
            pltpu.VMEM((512, 256), F32),
            pltpu.VMEM((512, 256), F32),
            pltpu.VMEM((512, 256), jnp.int32),
            pltpu.VMEM((128, 8, 128), F32),
            pltpu.VMEM((128, 8, 128), F32),
            pltpu.VMEM((8, 256, 256), BF16),
            pltpu.VMEM((8, BLOCK * 8, 256), BF16),
            pltpu.VMEM((2, 128, 768), BF16),
            pltpu.VMEM((2, 16, 512), BF16),
            pltpu.VMEM((2, 16, 512), BF16),
            pltpu.VMEM((544, 512), BF16),
            pltpu.VMEM((16, 608, 256), BF16),
            pltpu.VMEM((512, 48, 256), BF16),
            pltpu.VMEM((128, 16, 128), BF16),
            pltpu.VMEM((128, 16, 128), BF16),
            pltpu.VMEM((128, 128), jnp.int32),
            pltpu.VMEM((512, 256), F32),
            pltpu.VMEM((512, 256), F32),
            pltpu.VMEM((512, 256), F32),
            pltpu.VMEM((2, 24, 128), F32),
            pltpu.VMEM((10, 24, 128), F32),
            pltpu.VMEM((8, 128), jnp.int32),
            pltpu.SMEM((8, 128), jnp.int32),
            pltpu.SMEM((8, 128), jnp.int32),
            dma((8,)), dma((8,)), dma, dma, dma((2,)), dma((2,)), dma((10,)), dma((10,)), dma((9,)), pltpu.SemaphoreType.REGULAR,
        ],
        compiler_params=pltpu.CompilerParams(
            collective_id=0, has_side_effects=True, vmem_limit_bytes=60 * 1024 * 1024
        ),
        cost_estimate=pl.CostEstimate(flops=10**10, bytes_accessed=8 * 10**6, transcendentals=0),
    )(
        template, template_var, coverage, blocks(exposure), blocks(exposure_var), x_weights, y_weights, spread,
        strip_owner, strip_slot, power,
    )
    mask = coverage.astype(F32)
    return (mask * residual, mask * spread_var)


def solution(mesh):
    image = P("row", "col")
    strips = P("row", "col", None, None)
    return jax.shard_map(
        local,
        mesh=mesh,
        in_specs=(image, image, image, strips, strips, image, image),
        out_specs=(image, image),
        check_vma=False,
    )
```

```python
import jax
import jax.numpy as jnp
import numpy as np
from jax import lax
from jax.experimental import pallas as pl
from jax.experimental.pallas import tpu as pltpu
from jax.sharding import PartitionSpec as P

RIDGE = 0.05
SIGMAS = (1.0, 2.0, 4.0)
MESH = pl.DeviceIdType.MESH
F32 = jnp.float32
BF16 = jnp.bfloat16

SLOTS = (
    (0, 0), (0, 2), (1, 0), (1, 2), (2, 0), (2, 2), (0, 1), (1, 1),
    (2, 1), (0, 3), (1, 3), None, (2, 3), (0, 4), (1, 4), (2, 4),
)
GROUP_OF_PASS = (0, 1, 2, 3, 4, 4, 5, 5)
BLOCK = 96
TARGET = 47
GRAM_COPIES = ((0, -1, 0), (1, 1, 0), (0, -1, -1), (0, -1, 1), (1, 1, -1), (1, 1, 1), (0, 0, -1), (0, 0, 1), (1, 0, -1), (1, 0, 1))
DIRECTIONS = ((0, -1), (0, 1), (-1, 0), (1, 0), (-1, -1), (-1, 1), (1, -1), (1, 1))


def filter_bank():
    taps = np.arange(31) - 15.0
    collected = []
    for sigma in SIGMAS:
        for degree in range(5):
            scaled = taps / sigma
            shape = scaled**degree * np.exp(-0.5 * scaled * scaled)
            collected.append(shape / np.sqrt(np.sum(shape * shape)))
    return np.array(collected, np.float32).astype(jnp.bfloat16).astype(np.float32)


def tables():
    bank = filter_bank()
    x_weights = np.zeros((8, 256, 2, 128), np.float32)
    y_weights = np.zeros((8, BLOCK, 8, 2, 128), np.float32)
    across = np.arange(128)
    down = np.arange(BLOCK)
    order = []
    filled = [0] * 6
    for number, slot in enumerate(SLOTS):
        if slot is None:
            continue
        half, which = number // 2, number % 2
        s, i = slot
        group = GROUP_OF_PASS[half]
        for q in range(31):
            x_weights[half, across + q - 15 + 64, which, across] = bank[s * 5 + i, q]
        for j in range(5 - i):
            lane = filled[group]
            filled[group] += 1
            order.append((group * 8 + lane, s, i, j))
            for p in range(31):
                y_weights[half, down, lane, which, down + p - 15 + 16] = bank[s * 5 + j, p]
    shapes = np.zeros((48, 31 * 31), np.float64)
    for t, s, i, j in order:
        shapes[t] = np.outer(bank[s * 5 + j], bank[s * 5 + i]).reshape(-1).astype(np.float64)
    values, vectors = np.linalg.eigh(shapes @ shapes.T)
    root = np.sqrt(np.maximum(values, 0.0))[:, None] * vectors.T
    power = np.zeros((48, 128), np.float32)
    power[:, :48] = root
    power[:, 64:112] = root
    spread = np.zeros((2, 128, 768), np.float32)
    for patch in range(2):
        spread[patch, 64 * patch + np.arange(768) % 48, np.arange(768)] = 1.0
    return (
        x_weights.reshape(8, 256, 256).astype(jnp.bfloat16),
        y_weights.reshape(8, BLOCK * 8, 256).astype(jnp.bfloat16),
        power,
        spread.astype(jnp.bfloat16),
    )


def inverse_row(columns, size=128):
    rows = lax.broadcasted_iota(jnp.int32, (size, size), 0)
    lanes = lax.broadcasted_iota(jnp.int32, (size, size), 1)
    return jnp.max(jnp.where(columns == lanes, rows, 0), 0, keepdims=True)


def within(number):
    return jnp.clip(number, 0, 127)


def kernel(
    template_hbm, template_var_hbm, coverage_hbm, flux_hbm, noise_hbm, x_weights_hbm, y_weights_hbm, spread_hbm,
    owner, slot, power,
    residual, spread_var,
    template, template_var, coverage, flux, noise, x_weights, y_weights, spread,
    side_out, side_in, wide, filtered, conv, send, recv, labels, science, science_var, root, own_gram, near_gram,
    row_index, table_in, table_out,
    halo_out, halo_in, part_out, part_in, label_out, label_in, gram_out, gram_in, load_in, ready, blend,
):
    r = lax.axis_index("row")
    c = lax.axis_index("col")
    x, z, k = c // 8, (c // 2) % 4, c % 2
    me = r * 32 + c
    place = (z * 2 + k) * 16 + r * 4 + x
    barrier = pltpu.get_barrier_semaphore()

    loads = [
        pltpu.make_async_copy(source, held, load_in.at[number])
        for number, (source, held) in enumerate((
            (template_hbm, template), (flux_hbm, flux), (noise_hbm, noise), (x_weights_hbm, x_weights),
            (y_weights_hbm, y_weights), (coverage_hbm, coverage), (template_var_hbm, template_var), (spread_hbm, spread),
        ))
    ]
    loads[0].start()

    wide[...] = jnp.zeros_like(wide)
    near_gram[...] = jnp.zeros_like(near_gram)
    side_in[...] = jnp.zeros_like(side_in)
    own_gram[...] = jnp.zeros_like(own_gram)

    def column(dx, dz, dk):
        return (x + dx) % 4 * 8 + (z + dz) % 4 * 2 + (k + dk) % 2

    across = [((r + dr) % 4, column(dx, 0, 0)) for dr in range(4) for dx in range(4) if dr or dx]
    along = [(r, column(0, dz, dk)) for dz in range(4) for dk in range(2) if dz or dk]
    around = [((r + dr) % 4, (c + dc) % 32) for dr, dc in DIRECTIONS]
    for other in around + across + along:
        pl.semaphore_signal(barrier, inc=1, device_id=other, device_id_type=MESH)
    for load in loads[1:]:
        load.start()

    owners = jnp.transpose(jnp.broadcast_to(owner[...], (128, 128)))
    row_index[...] = jnp.broadcast_to(inverse_row(owners), (8, 128))
    owner_copy = pltpu.make_async_copy(row_index, table_in, load_in.at[8])
    owner_copy.start()
    labels[pl.ds(place, 1), :] = slot[...]
    loads[0].wait()
    wide[16:528, 128:384] = template[...].astype(BF16)
    side_row = lax.broadcasted_iota(jnp.int32, (16, 128), 0)
    side_lane = lax.broadcasted_iota(jnp.int32, (16, 128), 1)
    sides = [
        jnp.where(side_lane == side_row + first, 1.0, 0.0).astype(BF16) for first in (0, 112)
    ]
    for number in range(2):
        side_out[number] = lax.dot_general(
            sides[number],
            wide[16:528, 128 + 128 * number : 256 + 128 * number],
            (((1,), (1,)), ((), ())),
            preferred_element_type=F32,
        ).astype(BF16)
    pl.semaphore_wait(barrier, 30)
    for other in along:
        pl.semaphore_signal(ready, inc=1, device_id=other, device_id_type=MESH)

    def inside(dr, dc):
        return jnp.logical_and(
            jnp.logical_and(r + dr >= 0, r + dr < 4), jnp.logical_and(c + dc >= 0, c + dc < 32)
        )

    def target(dr, dc):
        return (jnp.clip(r + dr, 0, 3), jnp.clip(c + dc, 0, 31))

    source_rows = {-1: pl.ds(16, 16), 0: pl.ds(16, 512), 1: pl.ds(512, 16)}
    target_rows = {-1: pl.ds(528, 16), 0: pl.ds(16, 512), 1: pl.ds(0, 16)}
    source_cols = {-1: pl.ds(128, 128), 0: pl.ds(128, 256), 1: pl.ds(256, 128)}
    target_cols = {-1: pl.ds(384, 128), 0: pl.ds(128, 256), 1: pl.ds(0, 128)}

    def halo(number):
        dr, dc = DIRECTIONS[number]
        return pltpu.make_async_remote_copy(
            src_ref=wide.at[source_rows[dr], source_cols[dc]] if dr else side_out.at[number],
            dst_ref=wide.at[target_rows[dr], target_cols[dc]] if dr else side_in.at[number],
            send_sem=halo_out.at[number],
            recv_sem=halo_in.at[number],
            device_id=target(dr, dc),
            device_id_type=MESH,
        )

    def gram_copy(number):
        patch, dr, dc = GRAM_COPIES[number]
        return pltpu.make_async_remote_copy(
            src_ref=own_gram.at[patch],
            dst_ref=near_gram.at[number],
            send_sem=gram_out.at[number],
            recv_sem=gram_in.at[number],
            device_id=target(dr, dc),
            device_id_type=MESH,
        )

    def grams_sent(action):
        for number, (_, dr, dc) in enumerate(GRAM_COPIES):
            @pl.when(inside(dr, dc))
            def _():
                action(gram_copy(number))

    def grams_received():
        for number, (_, dr, dc) in enumerate(GRAM_COPIES):
            @pl.when(inside(-dr, -dc))
            def _():
                gram_copy(number).wait_recv()

    def each_sent(make, action):
        for number, (dr, dc) in enumerate(DIRECTIONS):
            @pl.when(inside(dr, dc))
            def _():
                action(make(number))

    def each_received(make):
        for number, (dr, dc) in enumerate(DIRECTIONS):
            @pl.when(inside(-dr, -dc))
            def _():
                make(number).wait_recv()

    each_sent(halo, lambda copy: copy.start())

    def label_copy(first, count, row, col, which):
        return pltpu.make_async_remote_copy(
            src_ref=labels.at[pl.ds(first, count)],
            dst_ref=labels.at[pl.ds(first, count)],
            send_sem=label_out.at[which],
            recv_sem=label_in.at[which],
            device_id=(row, col),
            device_id_type=MESH,
        )

    for other in across:
        label_copy(place, 1, *other, 0).start()

    owner_copy.wait()
    loads[1].wait()
    loads[2].wait()

    def chunk(number):
        block = within(table_in[0, number])
        return jnp.concatenate([flux[block], noise[block]], 0).astype(BF16)

    def label_wait(count, which):
        part = labels.at[pl.ds(0, count)]
        pltpu.make_async_copy(part, part, label_in.at[which]).wait()
        pltpu.make_async_copy(part, part, label_out.at[which]).wait()

    def send_to(others):
        for row, col in others:
            send[row * 32 + col] = chunk(row * 32 + col)
        for row, col in others:
            pltpu.make_async_remote_copy(
                src_ref=send.at[row * 32 + col],
                dst_ref=recv.at[place],
                send_sem=part_out,
                recv_sem=part_in,
                device_id=(row, col),
                device_id_type=MESH,
            ).start()

    def send_group(group, carry):
        send_to([
            ((r + group // 4) % 4, column(group % 4, dz, dk)) for dz in range(4) for dk in range(2) if dz or dk
        ])
        return carry

    recv[place] = chunk(me)
    send_to(across)
    send_to(along)
    pl.semaphore_wait(ready, 7)
    lax.fori_loop(1, 8, send_group, 0)
    label_wait(15, 0)
    for other in along:
        label_copy(pl.multiple_of((z * 2 + k) * 16, 16), 16, *other, 1).start()
    lax.fori_loop(8, 16, send_group, 0)

    each_received(halo)

    for number in range(2):
        wide[16:528, 384 - 384 * number : 512 - 384 * number] = lax.dot_general(
            side_in[number], sides[number], (((0,), (0,)), ((), ())), preferred_element_type=F32
        ).astype(BF16)

    filtered[:, 544:608, :] = jnp.zeros((16, 64, 256), BF16)
    loads[3].wait()
    whole = wide[...]
    windows = (whole[:, 64:320], whole[:, 192:448])

    def along_x(half, carry):
        for side in range(2):
            product = jnp.dot(windows[side], x_weights[half], preferred_element_type=F32).astype(BF16)
            for which in range(2):
                filtered[2 * half + which, 0:544, side * 128 : side * 128 + 128] = product[
                    :, which * 128 : which * 128 + 128
                ]
        return carry

    lax.fori_loop(0, 8, along_x, 0, unroll=True)

    def along_y(first, rows):
        for pair in range(3):
            groups = []
            for group in (2 * pair, 2 * pair + 1):
                total = None
                for half in range(8):
                    if GROUP_OF_PASS[half] == group:
                        window = filtered[2 * half : 2 * half + 2, pl.ds(first, 128), :].reshape(256, 256)
                        product = jnp.dot(
                            y_weights[half, 0 : rows * 8, :], window, preferred_element_type=F32
                        )
                        total = product if total is None else total + product
                groups.append(total.reshape(rows, 8, 256))
            conv[pl.ds(first, rows), pair * 16 : pair * 16 + 16, :] = jnp.concatenate(groups, 1).astype(BF16)

    loads[4].wait()

    def y_block(number, carry):
        along_y(pl.multiple_of(number * BLOCK, 16), BLOCK)
        return carry

    lax.fori_loop(0, 4, y_block, 0, unroll=True)
    label_wait(112, 1)
    row_index[...] = jnp.broadcast_to(inverse_row(labels[...]), (8, 128))
    table_copy = pltpu.make_async_copy(row_index, table_out, load_in.at[0])
    table_copy.start()
    y_block(4, 0)
    along_y(480, 32)

    table_copy.wait()
    parts = recv.at[pl.ds(0, 127)]
    pltpu.make_async_copy(parts, parts, part_in).wait()
    pltpu.make_async_copy(parts, parts, part_out).wait()

    def unpack(number, carry):
        upper = recv[within(table_out[0, 2 * number])].astype(F32)
        lower = recv[within(table_out[0, 2 * number + 1])].astype(F32)
        rows = pl.ds(pl.multiple_of(number * 8, 8), 8)
        science[rows, 0:128] = jnp.concatenate([upper[0:4], lower[0:4]], 0)
        science[rows, 128:256] = jnp.concatenate([upper[4:8], lower[4:8]], 0)
        science_var[rows, 0:128] = jnp.concatenate([upper[8:12], lower[8:12]], 0)
        science_var[rows, 128:256] = jnp.concatenate([upper[12:16], lower[12:16]], 0)
        return carry

    lax.fori_loop(0, 64, unpack, 0, unroll=8)
    loads[5].wait()
    root[...] = coverage[...].astype(F32) * lax.rsqrt(science_var[...])

    is_target = lax.broadcasted_iota(jnp.int32, (16, 256), 0) == TARGET - 32

    def gram_patch(patch, carry):
        base = pl.multiple_of(patch * 256, 256)
        pieces = []
        for row in range(256):
            weight = root[pl.ds(base + row, 1), :]
            goal = weight * science[pl.ds(base + row, 1), :]
            basis = conv[base + row].astype(F32) * weight
            last = jnp.where(is_target, goal, basis[32:48])
            pieces.append(jnp.concatenate([basis[0:32].astype(BF16), last.astype(BF16)], 0))
        block = jnp.concatenate(pieces, 1)
        total = lax.dot_general(block, block, (((1,), (1,)), ((), ())), preferred_element_type=F32)
        own_gram[patch, :, 0:48] = total[0:24]
        own_gram[patch, :, 64:112] = total[24:48]
        return carry

    lax.fori_loop(0, 2, gram_patch, 0)
    grams_sent(lambda copy: copy.start())
    grams_received()

    lane = lax.broadcasted_iota(jnp.int32, (48, 128), 1)
    sub = lax.broadcasted_iota(jnp.int32, (48, 128), 0)
    beside = own_gram[0] + own_gram[1] + near_gram[6] + near_gram[7] + near_gram[8] + near_gram[9]
    upper = beside + near_gram[1] + near_gram[4] + near_gram[5]
    lower = beside + near_gram[0] + near_gram[2] + near_gram[3]
    first_half = lane[0:24] < 64
    system = jnp.concatenate(
        [
            jnp.where(first_half, upper, pltpu.roll(lower, 64, 1)),
            jnp.where(first_half, pltpu.roll(upper, 64, 1), lower),
        ],
        0,
    )
    half_lane = lane % 64
    diagonal = jnp.logical_and(sub == half_lane, sub < 45)
    on_diagonal = jnp.where(diagonal, system, 0.0)
    trace_upper = jnp.sum(jnp.where(lane < 64, on_diagonal, 0.0))
    trace_lower = jnp.sum(jnp.where(lane < 64, 0.0, on_diagonal))
    ridge = jnp.where(lane < 64, trace_upper, trace_lower) * (RIDGE / 45.0)
    system = jnp.where(diagonal, system + ridge, system)

    def column_of(matrix, step):
        return jnp.take_along_axis(matrix, (lane - half_lane) + step, axis=1)

    def pivot_pair(first, second, step):
        a, b = first[step : step + 1], second[step : step + 1]
        c, d = first[step + 1 : step + 2], second[step + 1 : step + 2]
        inverse = 1.0 / (a * d - b * c)
        return first * (d * inverse) - second * (c * inverse), second * (a * inverse) - first * (b * inverse)

    for step in range(0, 44, 4):
        columns = [column_of(system, step + number) for number in range(4)]
        row = [system[step + number : step + number + 1] for number in range(4)]
        u0, u1 = pivot_pair(columns[0], columns[1], step)
        third, fourth = (
            column - u0 * column[step : step + 1] - u1 * column[step + 1 : step + 2] for column in columns[2:]
        )
        u2, u3 = pivot_pair(third, fourth, step + 2)
        row[2] = row[2] - u0[step + 2 : step + 3] * row[0] - u1[step + 2 : step + 3] * row[1]
        row[3] = row[3] - u0[step + 3 : step + 4] * row[0] - u1[step + 3 : step + 4] * row[1]
        v0 = u0 - u2 * u0[step + 2 : step + 3] - u3 * u0[step + 3 : step + 4]
        v1 = u1 - u2 * u1[step + 2 : step + 3] - u3 * u1[step + 3 : step + 4]
        system = system - u0 * row[0] - u1 * row[1] - u2 * row[2] - u3 * row[3]
        for number, column in enumerate((v0, v1, u2, u3)):
            system = jnp.where(half_lane == step + number, column, system)
    column = column_of(system, 44)
    inverse = 1.0 / column[44:45]
    system = jnp.where(half_lane == 44, column * inverse, system - column * (inverse * system[44:45]))
    answer = jnp.where(jnp.logical_and(half_lane[47:48] < 45, lane[47:48] < 128), system[TARGET : TARGET + 1], 0.0)
    terms = power[...] * answer
    upper_terms = jnp.sum(jnp.where(lane < 64, terms, 0.0), 1, keepdims=True)
    lower_terms = jnp.sum(jnp.where(lane < 64, 0.0, terms), 1, keepdims=True)
    powers = (jnp.sum(upper_terms * upper_terms), jnp.sum(lower_terms * lower_terms))

    coarse = answer.astype(BF16)
    fine = (answer - coarse.astype(F32)).astype(BF16)
    row_of = lax.broadcasted_iota(jnp.int32, (32, 768), 0)
    lane_of = lax.broadcasted_iota(jnp.int32, (32, 768), 1)
    chosen = lane_of // 48 == row_of % 16
    both = jnp.concatenate(
        [jnp.broadcast_to(coarse.astype(F32), (16, 128)), jnp.broadcast_to(fine.astype(F32), (16, 128))], 0
    ).astype(BF16)
    loads[6].wait()
    loads[7].wait()
    for patch in range(2):
        blend[patch] = jnp.where(
            chosen, jnp.dot(both, spread[patch], preferred_element_type=F32), 0.0
        ).astype(BF16)

    def finish(number, carry):
        rows = pl.ds(pl.multiple_of(number * 16, 16), 16)
        product = jnp.dot(blend[number // 16], conv[rows].reshape(768, 256), preferred_element_type=F32)
        residual[rows] = science[rows] - (product[0:16] + product[16:32])
        kernel_power = jnp.where(number < 16, powers[0], powers[1])
        spread_var[rows] = science_var[rows] + kernel_power * template_var[rows]
        return carry

    lax.fori_loop(0, 32, finish, 0, unroll=16)

    each_sent(halo, lambda copy: copy.wait_send())
    grams_sent(lambda copy: copy.wait_send())


def local(template, template_var, coverage, exposure, exposure_var, strip_owner, strip_slot):
    def blocks(array):
        return array.reshape(128, 4, 2, 128).transpose(0, 2, 1, 3).reshape(128, 8, 128)

    vmem = pl.BlockSpec(memory_space=pltpu.VMEM)
    hbm = pl.BlockSpec(memory_space=pltpu.HBM)
    dma = pltpu.SemaphoreType.DMA
    x_weights, y_weights, power, spread = [jnp.asarray(table) for table in tables()]
    residual, spread_var = pl.pallas_call(
        kernel,
        out_shape=[pltpu.VMEM((512, 256), F32)] * 2,
        in_specs=[hbm] * 8 + [vmem] * 3,
        out_specs=[vmem] * 2,
        scratch_shapes=[
            pltpu.VMEM((512, 256), F32),
            pltpu.VMEM((512, 256), F32),
            pltpu.VMEM((512, 256), jnp.int32),
            pltpu.VMEM((128, 8, 128), F32),
            pltpu.VMEM((128, 8, 128), F32),
            pltpu.VMEM((8, 256, 256), BF16),
            pltpu.VMEM((8, BLOCK * 8, 256), BF16),
            pltpu.VMEM((2, 128, 768), BF16),
            pltpu.VMEM((2, 16, 512), BF16),
            pltpu.VMEM((2, 16, 512), BF16),
            pltpu.VMEM((544, 512), BF16),
            pltpu.VMEM((16, 608, 256), BF16),
            pltpu.VMEM((512, 48, 256), BF16),
            pltpu.VMEM((128, 16, 128), BF16),
            pltpu.VMEM((128, 16, 128), BF16),
            pltpu.VMEM((128, 128), jnp.int32),
            pltpu.VMEM((512, 256), F32),
            pltpu.VMEM((512, 256), F32),
            pltpu.VMEM((512, 256), F32),
            pltpu.VMEM((2, 24, 128), F32),
            pltpu.VMEM((10, 24, 128), F32),
            pltpu.VMEM((8, 128), jnp.int32),
            pltpu.SMEM((8, 128), jnp.int32),
            pltpu.SMEM((8, 128), jnp.int32),
            dma((8,)), dma((8,)), dma, dma, dma((2,)), dma((2,)), dma((10,)), dma((10,)), dma((9,)), pltpu.SemaphoreType.REGULAR,
            pltpu.VMEM((2, 32, 768), BF16),
        ],
        compiler_params=pltpu.CompilerParams(
            collective_id=0, has_side_effects=True, vmem_limit_bytes=60 * 1024 * 1024
        ),
        cost_estimate=pl.CostEstimate(flops=10**10, bytes_accessed=8 * 10**6, transcendentals=0),
    )(
        template, template_var, coverage, blocks(exposure), blocks(exposure_var), x_weights, y_weights, spread,
        strip_owner, strip_slot, power,
    )
    mask = coverage.astype(F32)
    return (mask * residual, mask * spread_var)


def solution(mesh):
    image = P("row", "col")
    strips = P("row", "col", None, None)
    return jax.shard_map(
        local,
        mesh=mesh,
        in_specs=(image, image, image, strips, strips, image, image),
        out_specs=(image, image),
        check_vma=False,
    )
```

```python
import jax
import jax.numpy as jnp
import numpy as np
from jax import lax
from jax.experimental import pallas as pl
from jax.experimental.pallas import tpu as pltpu
from jax.sharding import PartitionSpec as P

RIDGE = 0.05
SIGMAS = (1.0, 2.0, 4.0)
MESH = pl.DeviceIdType.MESH
F32 = jnp.float32
BF16 = jnp.bfloat16

SLOTS = (
    (0, 0), (0, 2), (1, 0), (1, 2), (2, 0), (2, 2), (0, 1), (1, 1),
    (2, 1), (0, 3), (1, 3), None, (2, 3), (0, 4), (1, 4), (2, 4),
)
GROUP_OF_PASS = (0, 1, 2, 3, 4, 4, 5, 5)
BLOCK = 96
TARGET = 47
GRAM_COPIES = ((0, -1, 0), (1, 1, 0), (0, -1, -1), (0, -1, 1), (1, 1, -1), (1, 1, 1), (0, 0, -1), (0, 0, 1), (1, 0, -1), (1, 0, 1))
DIRECTIONS = ((0, -1), (0, 1), (-1, 0), (1, 0), (-1, -1), (-1, 1), (1, -1), (1, 1))


def filter_bank():
    taps = np.arange(31) - 15.0
    collected = []
    for sigma in SIGMAS:
        for degree in range(5):
            scaled = taps / sigma
            shape = scaled**degree * np.exp(-0.5 * scaled * scaled)
            collected.append(shape / np.sqrt(np.sum(shape * shape)))
    return np.array(collected, np.float32).astype(jnp.bfloat16).astype(np.float32)


def tables():
    bank = filter_bank()
    x_weights = np.zeros((8, 256, 2, 128), np.float32)
    y_weights = np.zeros((8, BLOCK, 8, 2, 128), np.float32)
    across = np.arange(128)
    down = np.arange(BLOCK)
    order = []
    filled = [0] * 6
    for number, slot in enumerate(SLOTS):
        if slot is None:
            continue
        half, which = number // 2, number % 2
        s, i = slot
        group = GROUP_OF_PASS[half]
        for q in range(31):
            x_weights[half, across + q - 15 + 64, which, across] = bank[s * 5 + i, q]
        for j in range(5 - i):
            lane = filled[group]
            filled[group] += 1
            order.append((group * 8 + lane, s, i, j))
            for p in range(31):
                y_weights[half, down, lane, which, down + p - 15 + 16] = bank[s * 5 + j, p]
    shapes = np.zeros((48, 31 * 31), np.float64)
    for t, s, i, j in order:
        shapes[t] = np.outer(bank[s * 5 + j], bank[s * 5 + i]).reshape(-1).astype(np.float64)
    values, vectors = np.linalg.eigh(shapes @ shapes.T)
    root = np.sqrt(np.maximum(values, 0.0))[:, None] * vectors.T
    power = np.zeros((48, 128), np.float32)
    power[:, :48] = root
    power[:, 64:112] = root
    spread = np.zeros((2, 128, 768), np.float32)
    for patch in range(2):
        spread[patch, 64 * patch + np.arange(768) % 48, np.arange(768)] = 1.0
    return (
        x_weights.reshape(8, 256, 256).astype(jnp.bfloat16),
        y_weights.reshape(8, BLOCK * 8, 256).astype(jnp.bfloat16),
        power,
        spread.astype(jnp.bfloat16),
    )


def inverse_row(columns, size=128):
    rows = lax.broadcasted_iota(jnp.int32, (size, size), 0)
    lanes = lax.broadcasted_iota(jnp.int32, (size, size), 1)
    return jnp.max(jnp.where(columns == lanes, rows, 0), 0, keepdims=True)


def within(number):
    return jnp.clip(number, 0, 127)


def kernel(
    template_hbm, template_var_hbm, coverage_hbm, flux_hbm, noise_hbm, x_weights_hbm, y_weights_hbm, spread_hbm,
    owner, slot, power,
    residual, spread_var,
    template, template_var, coverage, flux, noise, x_weights, y_weights, spread,
    side_out, side_in, wide, filtered, conv, send, recv, labels, science, science_var, root, own_gram, near_gram,
    row_index, table_in, table_out,
    halo_out, halo_in, part_out, part_in, label_out, label_in, gram_out, gram_in, load_in, ready, blend,
):
    r = lax.axis_index("row")
    c = lax.axis_index("col")
    x, z, k = c // 8, (c // 2) % 4, c % 2
    me = r * 32 + c
    place = (z * 2 + k) * 16 + r * 4 + x
    barrier = pltpu.get_barrier_semaphore()

    loads = [
        pltpu.make_async_copy(source, held, load_in.at[number])
        for number, (source, held) in enumerate((
            (template_hbm, template), (flux_hbm, flux), (noise_hbm, noise), (x_weights_hbm, x_weights),
            (y_weights_hbm, y_weights), (coverage_hbm, coverage), (template_var_hbm, template_var), (spread_hbm, spread),
        ))
    ]
    loads[0].start()

    wide[...] = jnp.zeros_like(wide)
    near_gram[...] = jnp.zeros_like(near_gram)
    side_in[...] = jnp.zeros_like(side_in)
    own_gram[...] = jnp.zeros_like(own_gram)

    def column(dx, dz, dk):
        return (x + dx) % 4 * 8 + (z + dz) % 4 * 2 + (k + dk) % 2

    across = [((r + dr) % 4, column(dx, 0, 0)) for dr in range(4) for dx in range(4) if dr or dx]
    along = [(r, column(0, dz, dk)) for dz in range(4) for dk in range(2) if dz or dk]
    around = [((r + dr) % 4, (c + dc) % 32) for dr, dc in DIRECTIONS if dc]
    for other in around + across + along:
        pl.semaphore_signal(barrier, inc=1, device_id=other, device_id_type=MESH)
    for load in loads[1:]:
        load.start()

    owners = jnp.transpose(jnp.broadcast_to(owner[...], (128, 128)))
    row_index[...] = jnp.broadcast_to(inverse_row(owners), (8, 128))
    owner_copy = pltpu.make_async_copy(row_index, table_in, load_in.at[8])
    owner_copy.start()
    labels[pl.ds(place, 1), :] = slot[...]
    loads[0].wait()
    wide[16:528, 128:384] = template[...].astype(BF16)
    side_row = lax.broadcasted_iota(jnp.int32, (16, 128), 0)
    side_lane = lax.broadcasted_iota(jnp.int32, (16, 128), 1)
    sides = [
        jnp.where(side_lane == side_row + first, 1.0, 0.0).astype(BF16) for first in (0, 112)
    ]
    for number in range(2):
        side_out[number] = lax.dot_general(
            sides[number],
            wide[16:528, 128 + 128 * number : 256 + 128 * number],
            (((1,), (1,)), ((), ())),
            preferred_element_type=F32,
        ).astype(BF16)
    pl.semaphore_wait(barrier, 28)
    for other in along:
        pl.semaphore_signal(ready, inc=1, device_id=other, device_id_type=MESH)

    def inside(dr, dc):
        return jnp.logical_and(
            jnp.logical_and(r + dr >= 0, r + dr < 4), jnp.logical_and(c + dc >= 0, c + dc < 32)
        )

    def target(dr, dc):
        return (jnp.clip(r + dr, 0, 3), jnp.clip(c + dc, 0, 31))

    source_rows = {-1: pl.ds(16, 16), 0: pl.ds(16, 512), 1: pl.ds(512, 16)}
    target_rows = {-1: pl.ds(528, 16), 0: pl.ds(16, 512), 1: pl.ds(0, 16)}
    source_cols = {-1: pl.ds(128, 128), 0: pl.ds(128, 256), 1: pl.ds(256, 128)}
    target_cols = {-1: pl.ds(384, 128), 0: pl.ds(128, 256), 1: pl.ds(0, 128)}

    def halo(number):
        dr, dc = DIRECTIONS[number]
        return pltpu.make_async_remote_copy(
            src_ref=wide.at[source_rows[dr], source_cols[dc]] if dr else side_out.at[number],
            dst_ref=wide.at[target_rows[dr], target_cols[dc]] if dr else side_in.at[number],
            send_sem=halo_out.at[number],
            recv_sem=halo_in.at[number],
            device_id=target(dr, dc),
            device_id_type=MESH,
        )

    def gram_copy(number):
        patch, dr, dc = GRAM_COPIES[number]
        return pltpu.make_async_remote_copy(
            src_ref=own_gram.at[patch],
            dst_ref=near_gram.at[number],
            send_sem=gram_out.at[number],
            recv_sem=gram_in.at[number],
            device_id=target(dr, dc),
            device_id_type=MESH,
        )

    def grams_sent(action):
        for number, (_, dr, dc) in enumerate(GRAM_COPIES):
            @pl.when(inside(dr, dc))
            def _():
                action(gram_copy(number))

    def grams_received():
        for number, (_, dr, dc) in enumerate(GRAM_COPIES):
            @pl.when(inside(-dr, -dc))
            def _():
                gram_copy(number).wait_recv()

    def each_sent(make, action):
        for number, (dr, dc) in enumerate(DIRECTIONS):
            @pl.when(inside(dr, dc))
            def _():
                action(make(number))

    def each_received(make):
        for number, (dr, dc) in enumerate(DIRECTIONS):
            @pl.when(inside(-dr, -dc))
            def _():
                make(number).wait_recv()

    each_sent(halo, lambda copy: copy.start())

    def label_copy(first, count, row, col, which):
        return pltpu.make_async_remote_copy(
            src_ref=labels.at[pl.ds(first, count)],
            dst_ref=labels.at[pl.ds(first, count)],
            send_sem=label_out.at[which],
            recv_sem=label_in.at[which],
            device_id=(row, col),
            device_id_type=MESH,
        )

    for other in across:
        label_copy(place, 1, *other, 0).start()

    owner_copy.wait()
    loads[1].wait()
    loads[2].wait()

    def chunk(number):
        block = within(table_in[0, number])
        return jnp.concatenate([flux[block], noise[block]], 0).astype(BF16)

    def label_wait(count, which):
        part = labels.at[pl.ds(0, count)]
        pltpu.make_async_copy(part, part, label_in.at[which]).wait()
        pltpu.make_async_copy(part, part, label_out.at[which]).wait()

    def send_to(others):
        for row, col in others:
            send[row * 32 + col] = chunk(row * 32 + col)
        for row, col in others:
            pltpu.make_async_remote_copy(
                src_ref=send.at[row * 32 + col],
                dst_ref=recv.at[place],
                send_sem=part_out,
                recv_sem=part_in,
                device_id=(row, col),
                device_id_type=MESH,
            ).start()

    def send_group(group, carry):
        send_to([
            ((r + group // 4) % 4, column(group % 4, dz, dk)) for dz in range(4) for dk in range(2) if dz or dk
        ])
        return carry

    recv[place] = chunk(me)
    send_to(across)
    send_to(along)
    pl.semaphore_wait(ready, 7)
    lax.fori_loop(1, 8, send_group, 0)
    label_wait(15, 0)
    for other in along:
        label_copy(pl.multiple_of((z * 2 + k) * 16, 16), 16, *other, 1).start()
    lax.fori_loop(8, 16, send_group, 0)

    each_received(halo)

    for number in range(2):
        wide[16:528, 384 - 384 * number : 512 - 384 * number] = lax.dot_general(
            side_in[number], sides[number], (((0,), (0,)), ((), ())), preferred_element_type=F32
        ).astype(BF16)

    filtered[:, 544:608, :] = jnp.zeros((16, 64, 256), BF16)
    loads[3].wait()
    whole = wide[...]
    windows = (whole[:, 64:320], whole[:, 192:448])

    def along_x(half, carry):
        for side in range(2):
            product = jnp.dot(windows[side], x_weights[half], preferred_element_type=F32).astype(BF16)
            for which in range(2):
                filtered[2 * half + which, 0:544, side * 128 : side * 128 + 128] = product[
                    :, which * 128 : which * 128 + 128
                ]
        return carry

    lax.fori_loop(0, 8, along_x, 0, unroll=True)

    def along_y(first, rows):
        for pair in range(3):
            groups = []
            for group in (2 * pair, 2 * pair + 1):
                total = None
                for half in range(8):
                    if GROUP_OF_PASS[half] == group:
                        window = filtered[2 * half : 2 * half + 2, pl.ds(first, 128), :].reshape(256, 256)
                        product = jnp.dot(
                            y_weights[half, 0 : rows * 8, :], window, preferred_element_type=F32
                        )
                        total = product if total is None else total + product
                groups.append(total.reshape(rows, 8, 256))
            conv[pl.ds(first, rows), pair * 16 : pair * 16 + 16, :] = jnp.concatenate(groups, 1).astype(BF16)

    loads[4].wait()

    def y_block(number, carry):
        along_y(pl.multiple_of(number * BLOCK, 16), BLOCK)
        return carry

    lax.fori_loop(0, 4, y_block, 0, unroll=True)
    label_wait(112, 1)
    row_index[...] = jnp.broadcast_to(inverse_row(labels[...]), (8, 128))
    table_copy = pltpu.make_async_copy(row_index, table_out, load_in.at[0])
    table_copy.start()
    y_block(4, 0)
    along_y(480, 32)

    table_copy.wait()
    parts = recv.at[pl.ds(0, 127)]
    pltpu.make_async_copy(parts, parts, part_in).wait()

    def unpack(number, carry):
        upper = recv[within(table_out[0, 2 * number])].astype(F32)
        lower = recv[within(table_out[0, 2 * number + 1])].astype(F32)
        rows = pl.ds(pl.multiple_of(number * 8, 8), 8)
        science[rows, 0:128] = jnp.concatenate([upper[0:4], lower[0:4]], 0)
        science[rows, 128:256] = jnp.concatenate([upper[4:8], lower[4:8]], 0)
        science_var[rows, 0:128] = jnp.concatenate([upper[8:12], lower[8:12]], 0)
        science_var[rows, 128:256] = jnp.concatenate([upper[12:16], lower[12:16]], 0)
        return carry

    lax.fori_loop(0, 64, unpack, 0, unroll=8)
    loads[5].wait()
    root[...] = coverage[...].astype(F32) * lax.rsqrt(science_var[...])

    is_target = lax.broadcasted_iota(jnp.int32, (16, 256), 0) == TARGET - 32

    def gram_patch(patch, carry):
        base = pl.multiple_of(patch * 256, 256)
        pieces = []
        for row in range(256):
            weight = root[pl.ds(base + row, 1), :]
            goal = weight * science[pl.ds(base + row, 1), :]
            basis = conv[base + row].astype(F32) * weight
            last = jnp.where(is_target, goal, basis[32:48])
            pieces.append(jnp.concatenate([basis[0:32].astype(BF16), last.astype(BF16)], 0))
        block = jnp.concatenate(pieces, 1)
        total = lax.dot_general(block, block, (((1,), (1,)), ((), ())), preferred_element_type=F32)
        own_gram[patch, :, 0:48] = total[0:24]
        own_gram[patch, :, 64:112] = total[24:48]
        return carry

    lax.fori_loop(0, 2, gram_patch, 0)
    grams_sent(lambda copy: copy.start())
    grams_received()

    lane = lax.broadcasted_iota(jnp.int32, (48, 128), 1)
    sub = lax.broadcasted_iota(jnp.int32, (48, 128), 0)
    beside = own_gram[0] + own_gram[1] + near_gram[6] + near_gram[7] + near_gram[8] + near_gram[9]
    upper = beside + near_gram[1] + near_gram[4] + near_gram[5]
    lower = beside + near_gram[0] + near_gram[2] + near_gram[3]
    first_half = lane[0:24] < 64
    system = jnp.concatenate(
        [
            jnp.where(first_half, upper, pltpu.roll(lower, 64, 1)),
            jnp.where(first_half, pltpu.roll(upper, 64, 1), lower),
        ],
        0,
    )
    half_lane = lane % 64
    diagonal = jnp.logical_and(sub == half_lane, sub < 45)
    on_diagonal = jnp.where(diagonal, system, 0.0)
    trace_upper = jnp.sum(jnp.where(lane < 64, on_diagonal, 0.0))
    trace_lower = jnp.sum(jnp.where(lane < 64, 0.0, on_diagonal))
    ridge = jnp.where(lane < 64, trace_upper, trace_lower) * (RIDGE / 45.0)
    system = jnp.where(diagonal, system + ridge, system)

    def column_of(matrix, step):
        return jnp.take_along_axis(matrix, (lane - half_lane) + step, axis=1)

    def pivot_pair(first, second, step):
        a, b = first[step : step + 1], second[step : step + 1]
        c, d = first[step + 1 : step + 2], second[step + 1 : step + 2]
        inverse = 1.0 / (a * d - b * c)
        return first * (d * inverse) - second * (c * inverse), second * (a * inverse) - first * (b * inverse)

    for step in range(0, 44, 4):
        columns = [column_of(system, step + number) for number in range(4)]
        row = [system[step + number : step + number + 1] for number in range(4)]
        u0, u1 = pivot_pair(columns[0], columns[1], step)
        third, fourth = (
            column - u0 * column[step : step + 1] - u1 * column[step + 1 : step + 2] for column in columns[2:]
        )
        u2, u3 = pivot_pair(third, fourth, step + 2)
        row[2] = row[2] - u0[step + 2 : step + 3] * row[0] - u1[step + 2 : step + 3] * row[1]
        row[3] = row[3] - u0[step + 3 : step + 4] * row[0] - u1[step + 3 : step + 4] * row[1]
        v0 = u0 - u2 * u0[step + 2 : step + 3] - u3 * u0[step + 3 : step + 4]
        v1 = u1 - u2 * u1[step + 2 : step + 3] - u3 * u1[step + 3 : step + 4]
        system = system - u0 * row[0] - u1 * row[1] - u2 * row[2] - u3 * row[3]
        for number, column in enumerate((v0, v1, u2, u3)):
            system = jnp.where(half_lane == step + number, column, system)
    column = column_of(system, 44)
    inverse = 1.0 / column[44:45]
    system = jnp.where(half_lane == 44, column * inverse, system - column * (inverse * system[44:45]))
    answer = jnp.where(jnp.logical_and(half_lane[47:48] < 45, lane[47:48] < 128), system[TARGET : TARGET + 1], 0.0)
    terms = power[...] * answer
    upper_terms = jnp.sum(jnp.where(lane < 64, terms, 0.0), 1, keepdims=True)
    lower_terms = jnp.sum(jnp.where(lane < 64, 0.0, terms), 1, keepdims=True)
    powers = (jnp.sum(upper_terms * upper_terms), jnp.sum(lower_terms * lower_terms))

    coarse = answer.astype(BF16)
    fine = (answer - coarse.astype(F32)).astype(BF16)
    row_of = lax.broadcasted_iota(jnp.int32, (32, 768), 0)
    lane_of = lax.broadcasted_iota(jnp.int32, (32, 768), 1)
    chosen = lane_of // 48 == row_of % 16
    both = jnp.concatenate(
        [jnp.broadcast_to(coarse.astype(F32), (16, 128)), jnp.broadcast_to(fine.astype(F32), (16, 128))], 0
    ).astype(BF16)
    loads[6].wait()
    loads[7].wait()
    for patch in range(2):
        blend[patch] = jnp.where(
            chosen, jnp.dot(both, spread[patch], preferred_element_type=F32), 0.0
        ).astype(BF16)

    def finish(number, carry):
        rows = pl.ds(pl.multiple_of(number * 16, 16), 16)
        product = jnp.dot(blend[number // 16], conv[rows].reshape(768, 256), preferred_element_type=F32)
        residual[rows] = science[rows] - (product[0:16] + product[16:32])
        kernel_power = jnp.where(number < 16, powers[0], powers[1])
        spread_var[rows] = science_var[rows] + kernel_power * template_var[rows]
        return carry

    lax.fori_loop(0, 32, finish, 0, unroll=16)

    each_sent(halo, lambda copy: copy.wait_send())
    grams_sent(lambda copy: copy.wait_send())
    pltpu.make_async_copy(parts, parts, part_out).wait()


def local(template, template_var, coverage, exposure, exposure_var, strip_owner, strip_slot):
    def blocks(array):
        return array.reshape(128, 4, 2, 128).transpose(0, 2, 1, 3).reshape(128, 8, 128)

    vmem = pl.BlockSpec(memory_space=pltpu.VMEM)
    hbm = pl.BlockSpec(memory_space=pltpu.HBM)
    dma = pltpu.SemaphoreType.DMA
    x_weights, y_weights, power, spread = [jnp.asarray(table) for table in tables()]
    residual, spread_var = pl.pallas_call(
        kernel,
        out_shape=[pltpu.VMEM((512, 256), F32)] * 2,
        in_specs=[hbm] * 8 + [vmem] * 3,
        out_specs=[vmem] * 2,
        scratch_shapes=[
            pltpu.VMEM((512, 256), F32),
            pltpu.VMEM((512, 256), F32),
            pltpu.VMEM((512, 256), jnp.int32),
            pltpu.VMEM((128, 8, 128), F32),
            pltpu.VMEM((128, 8, 128), F32),
            pltpu.VMEM((8, 256, 256), BF16),
            pltpu.VMEM((8, BLOCK * 8, 256), BF16),
            pltpu.VMEM((2, 128, 768), BF16),
            pltpu.VMEM((2, 16, 512), BF16),
            pltpu.VMEM((2, 16, 512), BF16),
            pltpu.VMEM((544, 512), BF16),
            pltpu.VMEM((16, 608, 256), BF16),
            pltpu.VMEM((512, 48, 256), BF16),
            pltpu.VMEM((128, 16, 128), BF16),
            pltpu.VMEM((128, 16, 128), BF16),
            pltpu.VMEM((128, 128), jnp.int32),
            pltpu.VMEM((512, 256), F32),
            pltpu.VMEM((512, 256), F32),
            pltpu.VMEM((512, 256), F32),
            pltpu.VMEM((2, 24, 128), F32),
            pltpu.VMEM((10, 24, 128), F32),
            pltpu.VMEM((8, 128), jnp.int32),
            pltpu.SMEM((8, 128), jnp.int32),
            pltpu.SMEM((8, 128), jnp.int32),
            dma((8,)), dma((8,)), dma, dma, dma((2,)), dma((2,)), dma((10,)), dma((10,)), dma((9,)), pltpu.SemaphoreType.REGULAR,
            pltpu.VMEM((2, 32, 768), BF16),
        ],
        compiler_params=pltpu.CompilerParams(
            collective_id=0, has_side_effects=True, vmem_limit_bytes=60 * 1024 * 1024
        ),
        cost_estimate=pl.CostEstimate(flops=10**10, bytes_accessed=8 * 10**6, transcendentals=0),
    )(
        template, template_var, coverage, blocks(exposure), blocks(exposure_var), x_weights, y_weights, spread,
        strip_owner, strip_slot, power,
    )
    mask = coverage.astype(F32)
    return (mask * residual, mask * spread_var)


def solution(mesh):
    image = P("row", "col")
    strips = P("row", "col", None, None)
    return jax.shard_map(
        local,
        mesh=mesh,
        in_specs=(image, image, image, strips, strips, image, image),
        out_specs=(image, image),
        check_vma=False,
    )
```

```python
import jax
import jax.numpy as jnp
import numpy as np
from jax import lax
from jax.experimental import pallas as pl
from jax.experimental.pallas import tpu as pltpu
from jax.sharding import PartitionSpec as P

RIDGE = 0.05
SIGMAS = (1.0, 2.0, 4.0)
MESH = pl.DeviceIdType.MESH
F32 = jnp.float32
BF16 = jnp.bfloat16

SLOTS = (
    (0, 0), (0, 2), (1, 0), (1, 2), (2, 0), (2, 2), (0, 1), (1, 1),
    (2, 1), (0, 3), (1, 3), None, (2, 3), (0, 4), (1, 4), (2, 4),
)
GROUP_OF_PASS = (0, 1, 2, 3, 4, 4, 5, 5)
BLOCK = 96
TARGET = 47
GRAM_COPIES = ((0, -1, 0), (1, 1, 0), (0, -1, -1), (0, -1, 1), (1, 1, -1), (1, 1, 1), (0, 0, -1), (0, 0, 1), (1, 0, -1), (1, 0, 1))
DIRECTIONS = ((0, -1), (0, 1), (-1, 0), (1, 0), (-1, -1), (-1, 1), (1, -1), (1, 1))


def filter_bank():
    taps = np.arange(31) - 15.0
    collected = []
    for sigma in SIGMAS:
        for degree in range(5):
            scaled = taps / sigma
            shape = scaled**degree * np.exp(-0.5 * scaled * scaled)
            collected.append(shape / np.sqrt(np.sum(shape * shape)))
    return np.array(collected, np.float32).astype(jnp.bfloat16).astype(np.float32)


def tables():
    bank = filter_bank()
    x_weights = np.zeros((8, 256, 2, 128), np.float32)
    y_weights = np.zeros((8, BLOCK, 8, 2, 128), np.float32)
    across = np.arange(128)
    down = np.arange(BLOCK)
    order = []
    filled = [0] * 6
    for number, slot in enumerate(SLOTS):
        if slot is None:
            continue
        half, which = number // 2, number % 2
        s, i = slot
        group = GROUP_OF_PASS[half]
        for q in range(31):
            x_weights[half, across + q - 15 + 64, which, across] = bank[s * 5 + i, q]
        for j in range(5 - i):
            lane = filled[group]
            filled[group] += 1
            order.append((group * 8 + lane, s, i, j))
            for p in range(31):
                y_weights[half, down, lane, which, down + p - 15 + 16] = bank[s * 5 + j, p]
    shapes = np.zeros((48, 31 * 31), np.float64)
    for t, s, i, j in order:
        shapes[t] = np.outer(bank[s * 5 + j], bank[s * 5 + i]).reshape(-1).astype(np.float64)
    values, vectors = np.linalg.eigh(shapes @ shapes.T)
    root = np.sqrt(np.maximum(values, 0.0))[:, None] * vectors.T
    power = np.zeros((48, 128), np.float32)
    power[:, :48] = root
    power[:, 64:112] = root
    spread = np.zeros((2, 128, 768), np.float32)
    for patch in range(2):
        spread[patch, 64 * patch + np.arange(768) % 48, np.arange(768)] = 1.0
    return (
        x_weights.reshape(8, 256, 256).astype(jnp.bfloat16),
        y_weights.reshape(8, BLOCK * 8, 256).astype(jnp.bfloat16),
        power,
        spread.astype(jnp.bfloat16),
    )


def inverse_row(columns, size=128):
    rows = lax.broadcasted_iota(jnp.int32, (size, size), 0)
    lanes = lax.broadcasted_iota(jnp.int32, (size, size), 1)
    return jnp.max(jnp.where(columns == lanes, rows, 0), 0, keepdims=True)


def within(number):
    return jnp.clip(number, 0, 127)


def kernel(
    template_hbm, template_var_hbm, coverage_hbm, flux_hbm, noise_hbm, x_weights_hbm, y_weights_hbm, spread_hbm,
    owner, slot, power,
    residual, spread_var,
    template, template_var, coverage, flux, noise, x_weights, y_weights, spread,
    side_out, side_in, wide, filtered, conv, send, recv, labels, science, science_var, root, own_gram, near_gram,
    row_index, table_in, table_out,
    halo_out, halo_in, part_out, part_in, label_out, label_in, gram_out, gram_in, load_in, ready, blend,
):
    r = lax.axis_index("row")
    c = lax.axis_index("col")
    x, z, k = c // 8, (c // 2) % 4, c % 2
    me = r * 32 + c
    place = (z * 2 + k) * 16 + r * 4 + x
    barrier = pltpu.get_barrier_semaphore()

    loads = [
        pltpu.make_async_copy(source, held, load_in.at[number])
        for number, (source, held) in enumerate((
            (template_hbm, template), (flux_hbm, flux), (noise_hbm, noise), (x_weights_hbm, x_weights),
            (y_weights_hbm, y_weights), (coverage_hbm, coverage), (template_var_hbm, template_var), (spread_hbm, spread),
        ))
    ]
    loads[0].start()

    wide[...] = jnp.zeros_like(wide)
    near_gram[...] = jnp.zeros_like(near_gram)
    side_in[...] = jnp.zeros_like(side_in)
    own_gram[...] = jnp.zeros_like(own_gram)

    def column(dx, dz, dk):
        return (x + dx) % 4 * 8 + (z + dz) % 4 * 2 + (k + dk) % 2

    across = [((r + dr) % 4, column(dx, 0, 0)) for dr in range(4) for dx in range(4) if dr or dx]
    along = [(r, column(0, dz, dk)) for dz in range(4) for dk in range(2) if dz or dk]
    around = [((r + dr) % 4, (c + dc) % 32) for dr, dc in DIRECTIONS if dc]
    for other in around + across + along:
        pl.semaphore_signal(barrier, inc=1, device_id=other, device_id_type=MESH)
    for load in loads[1:]:
        load.start()

    owners = jnp.transpose(jnp.broadcast_to(owner[...], (128, 128)))
    row_index[...] = jnp.broadcast_to(inverse_row(owners), (8, 128))
    owner_copy = pltpu.make_async_copy(row_index, table_in, load_in.at[8])
    owner_copy.start()
    labels[pl.ds(place, 1), :] = slot[...]
    loads[0].wait()
    wide[16:528, 128:384] = template[...].astype(BF16)
    side_row = lax.broadcasted_iota(jnp.int32, (16, 128), 0)
    side_lane = lax.broadcasted_iota(jnp.int32, (16, 128), 1)
    sides = [
        jnp.where(side_lane == side_row + first, 1.0, 0.0).astype(BF16) for first in (0, 112)
    ]
    for number in range(2):
        side_out[number] = lax.dot_general(
            sides[number],
            wide[16:528, 128 + 128 * number : 256 + 128 * number],
            (((1,), (1,)), ((), ())),
            preferred_element_type=F32,
        ).astype(BF16)
    pl.semaphore_wait(barrier, 28)
    for other in along:
        pl.semaphore_signal(ready, inc=1, device_id=other, device_id_type=MESH)

    def inside(dr, dc):
        return jnp.logical_and(
            jnp.logical_and(r + dr >= 0, r + dr < 4), jnp.logical_and(c + dc >= 0, c + dc < 32)
        )

    def target(dr, dc):
        return (jnp.clip(r + dr, 0, 3), jnp.clip(c + dc, 0, 31))

    source_rows = {-1: pl.ds(16, 16), 0: pl.ds(16, 512), 1: pl.ds(512, 16)}
    target_rows = {-1: pl.ds(528, 16), 0: pl.ds(16, 512), 1: pl.ds(0, 16)}
    source_cols = {-1: pl.ds(128, 128), 0: pl.ds(128, 256), 1: pl.ds(256, 128)}
    target_cols = {-1: pl.ds(384, 128), 0: pl.ds(128, 256), 1: pl.ds(0, 128)}

    def halo(number):
        dr, dc = DIRECTIONS[number]
        return pltpu.make_async_remote_copy(
            src_ref=wide.at[source_rows[dr], source_cols[dc]] if dr else side_out.at[number],
            dst_ref=wide.at[target_rows[dr], target_cols[dc]] if dr else side_in.at[number],
            send_sem=halo_out.at[number],
            recv_sem=halo_in.at[number],
            device_id=target(dr, dc),
            device_id_type=MESH,
        )

    def gram_copy(number):
        patch, dr, dc = GRAM_COPIES[number]
        return pltpu.make_async_remote_copy(
            src_ref=own_gram.at[patch],
            dst_ref=near_gram.at[number],
            send_sem=gram_out.at[number],
            recv_sem=gram_in.at[number],
            device_id=target(dr, dc),
            device_id_type=MESH,
        )

    def grams_sent(action):
        for number, (_, dr, dc) in enumerate(GRAM_COPIES):
            @pl.when(inside(dr, dc))
            def _():
                action(gram_copy(number))

    def grams_received():
        for number, (_, dr, dc) in enumerate(GRAM_COPIES):
            @pl.when(inside(-dr, -dc))
            def _():
                gram_copy(number).wait_recv()

    def each_sent(make, action):
        for number, (dr, dc) in enumerate(DIRECTIONS):
            @pl.when(inside(dr, dc))
            def _():
                action(make(number))

    def each_received(make):
        for number, (dr, dc) in enumerate(DIRECTIONS):
            @pl.when(inside(-dr, -dc))
            def _():
                make(number).wait_recv()

    each_sent(halo, lambda copy: copy.start())

    def label_copy(first, count, row, col, which):
        return pltpu.make_async_remote_copy(
            src_ref=labels.at[pl.ds(first, count)],
            dst_ref=labels.at[pl.ds(first, count)],
            send_sem=label_out.at[which],
            recv_sem=label_in.at[which],
            device_id=(row, col),
            device_id_type=MESH,
        )

    for other in across:
        label_copy(place, 1, *other, 0).start()

    owner_copy.wait()
    loads[1].wait()
    loads[2].wait()

    def chunk(number):
        block = within(table_in[0, number])
        return jnp.concatenate([flux[block], noise[block]], 0).astype(BF16)

    def label_wait(count, which):
        part = labels.at[pl.ds(0, count)]
        pltpu.make_async_copy(part, part, label_in.at[which]).wait()
        pltpu.make_async_copy(part, part, label_out.at[which]).wait()

    def send_to(others):
        for row, col in others:
            send[row * 32 + col] = chunk(row * 32 + col)
        for row, col in others:
            pltpu.make_async_remote_copy(
                src_ref=send.at[row * 32 + col],
                dst_ref=recv.at[place],
                send_sem=part_out,
                recv_sem=part_in,
                device_id=(row, col),
                device_id_type=MESH,
            ).start()

    def send_group(group, carry):
        send_to([
            ((r + group // 4) % 4, column(group % 4, dz, dk)) for dz in range(4) for dk in range(2) if dz or dk
        ])
        return carry

    recv[place] = chunk(me)
    send_to(across)
    send_to(along)
    pl.semaphore_wait(ready, 7)
    lax.fori_loop(1, 8, send_group, 0)
    label_wait(15, 0)
    for other in along:
        label_copy(pl.multiple_of((z * 2 + k) * 16, 16), 16, *other, 1).start()
    lax.fori_loop(8, 16, send_group, 0)

    each_received(halo)

    for number in range(2):
        wide[16:528, 384 - 384 * number : 512 - 384 * number] = lax.dot_general(
            side_in[number], sides[number], (((0,), (0,)), ((), ())), preferred_element_type=F32
        ).astype(BF16)

    filtered[:, 544:608, :] = jnp.zeros((16, 64, 256), BF16)
    loads[3].wait()
    whole = wide[...]
    windows = (whole[:, 64:320], whole[:, 192:448])

    def along_x(half, carry):
        for side in range(2):
            product = jnp.dot(windows[side], x_weights[half], preferred_element_type=F32).astype(BF16)
            for which in range(2):
                filtered[2 * half + which, 0:544, side * 128 : side * 128 + 128] = product[
                    :, which * 128 : which * 128 + 128
                ]
        return carry

    lax.fori_loop(0, 8, along_x, 0, unroll=True)

    def along_y(first, rows):
        for pair in range(3):
            groups = []
            for group in (2 * pair, 2 * pair + 1):
                total = None
                for half in range(8):
                    if GROUP_OF_PASS[half] == group:
                        window = filtered[2 * half : 2 * half + 2, pl.ds(first, 128), :].reshape(256, 256)
                        product = jnp.dot(
                            y_weights[half, 0 : rows * 8, :], window, preferred_element_type=F32
                        )
                        total = product if total is None else total + product
                groups.append(total.reshape(rows, 8, 256))
            conv[pl.ds(first, rows), pair * 16 : pair * 16 + 16, :] = jnp.concatenate(groups, 1).astype(BF16)

    loads[4].wait()

    def y_block(number, carry):
        along_y(pl.multiple_of(number * BLOCK, 16), BLOCK)
        return carry

    lax.fori_loop(0, 4, y_block, 0, unroll=True)
    label_wait(112, 1)
    row_index[...] = jnp.broadcast_to(inverse_row(labels[...]), (8, 128))
    table_copy = pltpu.make_async_copy(row_index, table_out, load_in.at[0])
    table_copy.start()
    y_block(4, 0)
    along_y(480, 32)

    table_copy.wait()
    parts = recv.at[pl.ds(0, 127)]
    pltpu.make_async_copy(parts, parts, part_in).wait()

    def unpack(number, carry):
        upper = recv[within(table_out[0, 2 * number])].astype(F32)
        lower = recv[within(table_out[0, 2 * number + 1])].astype(F32)
        rows = pl.ds(pl.multiple_of(number * 8, 8), 8)
        science[rows, 0:128] = jnp.concatenate([upper[0:4], lower[0:4]], 0)
        science[rows, 128:256] = jnp.concatenate([upper[4:8], lower[4:8]], 0)
        for side in range(2):
            lanes = pl.ds(128 * side, 128)
            part = slice(8 + 4 * side, 12 + 4 * side)
            noise_rows = jnp.concatenate([upper[part], lower[part]], 0)
            science_var[rows, lanes] = noise_rows
            root[rows, lanes] = coverage[rows, lanes].astype(F32) * lax.rsqrt(noise_rows)
        return carry

    loads[5].wait()

    lax.fori_loop(0, 64, unpack, 0, unroll=8)

    is_target = lax.broadcasted_iota(jnp.int32, (16, 256), 0) == TARGET - 32

    def gram_patch(patch, carry):
        base = pl.multiple_of(patch * 256, 256)
        pieces = []
        for row in range(256):
            weight = root[pl.ds(base + row, 1), :]
            goal = weight * science[pl.ds(base + row, 1), :]
            basis = conv[base + row].astype(F32) * weight
            last = jnp.where(is_target, goal, basis[32:48])
            pieces.append(jnp.concatenate([basis[0:32].astype(BF16), last.astype(BF16)], 0))
        block = jnp.concatenate(pieces, 1)
        total = lax.dot_general(block, block, (((1,), (1,)), ((), ())), preferred_element_type=F32)
        own_gram[patch, :, 0:48] = total[0:24]
        own_gram[patch, :, 64:112] = total[24:48]
        return carry

    lax.fori_loop(0, 2, gram_patch, 0)
    grams_sent(lambda copy: copy.start())
    grams_received()

    lane = lax.broadcasted_iota(jnp.int32, (48, 128), 1)
    sub = lax.broadcasted_iota(jnp.int32, (48, 128), 0)
    beside = own_gram[0] + own_gram[1] + near_gram[6] + near_gram[7] + near_gram[8] + near_gram[9]
    upper = beside + near_gram[1] + near_gram[4] + near_gram[5]
    lower = beside + near_gram[0] + near_gram[2] + near_gram[3]
    first_half = lane[0:24] < 64
    system = jnp.concatenate(
        [
            jnp.where(first_half, upper, pltpu.roll(lower, 64, 1)),
            jnp.where(first_half, pltpu.roll(upper, 64, 1), lower),
        ],
        0,
    )
    half_lane = lane % 64
    diagonal = jnp.logical_and(sub == half_lane, sub < 45)
    on_diagonal = jnp.where(diagonal, system, 0.0)
    trace_upper = jnp.sum(jnp.where(lane < 64, on_diagonal, 0.0))
    trace_lower = jnp.sum(jnp.where(lane < 64, 0.0, on_diagonal))
    ridge = jnp.where(lane < 64, trace_upper, trace_lower) * (RIDGE / 45.0)
    system = jnp.where(diagonal, system + ridge, system)

    def column_of(matrix, step):
        return jnp.take_along_axis(matrix, (lane - half_lane) + step, axis=1)

    def pivot_pair(first, second, step):
        a, b = first[step : step + 1], second[step : step + 1]
        c, d = first[step + 1 : step + 2], second[step + 1 : step + 2]
        inverse = 1.0 / (a * d - b * c)
        return first * (d * inverse) - second * (c * inverse), second * (a * inverse) - first * (b * inverse)

    for step in range(0, 44, 4):
        columns = [column_of(system, step + number) for number in range(4)]
        row = [system[step + number : step + number + 1] for number in range(4)]
        u0, u1 = pivot_pair(columns[0], columns[1], step)
        third, fourth = (
            column - u0 * column[step : step + 1] - u1 * column[step + 1 : step + 2] for column in columns[2:]
        )
        u2, u3 = pivot_pair(third, fourth, step + 2)
        row[2] = row[2] - u0[step + 2 : step + 3] * row[0] - u1[step + 2 : step + 3] * row[1]
        row[3] = row[3] - u0[step + 3 : step + 4] * row[0] - u1[step + 3 : step + 4] * row[1]
        v0 = u0 - u2 * u0[step + 2 : step + 3] - u3 * u0[step + 3 : step + 4]
        v1 = u1 - u2 * u1[step + 2 : step + 3] - u3 * u1[step + 3 : step + 4]
        system = system - u0 * row[0] - u1 * row[1] - u2 * row[2] - u3 * row[3]
        for number, column in enumerate((v0, v1, u2, u3)):
            system = jnp.where(half_lane == step + number, column, system)
    column = column_of(system, 44)
    inverse = 1.0 / column[44:45]
    system = jnp.where(half_lane == 44, column * inverse, system - column * (inverse * system[44:45]))
    answer = jnp.where(jnp.logical_and(half_lane[47:48] < 45, lane[47:48] < 128), system[TARGET : TARGET + 1], 0.0)
    terms = power[...] * answer
    upper_terms = jnp.sum(jnp.where(lane < 64, terms, 0.0), 1, keepdims=True)
    lower_terms = jnp.sum(jnp.where(lane < 64, 0.0, terms), 1, keepdims=True)
    powers = (jnp.sum(upper_terms * upper_terms), jnp.sum(lower_terms * lower_terms))

    coarse = answer.astype(BF16)
    fine = (answer - coarse.astype(F32)).astype(BF16)
    row_of = lax.broadcasted_iota(jnp.int32, (32, 768), 0)
    lane_of = lax.broadcasted_iota(jnp.int32, (32, 768), 1)
    chosen = lane_of // 48 == row_of % 16
    both = jnp.concatenate(
        [jnp.broadcast_to(coarse.astype(F32), (16, 128)), jnp.broadcast_to(fine.astype(F32), (16, 128))], 0
    ).astype(BF16)
    loads[6].wait()
    loads[7].wait()
    for patch in range(2):
        blend[patch] = jnp.where(
            chosen, jnp.dot(both, spread[patch], preferred_element_type=F32), 0.0
        ).astype(BF16)

    def finish(number, carry):
        rows = pl.ds(pl.multiple_of(number * 16, 16), 16)
        product = jnp.dot(blend[number // 16], conv[rows].reshape(768, 256), preferred_element_type=F32)
        residual[rows] = science[rows] - (product[0:16] + product[16:32])
        kernel_power = jnp.where(number < 16, powers[0], powers[1])
        spread_var[rows] = science_var[rows] + kernel_power * template_var[rows]
        return carry

    lax.fori_loop(0, 32, finish, 0, unroll=16)

    each_sent(halo, lambda copy: copy.wait_send())
    grams_sent(lambda copy: copy.wait_send())
    pltpu.make_async_copy(parts, parts, part_out).wait()


def local(template, template_var, coverage, exposure, exposure_var, strip_owner, strip_slot):
    def blocks(array):
        return array.reshape(128, 4, 2, 128).transpose(0, 2, 1, 3).reshape(128, 8, 128)

    vmem = pl.BlockSpec(memory_space=pltpu.VMEM)
    hbm = pl.BlockSpec(memory_space=pltpu.HBM)
    dma = pltpu.SemaphoreType.DMA
    x_weights, y_weights, power, spread = [jnp.asarray(table) for table in tables()]
    residual, spread_var = pl.pallas_call(
        kernel,
        out_shape=[pltpu.VMEM((512, 256), F32)] * 2,
        in_specs=[hbm] * 8 + [vmem] * 3,
        out_specs=[vmem] * 2,
        scratch_shapes=[
            pltpu.VMEM((512, 256), F32),
            pltpu.VMEM((512, 256), F32),
            pltpu.VMEM((512, 256), jnp.int32),
            pltpu.VMEM((128, 8, 128), F32),
            pltpu.VMEM((128, 8, 128), F32),
            pltpu.VMEM((8, 256, 256), BF16),
            pltpu.VMEM((8, BLOCK * 8, 256), BF16),
            pltpu.VMEM((2, 128, 768), BF16),
            pltpu.VMEM((2, 16, 512), BF16),
            pltpu.VMEM((2, 16, 512), BF16),
            pltpu.VMEM((544, 512), BF16),
            pltpu.VMEM((16, 608, 256), BF16),
            pltpu.VMEM((512, 48, 256), BF16),
            pltpu.VMEM((128, 16, 128), BF16),
            pltpu.VMEM((128, 16, 128), BF16),
            pltpu.VMEM((128, 128), jnp.int32),
            pltpu.VMEM((512, 256), F32),
            pltpu.VMEM((512, 256), F32),
            pltpu.VMEM((512, 256), F32),
            pltpu.VMEM((2, 24, 128), F32),
            pltpu.VMEM((10, 24, 128), F32),
            pltpu.VMEM((8, 128), jnp.int32),
            pltpu.SMEM((8, 128), jnp.int32),
            pltpu.SMEM((8, 128), jnp.int32),
            dma((8,)), dma((8,)), dma, dma, dma((2,)), dma((2,)), dma((10,)), dma((10,)), dma((9,)), pltpu.SemaphoreType.REGULAR,
            pltpu.VMEM((2, 32, 768), BF16),
        ],
        compiler_params=pltpu.CompilerParams(
            collective_id=0, has_side_effects=True, vmem_limit_bytes=60 * 1024 * 1024
        ),
        cost_estimate=pl.CostEstimate(flops=10**10, bytes_accessed=8 * 10**6, transcendentals=0),
    )(
        template, template_var, coverage, blocks(exposure), blocks(exposure_var), x_weights, y_weights, spread,
        strip_owner, strip_slot, power,
    )
    mask = coverage.astype(F32)
    return (mask * residual, mask * spread_var)


def solution(mesh):
    image = P("row", "col")
    strips = P("row", "col", None, None)
    return jax.shard_map(
        local,
        mesh=mesh,
        in_specs=(image, image, image, strips, strips, image, image),
        out_specs=(image, image),
        check_vma=False,
    )
```
